32 devices in a mesh: dp: 16 (over z, y, x), seq: 2 (over core).
Axes of the slice: x: 2, y: 2, z: 4, core: 2. Of those that a mesh axis runs over, the one named last changes fastest.
Arguments:
- inputs: bfloat16 [64, 1024, 256], P('dp', 'seq'), may hold values from -6 to 6
- cotangent: bfloat16 [64, 1024, 256], P('dp', 'seq'), may hold values from -6 to 6
- loss_mask: int32 [64, 1024], P('dp', 'seq'), may hold values from 0 to 1, as said below
- complement_map: int32 [256], replicated, may hold values from 0 to 255, each once
- owners: int32 [32], replicated, may hold values from 0 to 15, as said below
- weights: float32 [64, 13696], P('dp'), as said below
- first_moment: float32 [64, 13696], P('dp'), as said below
- second_moment: float32 [64, 13696], P('dp'), as said below
Outputs:
- output: bfloat16 [64, 1024, 256], P('dp', 'seq')
- grad_input: float32 [64, 1024, 256], P('dp', 'seq')
- new_weights: float32 [64, 13696], P('dp')
- new_first: float32 [64, 13696], P('dp')
- new_second: float32 [64, 13696], P('dp')
The draws below stay inside these ranges and needn't reach their ends.
Inputs may be any that keep to these rules, and one draw needn't show every extreme that they name: `loss_mask`: 1 marks a loss token; each window has its own rate, drawn between 8 and 22 percent. `complement_map`: each channel appears once. `owners`: at most 4 blocks share an owner, and some owner holds exactly 4. `weights`: rows that no block fills are zero. `first_moment`: rows that no block fills are zero. `second_moment`: entries of filled rows are positive; rows that no block fills are zero.
All inputs are finite; a program needn't handle non-finite values.
Results may differ from the reference program's by a relative error of at most 0.0093.
Values may be sent and summed in bfloat16 or wider, within the bound.
No kernel may reach another device: no remote copies, remote signals or barrier semaphores. Data moves between devices by JAX's collectives and lax.ppermute only.
A program may use at most 320 MiB of HBM per device.

```python
import math
from functools import partial
import jax
import jax.numpy as jnp
from jax import lax

D = 256
INNER = 512
STATE = 16
RANK = 16
KERNEL = 4
LENGTH = 1024
WIN_DEV = 4
SCAN_BLOCK = 64
SLOTS = 4
STEP_COUNT = 10
WINDOWS = 64
BLOCKS = 32
PARAMS = 438016
MATRIX_END = 425984
BLOCK_LEN = 13696
N_DP = 16


def owner_table(key):
    total = N_DP * SLOTS
    key_full, key_order, key_mix = jax.random.split(key, 3)
    full_device = jax.random.randint(key_full, (), 0, N_DP)
    position = jnp.arange(total, dtype=jnp.int32)
    scores = jax.random.permutation(key_order, total).astype(jnp.int32)
    scores = jnp.where(position // SLOTS == full_device, position - total, scores)
    order = jnp.argsort(scores, stable=True)
    chosen = order[:BLOCKS][jax.random.permutation(key_mix, BLOCKS)]
    return (chosen // SLOTS).astype(jnp.int32)


def slot_layout(owners, flat):
    order = jnp.arange(BLOCKS, dtype=jnp.int32)
    same = (owners[None, :] == owners[:, None]) & (order[None, :] < order[:, None])
    slots = owners * SLOTS + jnp.sum(same.astype(jnp.int32), axis=1)
    return jnp.zeros((N_DP * SLOTS, BLOCK_LEN), jnp.float32).at[slots].set(flat.reshape(BLOCKS, BLOCK_LEN))


def log_uniform(key, count, low_end, high_end):
    return jnp.exp(jax.random.uniform(key, (count,), jnp.float32, math.log(low_end), math.log(high_end)))


def grad_scale():
    position = jnp.arange(BLOCKS * BLOCK_LEN)
    return jnp.where(position < MATRIX_END, 0.3, 0.5) * math.sqrt(N_DP * WIN_DEV * LENGTH)


def draw_loss_mask(key, part):
    key = jax.random.fold_in(key, 5)
    key_rate, key_pick = jax.random.split(key)
    rate = jax.random.randint(key_rate, (WINDOWS, 1), 8, 23)
    return (jax.random.randint(key_pick, (WINDOWS, LENGTH), 0, 100) < rate).astype(jnp.int32)


def draw_owners(key, part):
    return owner_table(key)


def draw_weights(key, part):
    owners = owner_table(key)
    key = jax.random.fold_in(key, 11)
    keys = jax.random.split(key, 11)
    normal = jax.random.normal
    pieces = [normal(keys[0], (D * 2 * INNER,)) * D ** (-0.5), normal(keys[1], (INNER * (RANK + 2 * STATE),)) * INNER ** (-0.5), normal(keys[2], (RANK * INNER,)) * RANK ** (-0.5), normal(keys[3], (INNER * D,)) * (3.0 * INNER ** (-0.5)), normal(keys[4], (INNER * KERNEL,)) * KERNEL ** (-0.5), normal(keys[5], (INNER,)) * 0.5, jnp.log(jnp.expm1(log_uniform(keys[6], INNER, 0.001, 0.1))), jnp.log(log_uniform(keys[7], INNER * STATE, 1.0, 16.0)), jax.random.uniform(keys[8], (INNER,), jnp.float32, 0.5, 1.5), jax.random.uniform(keys[9], (D,), jnp.float32, 0.8, 1.2), normal(keys[10], (BLOCKS * BLOCK_LEN - PARAMS,)) * 0.1]
    return slot_layout(owners, jnp.concatenate(pieces))


def draw_first_moment(key, part):
    owners = owner_table(key)
    key = jax.random.fold_in(key, 13)
    values = jax.random.normal(key, (BLOCKS * BLOCK_LEN,)) * grad_scale() / 9.0
    return slot_layout(owners, values)


def draw_second_moment(key, part):
    owners = owner_table(key)
    key = jax.random.fold_in(key, 17)
    scale = grad_scale()
    values = scale * scale * (0.05 / 0.95) * log_uniform(key, BLOCKS * BLOCK_LEN, 1.0, 4.0)
    return slot_layout(owners, values)


def level_of(key, extent, cuts, smallest, top_value):
    loudness = 1.0
    for axis_at, blocks in cuts:
        steps = jax.random.uniform(jax.random.fold_in(jax.random.fold_in(key, 6), axis_at), (blocks,), jnp.float32, smallest / len(cuts), top_value / len(cuts))
        loudness = loudness * jnp.repeat(jnp.exp(steps), extent[axis_at] // blocks).reshape((-1,) + (1,) * (len(extent) - 1 - axis_at))
    return loudness


def scatter_about(own_key, extent, spread, limit, shards=(), kind=jnp.bfloat16):
    factor_of = level_of(own_key, extent, shards, -0.22, 0.18) if shards else 1.0
    drawn = jax.random.normal(own_key, extent, jnp.float32) * spread * factor_of
    return jnp.minimum(jnp.maximum(drawn, -limit), limit).astype(kind)


def setup_inputs(seed: int = 0) -> dict:
    streams_of = jax.random.split(jax.random.key(seed), 9)
    inputs = scatter_about(streams_of[0], (WINDOWS, LENGTH, D), 1.0, 6.0, ((0, 16), (1, 2)))
    cotangent = scatter_about(streams_of[1], (WINDOWS, LENGTH, D), 1.0, 6.0, ((0, 16), (1, 2)))
    loss_mask = draw_loss_mask(jax.random.fold_in(streams_of[8], 71), 0)
    complement_map = jax.random.permutation(streams_of[3], D).astype(jnp.int32)
    owners = draw_owners(jax.random.fold_in(streams_of[8], 71), 0)
    weights = draw_weights(jax.random.fold_in(streams_of[8], 71), 0)
    first_moment = draw_first_moment(jax.random.fold_in(streams_of[8], 71), 0)
    second_moment = draw_second_moment(jax.random.fold_in(streams_of[8], 71), 0)
    return dict(inputs=inputs, cotangent=cotangent, loss_mask=loss_mask, complement_map=complement_map, owners=owners, weights=weights, first_moment=first_moment, second_moment=second_moment)


@jax.custom_vjp
def low(v):
    return lax.optimization_barrier(v.astype(jnp.bfloat16)).astype(jnp.float32)

@jax.custom_vjp
def low_back(v):
    return v

def low_keep(v):
    return (low(v), None)

def low_pass(kept, grad):
    return (grad,)

def back_keep(v):
    return (v, None)

def back_low(kept, grad):
    return (low(grad),)
low.defvjp(low_keep, low_pass)
low_back.defvjp(back_keep, back_low)
BETA_ONE = 0.9
BETA_TWO = 0.95
ADAM_EPSILON = 1e-08
RATE_MATRIX = 0.1
RATE_VECTOR = 0.5
WEIGHT_DECAY = 0.1
NORM_EPSILON = 1e-05
HIGHEST_PREC = lax.Precision.HIGHEST

def param_shapes():
    return [(D, 2 * INNER), (INNER, RANK + 2 * STATE), (RANK, INNER), (INNER, D), (INNER, KERNEL), (INNER,), (INNER,), (INNER, STATE), (INNER,), (D,)]

def unpack_params(flat):
    pieces = []
    offset = 0
    for shape in param_shapes():
        count = math.prod(shape)
        pieces.append(flat[offset:offset + count].reshape(shape))
        offset += count
    return pieces

def slot_index(owners):
    count = owners.shape[0]
    order = jnp.arange(count, dtype=jnp.int32)
    same = (owners[None, :] == owners[:, None]) & (order[None, :] < order[:, None])
    return (owners * SLOTS + lax.optimization_barrier(jnp.sum(same.astype(jnp.int32), axis=1))).astype(jnp.int32)

def selective_scan(delta, act, entry, readout, a_log):
    decay_rate = -jnp.exp(a_log)
    blocks = LENGTH // SCAN_BLOCK

    def to_blocks(value):
        shaped = value.reshape(value.shape[:2] + (blocks, SCAN_BLOCK) + value.shape[3:])
        return jnp.moveaxis(shaped, 2, 0)

    @jax.checkpoint
    def run_block(state, pieces):

        def one_step(inner, column):
            step_delta, step_act, step_entry, step_read = column
            inner = jnp.exp(step_delta[..., None] * decay_rate) * inner + (step_delta * step_act)[..., None] * step_entry[..., None, :]
            return (inner, lax.optimization_barrier(jnp.sum(inner * step_read[..., None, :], axis=-1)))
        columns = tuple((jnp.moveaxis(item, 2, 0) for item in pieces))
        state, outputs = lax.scan(one_step, state, columns)
        return (state, jnp.moveaxis(outputs, 0, 2))
    start = jnp.zeros(delta.shape[:2] + (INNER, STATE), jnp.float32)
    final_state, outputs = lax.scan(run_block, start, tuple((to_blocks(value) for value in (delta, act, entry, readout))))
    return jnp.moveaxis(outputs, 0, 2).reshape(delta.shape)

def layer_forward(params, tokens, perm_matrix):
    w_in, w_x, w_dt, w_out, conv_w, conv_b, dt_bias, a_log, d_skip, gain = params
    mean_square = lax.optimization_barrier(jnp.mean(tokens * tokens, axis=-1, keepdims=True))
    normed = low(tokens * lax.rsqrt(mean_square + NORM_EPSILON) * gain)
    mirror = jnp.einsum('gtd,cd->gtc', normed[:, ::-1], perm_matrix, precision=HIGHEST_PREC)
    copies = jnp.stack([normed, mirror], axis=1)
    projected = jnp.einsum('gktd,df->gktf', copies, low(w_in), precision=HIGHEST_PREC)
    projected = low_back(low(projected))
    inner_in = projected[..., :INNER]
    gate_in = projected[..., INNER:]
    padded = jnp.pad(inner_in, ((0, 0), (0, 0), (KERNEL - 1, 0), (0, 0)))
    conv_out = conv_b + sum((conv_w[:, index] * padded[:, :, index:index + LENGTH] for index in range(KERNEL)))
    act = jax.nn.silu(conv_out)
    proj = jnp.einsum('gkte,ef->gktf', act, w_x, precision=HIGHEST_PREC)
    low_rank = proj[..., :RANK]
    entry = proj[..., RANK:RANK + STATE]
    readout = proj[..., RANK + STATE:]
    delta = jax.nn.softplus(jnp.einsum('gktr,re->gkte', low_rank, w_dt, precision=HIGHEST_PREC) + dt_bias)
    scanned = selective_scan(delta, act, entry, readout, a_log) + d_skip * act
    gated = low_back(low(scanned * jax.nn.silu(gate_in)))
    outputs = jnp.einsum('gkte,ed->gktd', gated, low(w_out), precision=HIGHEST_PREC)
    mapped = jnp.einsum('gtc,cd->gtd', outputs[:, 1, ::-1], perm_matrix, precision=HIGHEST_PREC)
    return tokens + outputs[:, 0] + mapped

def reference(inputs, cotangent, loss_mask, complement_map, owners, weights, first_moment, second_moment):
    slots = slot_index(owners)
    theta_blocks = weights[slots]
    params = unpack_params(theta_blocks.reshape(-1))
    perm_matrix = (complement_map[:, None] == jnp.arange(D, dtype=jnp.int32)[None, :]).astype(jnp.float32)
    group = math.gcd(WINDOWS, max(1, 4096 // LENGTH))
    count = WINDOWS // group
    tokens = inputs.astype(jnp.float32).reshape(count, group, LENGTH, D)
    upstream = (cotangent.astype(jnp.float32) * loss_mask.astype(jnp.float32)[..., None]).reshape(count, group, LENGTH, D)
    forward = partial(layer_forward, perm_matrix=perm_matrix)

    def one_group(totals, pieces):
        piece_tokens, piece_up = pieces
        result, pullback = jax.vjp(forward, params, piece_tokens)
        grad_params, grad_tokens = pullback(piece_up)
        totals = jax.tree.map(jnp.add, totals, grad_params)
        return (totals, (result.astype(jnp.bfloat16), grad_tokens))
    zeros = jax.tree.map(jnp.zeros_like, params)
    totals, (output, grad_input) = lax.scan(one_group, zeros, (tokens, upstream))
    flat_grad = jnp.concatenate([item.reshape(-1) for item in totals])
    flat_grad = jnp.pad(flat_grad, (0, BLOCKS * BLOCK_LEN - PARAMS)).reshape(BLOCKS, BLOCK_LEN)
    first = first_moment[slots]
    second = second_moment[slots]
    new_first = BETA_ONE * first + (1.0 - BETA_ONE) * flat_grad
    new_second = BETA_TWO * second + (1.0 - BETA_TWO) * flat_grad * flat_grad
    position = jnp.arange(BLOCKS * BLOCK_LEN, dtype=jnp.int32).reshape(BLOCKS, BLOCK_LEN)
    is_matrix = position < MATRIX_END
    rate = jnp.where(is_matrix, RATE_MATRIX, RATE_VECTOR)
    decay = jnp.where(is_matrix, WEIGHT_DECAY, 0.0)
    corrected = new_first / (1.0 - BETA_ONE ** STEP_COUNT) / (jnp.sqrt(new_second / (1.0 - BETA_TWO ** STEP_COUNT)) + ADAM_EPSILON)
    new_theta = theta_blocks - rate * (corrected + decay * theta_blocks)

    def pack(values):
        return jnp.zeros((N_DP * SLOTS, BLOCK_LEN), jnp.float32).at[slots].set(values)
    return (output.reshape(WINDOWS, LENGTH, D), grad_input.reshape(WINDOWS, LENGTH, D), pack(new_theta), pack(new_first), pack(new_second))
```

```python
import functools
import math

import jax
import jax.numpy as jnp
from jax import lax
from jax.experimental import pallas as pl
from jax.experimental.pallas import tpu as pltpu
from jax.sharding import PartitionSpec as P

D = 256
INNER = 512
STATE = 16
RANK = 16
KERNEL = 4
SLOTS = 4
STEP_COUNT = 10
PARAMS = 438016
MATRIX_END = 425984
BETA_ONE = 0.9
BETA_TWO = 0.95
ADAM_EPSILON = 1e-08
RATE_MATRIX = 0.1
RATE_VECTOR = 0.5
WEIGHT_DECAY = 0.1
NORM_EPSILON = 1e-05
LOG2E = 1.4426950408889634
LN2 = 0.6931471805599453
CHUNK = 128
GROUP = 16
LANES = 128
BF = jnp.bfloat16
F32 = jnp.float32
NT = (((1,), (1,)), ((), ()))
TN = (((0,), (0,)), ((), ()))


def split_low(value):
    high = value.astype(BF)
    return high, (value - high.astype(F32)).astype(BF)


def dot(a, b, dims=None):
    if dims is None:
        return jnp.dot(a, b, preferred_element_type=F32)
    return lax.dot_general(a, b, dims, preferred_element_type=F32)


def row_sum(value):
    return jnp.sum(value.reshape(value.shape[0] // 8, 8, value.shape[1]), axis=0)


def rows_of(ref, start, count):
    return ref.at[pl.ds(pl.multiple_of(start, count), count)]


def layer_kernel(
    chunks,
    x_ref,
    up_ref,
    flip_ref,
    w_in_ref,
    w_out_ref,
    wx_ref,
    wdt_ref,
    vec_ref,
    rate_ref,
    gain_ref,
    tile_ref,
    sums_ref,
    fold_ref,
    mask_ref,
    out_ref,
    gin_ref,
    gwin_ref,
    gwout_ref,
    gsmall_ref,
    gvec_ref,
    ggain_ref,
    states,
    act_s,
    slope_s,
    delta_s,
    ratio_s,
    dscan_s,
    inner_s,
    proj_s,
    projt_s,
    dread_s,
    dproj_s,
    gated_s,
    copy_s,
    dmix_s,
    mixed_s,
    dnorm_s,
    chunk_a,
    chunk_p,
    y_s,
    u_s,
    gslope_s,
    gsilu_s,
    halo_s,
    dconv_s,
    wide_s,
    diag_s,
    state_s,
):
    window = pl.program_id(0)
    natural = pl.program_id(1)
    phase = pl.program_id(2)
    forward = phase < chunks
    chunk = jnp.where(forward, phase, 2 * chunks - 1 - phase)
    place = jnp.where(natural == 1, chunk, chunks - 1 - chunk)
    row = pl.multiple_of(chunk * CHUNK, CHUNK)
    nat_row = pl.multiple_of(place * CHUNK, CHUNK)
    here = pl.ds(row, CHUNK)
    there = pl.ds(nat_row, CHUNK)
    groups = CHUNK // GROUP
    block = 32
    pieces = range(0, CHUNK, block)

    @pl.when((window == 0) & (natural == 0) & (phase == 0))
    def _():
        gwin_ref[...] = jnp.zeros_like(gwin_ref)
        gwout_ref[...] = jnp.zeros_like(gwout_ref)
        gsmall_ref[...] = jnp.zeros_like(gsmall_ref)
        gvec_ref[...] = jnp.zeros_like(gvec_ref)
        ggain_ref[...] = jnp.zeros_like(ggain_ref)

    @pl.when(phase == 0)
    def _():
        state_s[...] = jnp.zeros_like(state_s)
        halo_s[0:8, :] = jnp.zeros((8, INNER), F32)

    @pl.when(phase == chunks)
    def _():
        state_s[...] = jnp.zeros_like(state_s)
        dconv_s[0:8, :] = jnp.zeros((8, INNER), F32)

    def norm_parts():
        xf = x_ref[0].astype(F32)
        inv = lax.rsqrt(jnp.mean(xf * xf, axis=-1, keepdims=True) + NORM_EPSILON)
        return xf, inv

    def diagonal(high, low, which):
        for part, value in enumerate((high, low)):
            wide = dot(value, tile_ref[which])
            for g in range(groups):
                diag_s[g, part * GROUP : (part + 1) * GROUP, :] = (
                    wide[g * GROUP : (g + 1) * GROUP] * mask_ref[...]
                ).astype(BF)

    def spread(value, index):
        return jnp.broadcast_to(value[index : index + 1, :], (8, LANES))

    @pl.when(forward)
    def _():
        xf, inv = norm_parts()
        normed = (xf * inv * gain_ref[...]).astype(BF)
        copy = dot(flip_ref[0], normed).astype(BF)
        dmix = dot(flip_ref[0], up_ref[0]).astype(BF)
        copy_s[here, :] = copy
        dmix_s[here, :] = dmix
        halo_s[8:, :] = dot(copy, w_in_ref[0, :, :INNER]).astype(BF).astype(F32)
        gate_all = dot(copy, w_in_ref[0, :, INNER:])
        dgated_all = dot(dmix, w_out_ref[0], NT)
        for a in pieces:
            conv = vec_ref[4:5, :]
            for j in range(KERNEL):
                conv = conv + vec_ref[j : j + 1, :] * halo_s[a + 5 + j : a + 5 + j + block, :]
            inner_s[pl.ds(row + a, block), :] = halo_s[8 + a : 8 + a + block, :]
            sig = 1.0 / (1.0 + jnp.exp(-conv))
            act_s[pl.ds(row + a, block), :] = conv * sig
            slope_s[pl.ds(row + a, block), :] = sig * (1.0 + conv * (1.0 - sig))
            gate = gate_all[a : a + block].astype(BF).astype(F32)
            dgated = dgated_all[a : a + block].astype(BF).astype(F32)
            gsig = 1.0 / (1.0 + jnp.exp(-gate))
            gsilu = gate * gsig
            gsilu_s[a : a + block, :] = gsilu
            dscan_s[pl.ds(row + a, block), :] = dgated * gsilu
            gslope_s[a : a + block, :] = dgated * gsig * (1.0 + gate * (1.0 - gsig))
        halo_s[0:8, :] = halo_s[CHUNK : CHUNK + 8, :]
        act_high, act_low = split_low(act_s[here, :])
        proj = dot(act_high, wx_ref[0]) + dot(act_low, wx_ref[0]) + dot(act_high, wx_ref[1])
        proj_s[here, :] = proj
        columns = jnp.transpose(proj)
        projt_s[chunk] = columns[: 3 * STATE]
        proj_high, proj_low = split_low(proj)
        pre_all = (
            dot(proj_high, wdt_ref[0]) + dot(proj_low, wdt_ref[0]) + dot(proj_high, wdt_ref[1])
        )
        for a in pieces:
            pre = pre_all[a : a + block] + vec_ref[5:6, :]
            small = jnp.exp(-jnp.abs(pre))
            delta = jnp.maximum(pre, 0.0) + jnp.log1p(small)
            sig = jnp.where(pre >= 0.0, 1.0, small) / (1.0 + small)
            delta_s[pl.ds(row + a, block), :] = delta
            ratio_s[pl.ds(row + a, block), :] = jnp.where(delta > 1e-30, sig / delta, 1.0)
            u_s[a : a + block, :] = delta * act_s[pl.ds(row + a, block), :]
        diagonal(proj_high, proj_low, 1)
        state = [
            [state_s[8 * h : 8 * h + 8, LANES * e : LANES * (e + 1)] for e in range(4)]
            for h in range(2)
        ]
        last = [
            jnp.concatenate([state[0][e], state[1][e]], axis=0).astype(BF) for e in range(4)
        ]
        for g in range(groups):
            base = pl.multiple_of(row + g * GROUP, GROUP)
            steps = delta_s[pl.ds(base, GROUP), :]
            feeds = u_s[g * GROUP : (g + 1) * GROUP, :]
            for t in range(GROUP):
                at = g * GROUP + t
                entry = [
                    jnp.broadcast_to(
                        columns[STATE + 8 * h : STATE + 8 * h + 8, at : at + 1], (8, LANES)
                    )
                    for h in range(2)
                ]
                for e in range(4):
                    lanes = slice(LANES * e, LANES * (e + 1))
                    step = spread(steps[:, lanes], t)
                    feed = spread(feeds[:, lanes], t)
                    for h in range(2):
                        decay = jnp.exp2(step * rate_ref[8 * h : 8 * h + 8, lanes])
                        state[h][e] = decay * state[h][e] + feed * entry[h]
                    states[pl.ds(pl.multiple_of((base + t) * STATE, STATE), STATE), lanes] = last[e]
                    last[e] = jnp.concatenate([state[0][e], state[1][e]], axis=0).astype(BF)
                    chunk_a[at * STATE : (at + 1) * STATE, lanes] = last[e]
            held = chunk_a[g * GROUP * STATE : (g + 1) * GROUP * STATE, :]
            pair = dot(diag_s[g], held)
            y_s[g * GROUP : (g + 1) * GROUP, :] = pair[:GROUP] + pair[GROUP:]
            found = dot(dscan_s[pl.ds(base, GROUP), :].astype(BF), held, NT)
            wide_s[g * GROUP : (g + 1) * GROUP, :] = (found * mask_ref[...]).astype(BF)
        for h in range(2):
            for e in range(4):
                state_s[8 * h : 8 * h + 8, LANES * e : LANES * (e + 1)] = state[h][e]
        dread_s[here, :] = dot(wide_s[...], fold_ref[1])
        for a in pieces:
            scanned = y_s[a : a + block, :] + vec_ref[6:7, :] * act_s[pl.ds(row + a, block), :]
            gated_s[pl.ds(row + a, block), :] = (scanned * gsilu_s[a : a + block, :]).astype(BF)
            dproj_s[pl.ds(row + a, block), INNER:] = (
                scanned * gslope_s[a : a + block, :]
            ).astype(BF)
        back = dot(flip_ref[0], gated_s[here, :]).astype(BF)
        mixed = dot(back, w_out_ref[0])

        @pl.when(natural == 0)
        def _():
            mixed_s[there, :] = mixed

        @pl.when(natural == 1)
        def _():
            out_ref[0] = (x_ref[0].astype(F32) + (mixed + mixed_s[there, :])).astype(BF)

        @pl.when(phase == chunks - 1)
        def _():
            gwout_ref[1 - natural] += dot(gated_s[...], dmix_s[...], TN)

    @pl.when(jnp.logical_not(forward))
    def _():
        dconv_s[CHUNK : CHUNK + 8, :] = dconv_s[0:8, :]
        proj = proj_s[here, :]
        proj_high, proj_low = split_low(proj)
        diagonal(proj_high, proj_low, 0)
        columns = projt_s[chunk]
        for a in pieces:
            u_s[a : a + block, :] = (
                delta_s[pl.ds(row + a, block), :] * act_s[pl.ds(row + a, block), :]
            )
        carry = [
            [state_s[8 * h : 8 * h + 8, LANES * e : LANES * (e + 1)] for e in range(4)]
            for h in range(2)
        ]
        rate_sum = None
        for g in reversed(range(groups)):
            base = pl.multiple_of(row + g * GROUP, GROUP)
            steps = delta_s[pl.ds(base, GROUP), :]
            feeds = dscan_s[pl.ds(base, GROUP), :]
            for t in reversed(range(GROUP)):
                at = g * GROUP + t
                read = [
                    jnp.broadcast_to(
                        columns[2 * STATE + 8 * h : 2 * STATE + 8 * h + 8, at : at + 1], (8, LANES)
                    )
                    for h in range(2)
                ]
                for e in range(4):
                    lanes = slice(LANES * e, LANES * (e + 1))
                    step = spread(steps[:, lanes], t)
                    feed = spread(feeds[:, lanes], t)
                    before = states[
                        pl.ds(pl.multiple_of((base + t) * STATE, STATE), STATE), lanes
                    ].astype(F32)
                    lams = []
                    prods = []
                    for h in range(2):
                        power = step * rate_ref[8 * h : 8 * h + 8, lanes]
                        lam = feed * read[h] + carry[h][e]
                        carry[h][e] = jnp.exp2(power) * lam
                        lams.append(lam)
                        prods.append(power * (carry[h][e] * before[8 * h : 8 * h + 8]))
                    chunk_a[at * STATE : (at + 1) * STATE, lanes] = jnp.concatenate(
                        lams, axis=0
                    ).astype(BF)
                    chunk_p[at * STATE : (at + 1) * STATE, lanes] = jnp.concatenate(
                        prods, axis=0
                    ).astype(BF)
            span = slice(g * GROUP * STATE, (g + 1) * GROUP * STATE)
            held = chunk_a[span, :]
            pair = dot(diag_s[g], held)
            y_s[g * GROUP : (g + 1) * GROUP, :] = pair[:GROUP] + pair[GROUP:]
            both = dot(sums_ref[...], chunk_p[span, :])
            gslope_s[g * GROUP : (g + 1) * GROUP, :] = both[:GROUP]
            rate_sum = both[GROUP:] if rate_sum is None else rate_sum + both[GROUP:]
            found = dot(u_s[g * GROUP : (g + 1) * GROUP, :].astype(BF), held, NT)
            wide_s[g * GROUP : (g + 1) * GROUP, :] = (found * mask_ref[...]).astype(BF)
        for h in range(2):
            for e in range(4):
                state_s[8 * h : 8 * h + 8, LANES * e : LANES * (e + 1)] = carry[h][e]
        gsmall_ref[0:STATE, :] += rate_sum * LN2
        for a in pieces:
            here_a = pl.ds(row + a, block)
            dfeed = y_s[a : a + block, :]
            dpre = ratio_s[here_a, :] * (
                gslope_s[a : a + block, :] * LN2 + dfeed * u_s[a : a + block, :]
            )
            gsilu_s[a : a + block, :] = dpre
            dscan = dscan_s[here_a, :]
            y_s[a : a + block, :] = dscan * vec_ref[6:7, :] + dfeed * delta_s[here_a, :]
            gvec_ref[5] += row_sum(dpre)
            gvec_ref[6] += row_sum(dscan * act_s[here_a, :])
        dpre_high, dpre_low = split_low(gsilu_s[...])
        dproj = (
            dot(dpre_high, wdt_ref[0], NT)
            + dot(dpre_low, wdt_ref[0], NT)
            + dot(dpre_high, wdt_ref[1], NT)
            + dot(wide_s[...], fold_ref[0])
            + dread_s[here, :]
        )
        dproj_high, dproj_low = split_low(dproj)
        gsmall_ref[STATE : 2 * STATE, :] += dot(columns[:RANK].astype(BF), dpre_high)
        turned = jnp.transpose(dproj)[: 3 * STATE].astype(BF)
        gsmall_ref[2 * STATE : 5 * STATE, :] += dot(turned, act_s[here, :].astype(BF))
        extra = (
            dot(dproj_high, wx_ref[0], NT)
            + dot(dproj_low, wx_ref[0], NT)
            + dot(dproj_high, wx_ref[1], NT)
        )
        for a in pieces:
            dconv_s[a : a + block, :] = (
                y_s[a : a + block, :] + extra[a : a + block]
            ) * slope_s[pl.ds(row + a, block), :]
        for a in pieces:
            inner = inner_s[pl.ds(row + a, block), :]
            dinner = None
            for j in range(KERNEL):
                moved = dconv_s[a + 3 - j : a + 3 - j + block, :]
                term = vec_ref[j : j + 1, :] * moved
                dinner = term if dinner is None else dinner + term
                gvec_ref[j] += row_sum(moved * inner)
                if j == KERNEL - 1:
                    gvec_ref[4] += row_sum(moved)
            dproj_s[pl.ds(row + a, block), :INNER] = dinner.astype(BF)
        back = dot(flip_ref[0], dproj_s[here, :]).astype(BF)
        dnorm = dot(back, w_in_ref[0], NT)

        @pl.when(natural == 0)
        def _():
            dnorm_s[there, :] = dnorm

        @pl.when(natural == 1)
        def _():
            xf, inv = norm_parts()
            total = dnorm + dnorm_s[there, :]
            scaled = total * gain_ref[...]
            hat = xf * inv
            ggain_ref[...] += row_sum(total * hat)
            mean = jnp.mean(scaled * hat, axis=-1, keepdims=True)
            gin_ref[0] = up_ref[0].astype(F32) + inv * (scaled - hat * mean)

        @pl.when(phase == 2 * chunks - 1)
        def _():
            gwin_ref[1 - natural] += dot(copy_s[...], dproj_s[...], TN)


def run_layer(x, up, w_in, w_x, w_dt, w_out, conv_w, conv_b, dt_bias, a_log, d_skip, gain, perm):
    windows, length, _ = x.shape
    chunks = length // CHUNK
    w_in_pair = jnp.stack([w_in, dot(perm, w_in, TN).astype(BF)])
    w_out_pair = jnp.stack([w_out, dot(w_out, perm).astype(BF)])
    wx_pair = jnp.pad(jnp.stack(w_x), ((0, 0), (0, 0), (0, LANES - w_x[0].shape[1])))
    wdt_pair = jnp.pad(jnp.stack(w_dt), ((0, 0), (0, LANES - RANK), (0, 0)))
    vec = jnp.concatenate(
        [conv_w.T, conv_b[None], dt_bias[None], d_skip[None], jnp.zeros((1, INNER), F32)], axis=0
    )
    rate = (-LOG2E) * jnp.exp(a_log).T
    flip = jnp.stack([jnp.eye(CHUNK, dtype=BF), jnp.eye(CHUNK, dtype=BF)[::-1]])
    wide = GROUP * STATE
    lane = jnp.arange(wide)
    narrow = jnp.arange(LANES)
    tile = jnp.stack(
        [(narrow[:, None] == base + lane[None, :] % STATE) for base in (STATE, 2 * STATE)]
    ).astype(BF)
    fold = jnp.swapaxes(tile, 1, 2)
    mask = jnp.arange(GROUP)[:, None] == lane[None, :] // STATE
    sums = jnp.concatenate([mask, jnp.arange(STATE)[:, None] == lane[None, :] % STATE]).astype(BF)
    mask = mask.astype(F32)

    def of_chunk(w, q, p):
        c = jnp.where(p < chunks, p, 2 * chunks - 1 - p)
        return (w, jnp.where(q == 1, c, chunks - 1 - c), 0)

    def out_chunk(w, q, p):
        return (w, jnp.where(q == 1, jnp.minimum(p, chunks - 1), 0), 0)

    def gin_chunk(w, q, p):
        return (w, jnp.where(q == 1, jnp.minimum(2 * chunks - 1 - p, chunks - 1), chunks - 1), 0)

    def whole(shape):
        return pl.BlockSpec(shape, lambda w, q, p: (0,) * len(shape))

    def of_copy(shape):
        return pl.BlockSpec((1,) + shape[1:], lambda w, q, p: (1 - q,) + (0,) * (len(shape) - 1))

    piece = (1, CHUNK, D)
    operands = (
        x, up, flip, w_in_pair, w_out_pair, wx_pair, wdt_pair, vec, rate, gain[None], tile, sums, fold, mask,
    )
    in_specs = [
        pl.BlockSpec(piece, of_chunk),
        pl.BlockSpec(piece, of_chunk),
        of_copy(flip.shape),
        of_copy(w_in_pair.shape),
        of_copy(w_out_pair.shape),
    ] + [whole(item.shape) for item in operands[5:]]
    grads = [
        jax.ShapeDtypeStruct((2, D, 2 * INNER), F32),
        jax.ShapeDtypeStruct((2, INNER, D), F32),
        jax.ShapeDtypeStruct((5 * STATE, INNER), F32),
        jax.ShapeDtypeStruct((7, 8, INNER), F32),
        jax.ShapeDtypeStruct((8, D), F32),
    ]
    wide_f32 = pltpu.VMEM((length, INNER), F32)
    chunk_f32 = pltpu.VMEM((CHUNK, INNER), F32)
    return pl.pallas_call(
        functools.partial(layer_kernel, chunks),
        grid=(windows, 2, 2 * chunks),
        in_specs=in_specs,
        out_specs=[pl.BlockSpec(piece, out_chunk), pl.BlockSpec(piece, gin_chunk)]
        + [whole(item.shape) for item in grads],
        out_shape=[
            jax.ShapeDtypeStruct(x.shape, BF),
            jax.ShapeDtypeStruct(x.shape, F32),
        ]
        + grads,
        scratch_shapes=[
            pltpu.VMEM((length * STATE, INNER), BF),
            wide_f32,
            wide_f32,
            wide_f32,
            wide_f32,
            wide_f32,
            wide_f32,
            pltpu.VMEM((length, LANES), F32),
            pltpu.VMEM((chunks, 3 * STATE, CHUNK), F32),
            pltpu.VMEM((length, LANES), F32),
            pltpu.VMEM((length, 2 * INNER), BF),
            pltpu.VMEM((length, INNER), BF),
            pltpu.VMEM((length, D), BF),
            pltpu.VMEM((length, D), BF),
            pltpu.VMEM((length, D), F32),
            pltpu.VMEM((length, D), F32),
            pltpu.VMEM((CHUNK * STATE, INNER), BF),
            pltpu.VMEM((CHUNK * STATE, INNER), BF),
            chunk_f32,
            chunk_f32,
            chunk_f32,
            chunk_f32,
            pltpu.VMEM((CHUNK + 8, INNER), F32),
            pltpu.VMEM((CHUNK + 8, INNER), F32),
            pltpu.VMEM((CHUNK, wide), BF),
            pltpu.VMEM((CHUNK // GROUP, 2 * GROUP, wide), BF),
            pltpu.VMEM((STATE, INNER), F32),
        ],
        compiler_params=pltpu.CompilerParams(vmem_limit_bytes=62 * 2**20),
    )(*operands)


def layer_grads(results, complement_map):
    gwin, gwout, gsmall, gvec, ggain = results
    vec = jnp.sum(gvec, axis=1)
    return [
        gwin[0] + jnp.take(gwin[1], complement_map, axis=0),
        gsmall[2 * STATE :].T,
        gsmall[STATE : 2 * STATE],
        gwout[0] + jnp.take(gwout[1], complement_map, axis=1),
        vec[:KERNEL].T,
        vec[4],
        vec[5],
        gsmall[:STATE].T,
        vec[6],
        jnp.sum(ggain, axis=0),
    ]


def param_shapes():
    return [
        (D, 2 * INNER),
        (INNER, RANK + 2 * STATE),
        (RANK, INNER),
        (INNER, D),
        (INNER, KERNEL),
        (INNER,),
        (INNER,),
        (INNER, STATE),
        (INNER,),
        (D,),
    ]


def bounds():
    edges = [0]
    for shape in param_shapes():
        edges.append(edges[-1] + math.prod(shape))
    return edges


def slot_index(owners):
    count = owners.shape[0]
    order = jnp.arange(count, dtype=jnp.int32)
    same = (owners[None, :] == owners[:, None]) & (order[None, :] < order[:, None])
    return jnp.sum(same.astype(jnp.int32), axis=1)


def swap(value, axis, bit, size):
    return lax.ppermute(value, axis, [(i, i ^ bit) for i in range(size)])


def fine_blocks(block_len):
    edges = bounds()
    wanted = []
    for begin, end in ((edges[1], edges[3]), (edges[4], edges[10])):
        wanted.extend(range(begin // block_len, (end - 1) // block_len + 1))
    return sorted(set(wanted))


def gather_params(weights, owners, rank, matches):
    size = lax.axis_size("dp")
    me = lax.axis_index("dp")
    core = lax.axis_index("seq")
    block_len = weights.shape[1]
    half = block_len // 2
    mine = lax.dynamic_slice_in_dim(weights, core * half, half, 1)
    high, low = split_low(mine)
    special = fine_blocks(block_len)
    fine = jnp.sum(
        jnp.where(
            matches[:, special].T[:, :, None], low.astype(F32)[None], 0.0
        ),
        axis=1,
    ).astype(BF)
    many = high[None]
    spot = jnp.zeros_like(owners)
    bit = size // 2
    step = 0
    while bit:
        both = jnp.concatenate([many.reshape(-1, half), fine], axis=0)
        got = swap(both, "dp", bit, size)
        count = many.shape[0]
        many = jnp.concatenate([many, got[: count * SLOTS].reshape(count, SLOTS, half)], axis=0)
        fine = fine + got[count * SLOTS :]
        spot = spot + jnp.where(((owners ^ me) & bit) != 0, 1 << step, 0)
        step += 1
        bit //= 2
    rows = many.reshape(-1, half)[spot * SLOTS + rank]
    both = jnp.concatenate([rows, fine], axis=0)
    other = swap(both, "seq", 1, 2)
    first = jnp.where(core == 0, both, other)
    second = jnp.where(core == 0, other, both)
    full = jnp.concatenate([first, second], axis=1)
    blocks = owners.shape[0]
    return full[:blocks].reshape(-1), full[blocks:], special


def fine_range(table, special, block_len, begin, end):
    first, last = begin // block_len, (end - 1) // block_len
    rows = table[special.index(first) : special.index(last) + 1].reshape(-1)
    return rows[begin - first * block_len : end - first * block_len]


def on_device(
    inputs, cotangent, loss_mask, complement_map, owners, weights, first_moment, second_moment
):
    size = lax.axis_size("dp")
    me = lax.axis_index("dp")
    core = lax.axis_index("seq")
    blocks_count = owners.shape[0]
    block_len = weights.shape[1]
    half = block_len // 2
    upstream = cotangent * loss_mask.astype(BF)[..., None]
    sent = jnp.concatenate([inputs, upstream], axis=2)
    held = lax.all_to_all(sent, "seq", split_axis=0, concat_axis=1, tiled=True)
    x, up = held[:, :, :D], held[:, :, D:]

    rank = slot_index(owners)
    order = jnp.arange(blocks_count, dtype=jnp.int32)
    matches = (owners[None, :] == me) & (
        rank[None, :] == jnp.arange(SLOTS, dtype=jnp.int32)[:, None]
    )
    occupied = jnp.any(matches, axis=1)
    block_of = jnp.sum(jnp.where(matches, order[None, :], 0), axis=1)
    theta, fine, special = gather_params(weights, owners, rank, matches)
    edges = bounds()
    shapes = param_shapes()

    def high_of(index):
        return theta[edges[index] : edges[index + 1]].reshape(shapes[index])

    def low_of(index):
        return fine_range(fine, special, block_len, edges[index], edges[index + 1]).reshape(
            shapes[index]
        )

    def full_of(index):
        return high_of(index).astype(F32) + low_of(index).astype(F32)

    perm = (complement_map[:, None] == jnp.arange(D, dtype=jnp.int32)[None, :]).astype(BF)
    results = run_layer(
        x,
        up,
        high_of(0),
        (high_of(1), low_of(1)),
        (high_of(2), low_of(2)),
        high_of(3),
        *[full_of(index) for index in range(4, 10)],
        perm,
    )
    output, grad_input = results[:2]
    output = lax.all_to_all(output, "seq", split_axis=1, concat_axis=0, tiled=True)
    grad_input = lax.all_to_all(grad_input, "seq", split_axis=1, concat_axis=0, tiled=True)

    pieces = layer_grads(results[2:], complement_map)
    flat_grad = jnp.concatenate([item.reshape(-1) for item in pieces])
    grad_blocks = jnp.pad(flat_grad, (0, blocks_count * block_len - PARAMS)).reshape(
        blocks_count, block_len
    )
    given = lax.dynamic_slice_in_dim(grad_blocks, (1 - core) * half, half, 1)
    kept = lax.dynamic_slice_in_dim(grad_blocks, core * half, half, 1)
    chip = kept + swap(given, "seq", 1, 2)
    slot_of = owners * SLOTS + rank
    source = jnp.full((size * SLOTS,), blocks_count, jnp.int32).at[slot_of].set(order)
    padded = jnp.concatenate([chip.astype(BF), jnp.zeros((1, half), BF)], axis=0)
    routed = lax.all_to_all(padded[source], "dp", split_axis=0, concat_axis=0, tiled=True)
    owned_half = jnp.sum(routed.reshape(size, SLOTS, half).astype(F32), axis=0)
    other_half = swap(owned_half, "seq", 1, 2)
    owned = jnp.where(
        core == 0,
        jnp.concatenate([owned_half, other_half], axis=1),
        jnp.concatenate([other_half, owned_half], axis=1),
    )
    new_first = BETA_ONE * first_moment + (1.0 - BETA_ONE) * owned
    new_second = BETA_TWO * second_moment + (1.0 - BETA_TWO) * owned * owned
    position = block_of[:, None] * block_len + jnp.arange(block_len, dtype=jnp.int32)[None, :]
    is_matrix = position < MATRIX_END
    rate = jnp.where(is_matrix, RATE_MATRIX, RATE_VECTOR)
    decay = jnp.where(is_matrix, WEIGHT_DECAY, 0.0)
    corrected = (
        new_first
        / (1.0 - BETA_ONE**STEP_COUNT)
        / (jnp.sqrt(new_second / (1.0 - BETA_TWO**STEP_COUNT)) + ADAM_EPSILON)
    )
    new_theta = weights - rate * (corrected + decay * weights)
    keep = occupied[:, None]
    return (
        output,
        grad_input,
        jnp.where(keep, new_theta, 0.0),
        jnp.where(keep, new_first, 0.0),
        jnp.where(keep, new_second, 0.0),
    )


def solution(mesh):
    in_specs = (
        P("dp", "seq", None),
        P("dp", "seq", None),
        P("dp", "seq"),
        P(),
        P(),
        P("dp", None),
        P("dp", None),
        P("dp", None),
    )
    out_specs = (
        P("dp", "seq", None),
        P("dp", "seq", None),
        P("dp", None),
        P("dp", None),
        P("dp", None),
    )
    return jax.shard_map(
        on_device, mesh=mesh, in_specs=in_specs, out_specs=out_specs, check_vma=False
    )
```

```python
import functools
import math

import jax
import jax.numpy as jnp
from jax import lax
from jax.experimental import pallas as pl
from jax.experimental.pallas import tpu as pltpu
from jax.sharding import PartitionSpec as P

D = 256
INNER = 512
STATE = 16
RANK = 16
KERNEL = 4
SLOTS = 4
STEP_COUNT = 10
PARAMS = 438016
MATRIX_END = 425984
BETA_ONE = 0.9
BETA_TWO = 0.95
ADAM_EPSILON = 1e-08
RATE_MATRIX = 0.1
RATE_VECTOR = 0.5
WEIGHT_DECAY = 0.1
NORM_EPSILON = 1e-05
LOG2E = 1.4426950408889634
LN2 = 0.6931471805599453
CHUNK = 128
GROUP = 16
LANES = 128
BF = jnp.bfloat16
F32 = jnp.float32
NT = (((1,), (1,)), ((), ()))
TN = (((0,), (0,)), ((), ()))


def split_low(value):
    high = value.astype(BF)
    return high, (value - high.astype(F32)).astype(BF)


def dot(a, b, dims=None):
    if dims is None:
        return jnp.dot(a, b, preferred_element_type=F32)
    return lax.dot_general(a, b, dims, preferred_element_type=F32)


def row_sum(value):
    return jnp.sum(value.reshape(value.shape[0] // 8, 8, value.shape[1]), axis=0)


def rows_of(ref, start, count):
    return ref.at[pl.ds(pl.multiple_of(start, count), count)]


def layer_kernel(
    chunks,
    x_ref,
    up_ref,
    flip_ref,
    w_in_ref,
    w_out_ref,
    wx_ref,
    wdt_ref,
    vec_ref,
    rate_ref,
    gain_ref,
    tile_ref,
    sums_ref,
    fold_ref,
    mask_ref,
    out_ref,
    gin_ref,
    gwin_ref,
    gwout_ref,
    gsmall_ref,
    gvec_ref,
    ggain_ref,
    states,
    act_s,
    slope_s,
    delta_s,
    ratio_s,
    dscan_s,
    inner_s,
    proj_s,
    projt_s,
    dread_s,
    dproj_s,
    gated_s,
    copy_s,
    dmix_s,
    mixed_s,
    dnorm_s,
    chunk_a,
    chunk_p,
    y_s,
    u_s,
    gslope_s,
    gsilu_s,
    halo_s,
    dconv_s,
    wide_s,
    diag_s,
    state_s,
):
    window = pl.program_id(0)
    natural = pl.program_id(1)
    phase = pl.program_id(2)
    forward = phase < chunks
    chunk = jnp.where(forward, phase, 2 * chunks - 1 - phase)
    place = jnp.where(natural == 1, chunk, chunks - 1 - chunk)
    row = pl.multiple_of(chunk * CHUNK, CHUNK)
    nat_row = pl.multiple_of(place * CHUNK, CHUNK)
    here = pl.ds(row, CHUNK)
    there = pl.ds(nat_row, CHUNK)
    groups = CHUNK // GROUP
    block = 32
    pieces = range(0, CHUNK, block)

    @pl.when((window == 0) & (natural == 0) & (phase == 0))
    def _():
        gwin_ref[...] = jnp.zeros_like(gwin_ref)
        gwout_ref[...] = jnp.zeros_like(gwout_ref)
        gsmall_ref[...] = jnp.zeros_like(gsmall_ref)
        gvec_ref[...] = jnp.zeros_like(gvec_ref)
        ggain_ref[...] = jnp.zeros_like(ggain_ref)

    @pl.when(phase == 0)
    def _():
        state_s[...] = jnp.zeros_like(state_s)
        halo_s[0:8, :] = jnp.zeros((8, INNER), F32)

    @pl.when(phase == chunks)
    def _():
        state_s[...] = jnp.zeros_like(state_s)
        dconv_s[0:8, :] = jnp.zeros((8, INNER), F32)

    def norm_parts():
        xf = x_ref[0].astype(F32)
        inv = lax.rsqrt(jnp.mean(xf * xf, axis=-1, keepdims=True) + NORM_EPSILON)
        return xf, inv

    def diagonal(high, low, which):
        for part, value in enumerate((high, low)):
            wide = dot(value, tile_ref[which])
            for g in range(groups):
                diag_s[g, part * GROUP : (part + 1) * GROUP, :] = (
                    wide[g * GROUP : (g + 1) * GROUP] * mask_ref[...]
                ).astype(BF)

    def spread(value, index):
        return jnp.broadcast_to(value[index : index + 1, :], (8, LANES))

    @pl.when(forward)
    def _():
        xf, inv = norm_parts()
        normed = (xf * inv * gain_ref[...]).astype(BF)
        copy = dot(flip_ref[0], normed).astype(BF)
        dmix = dot(flip_ref[0], up_ref[0]).astype(BF)
        copy_s[here, :] = copy
        dmix_s[here, :] = dmix
        halo_s[8:, :] = dot(copy, w_in_ref[0, :, :INNER]).astype(BF).astype(F32)
        gate_all = dot(copy, w_in_ref[0, :, INNER:])
        dgated_all = dot(dmix, w_out_ref[0], NT)
        for a in pieces:
            conv = vec_ref[4:5, :]
            for j in range(KERNEL):
                conv = conv + vec_ref[j : j + 1, :] * halo_s[a + 5 + j : a + 5 + j + block, :]
            inner_s[pl.ds(row + a, block), :] = halo_s[8 + a : 8 + a + block, :]
            sig = 1.0 / (1.0 + jnp.exp(-conv))
            act_s[pl.ds(row + a, block), :] = conv * sig
            slope_s[pl.ds(row + a, block), :] = sig * (1.0 + conv * (1.0 - sig))
            gate = gate_all[a : a + block].astype(BF).astype(F32)
            dgated = dgated_all[a : a + block].astype(BF).astype(F32)
            gsig = 1.0 / (1.0 + jnp.exp(-gate))
            gsilu = gate * gsig
            gsilu_s[a : a + block, :] = gsilu
            dscan_s[pl.ds(row + a, block), :] = dgated * gsilu
            gslope_s[a : a + block, :] = dgated * gsig * (1.0 + gate * (1.0 - gsig))
        halo_s[0:8, :] = halo_s[CHUNK : CHUNK + 8, :]
        act_high, act_low = split_low(act_s[here, :])
        proj = dot(act_high, wx_ref[...]) + dot(act_low, wx_ref[...])
        proj_s[here, :] = proj
        columns = jnp.transpose(proj)
        projt_s[chunk] = columns[: 3 * STATE]
        proj_high, proj_low = split_low(proj)
        pre_all = dot(proj_high, wdt_ref[...]) + dot(proj_low, wdt_ref[...])
        for a in pieces:
            pre = pre_all[a : a + block] + vec_ref[5:6, :]
            small = jnp.exp(-jnp.abs(pre))
            delta = jnp.maximum(pre, 0.0) + jnp.log1p(small)
            sig = jnp.where(pre >= 0.0, 1.0, small) / (1.0 + small)
            delta_s[pl.ds(row + a, block), :] = delta
            ratio_s[pl.ds(row + a, block), :] = jnp.where(delta > 1e-30, sig / delta, 1.0)
            u_s[a : a + block, :] = delta * act_s[pl.ds(row + a, block), :]
        diagonal(proj_high, proj_low, 1)
        state = [
            [state_s[8 * h : 8 * h + 8, LANES * e : LANES * (e + 1)] for e in range(4)]
            for h in range(2)
        ]
        last = [
            jnp.concatenate([state[0][e], state[1][e]], axis=0).astype(BF) for e in range(4)
        ]
        for g in range(groups):
            base = pl.multiple_of(row + g * GROUP, GROUP)
            steps = delta_s[pl.ds(base, GROUP), :]
            feeds = u_s[g * GROUP : (g + 1) * GROUP, :]
            for t in range(GROUP):
                at = g * GROUP + t
                entry = [
                    jnp.broadcast_to(
                        columns[STATE + 8 * h : STATE + 8 * h + 8, at : at + 1], (8, LANES)
                    )
                    for h in range(2)
                ]
                for e in range(4):
                    lanes = slice(LANES * e, LANES * (e + 1))
                    step = spread(steps[:, lanes], t)
                    feed = spread(feeds[:, lanes], t)
                    for h in range(2):
                        decay = jnp.exp2(step * rate_ref[8 * h : 8 * h + 8, lanes])
                        state[h][e] = decay * state[h][e] + feed * entry[h]
                    states[pl.ds(pl.multiple_of((base + t) * STATE, STATE), STATE), lanes] = last[e]
                    last[e] = jnp.concatenate([state[0][e], state[1][e]], axis=0).astype(BF)
                    chunk_a[at * STATE : (at + 1) * STATE, lanes] = last[e]
            held = chunk_a[g * GROUP * STATE : (g + 1) * GROUP * STATE, :]
            pair = dot(diag_s[g], held)
            y_s[g * GROUP : (g + 1) * GROUP, :] = pair[:GROUP] + pair[GROUP:]
            found = dot(dscan_s[pl.ds(base, GROUP), :].astype(BF), held, NT)
            wide_s[g * GROUP : (g + 1) * GROUP, :] = (found * mask_ref[...]).astype(BF)
        for h in range(2):
            for e in range(4):
                state_s[8 * h : 8 * h + 8, LANES * e : LANES * (e + 1)] = state[h][e]
        dread_s[here, :] = dot(wide_s[...], fold_ref[1])
        for a in pieces:
            scanned = y_s[a : a + block, :] + vec_ref[6:7, :] * act_s[pl.ds(row + a, block), :]
            gated_s[pl.ds(row + a, block), :] = (scanned * gsilu_s[a : a + block, :]).astype(BF)
            dproj_s[pl.ds(row + a, block), INNER:] = (
                scanned * gslope_s[a : a + block, :]
            ).astype(BF)
        back = dot(flip_ref[0], gated_s[here, :]).astype(BF)
        mixed = dot(back, w_out_ref[0])

        @pl.when(natural == 0)
        def _():
            mixed_s[there, :] = mixed

        @pl.when(natural == 1)
        def _():
            out_ref[0] = (x_ref[0].astype(F32) + (mixed + mixed_s[there, :])).astype(BF)

        @pl.when(phase == chunks - 1)
        def _():
            gwout_ref[1 - natural] += dot(gated_s[...], dmix_s[...], TN)

    @pl.when(jnp.logical_not(forward))
    def _():
        dconv_s[CHUNK : CHUNK + 8, :] = dconv_s[0:8, :]
        proj = proj_s[here, :]
        proj_high, proj_low = split_low(proj)
        diagonal(proj_high, proj_low, 0)
        columns = projt_s[chunk]
        for a in pieces:
            u_s[a : a + block, :] = (
                delta_s[pl.ds(row + a, block), :] * act_s[pl.ds(row + a, block), :]
            )
        carry = [
            [state_s[8 * h : 8 * h + 8, LANES * e : LANES * (e + 1)] for e in range(4)]
            for h in range(2)
        ]
        rate_sum = None
        for g in reversed(range(groups)):
            base = pl.multiple_of(row + g * GROUP, GROUP)
            steps = delta_s[pl.ds(base, GROUP), :]
            feeds = dscan_s[pl.ds(base, GROUP), :]
            for t in reversed(range(GROUP)):
                at = g * GROUP + t
                read = [
                    jnp.broadcast_to(
                        columns[2 * STATE + 8 * h : 2 * STATE + 8 * h + 8, at : at + 1], (8, LANES)
                    )
                    for h in range(2)
                ]
                for e in range(4):
                    lanes = slice(LANES * e, LANES * (e + 1))
                    step = spread(steps[:, lanes], t)
                    feed = spread(feeds[:, lanes], t)
                    before = states[
                        pl.ds(pl.multiple_of((base + t) * STATE, STATE), STATE), lanes
                    ].astype(F32)
                    lams = []
                    prods = []
                    for h in range(2):
                        power = step * rate_ref[8 * h : 8 * h + 8, lanes]
                        lam = feed * read[h] + carry[h][e]
                        carry[h][e] = jnp.exp2(power) * lam
                        lams.append(lam)
                        prods.append(power * (carry[h][e] * before[8 * h : 8 * h + 8]))
                    chunk_a[at * STATE : (at + 1) * STATE, lanes] = jnp.concatenate(
                        lams, axis=0
                    ).astype(BF)
                    chunk_p[at * STATE : (at + 1) * STATE, lanes] = jnp.concatenate(
                        prods, axis=0
                    ).astype(BF)
            span = slice(g * GROUP * STATE, (g + 1) * GROUP * STATE)
            held = chunk_a[span, :]
            pair = dot(diag_s[g], held)
            y_s[g * GROUP : (g + 1) * GROUP, :] = pair[:GROUP] + pair[GROUP:]
            both = dot(sums_ref[...], chunk_p[span, :])
            gslope_s[g * GROUP : (g + 1) * GROUP, :] = both[:GROUP]
            rate_sum = both[GROUP:] if rate_sum is None else rate_sum + both[GROUP:]
            found = dot(u_s[g * GROUP : (g + 1) * GROUP, :].astype(BF), held, NT)
            wide_s[g * GROUP : (g + 1) * GROUP, :] = (found * mask_ref[...]).astype(BF)
        for h in range(2):
            for e in range(4):
                state_s[8 * h : 8 * h + 8, LANES * e : LANES * (e + 1)] = carry[h][e]
        gsmall_ref[0:STATE, :] += rate_sum * LN2
        for a in pieces:
            here_a = pl.ds(row + a, block)
            dfeed = y_s[a : a + block, :]
            dpre = ratio_s[here_a, :] * (
                gslope_s[a : a + block, :] * LN2 + dfeed * u_s[a : a + block, :]
            )
            gsilu_s[a : a + block, :] = dpre
            dscan = dscan_s[here_a, :]
            y_s[a : a + block, :] = dscan * vec_ref[6:7, :] + dfeed * delta_s[here_a, :]
            gvec_ref[5] += row_sum(dpre)
            gvec_ref[6] += row_sum(dscan * act_s[here_a, :])
        dpre_high, dpre_low = split_low(gsilu_s[...])
        dproj = (
            dot(dpre_high, wdt_ref[...], NT)
            + dot(dpre_low, wdt_ref[...], NT)
            + dot(wide_s[...], fold_ref[0])
            + dread_s[here, :]
        )
        dproj_high, dproj_low = split_low(dproj)
        gsmall_ref[STATE : 2 * STATE, :] += dot(columns[:RANK].astype(BF), dpre_high)
        turned = jnp.transpose(dproj)[: 3 * STATE].astype(BF)
        gsmall_ref[2 * STATE : 5 * STATE, :] += dot(turned, act_s[here, :].astype(BF))
        extra = dot(dproj_high, wx_ref[...], NT) + dot(dproj_low, wx_ref[...], NT)
        for a in pieces:
            dconv_s[a : a + block, :] = (
                y_s[a : a + block, :] + extra[a : a + block]
            ) * slope_s[pl.ds(row + a, block), :]
        for a in pieces:
            inner = inner_s[pl.ds(row + a, block), :]
            dinner = None
            for j in range(KERNEL):
                moved = dconv_s[a + 3 - j : a + 3 - j + block, :]
                term = vec_ref[j : j + 1, :] * moved
                dinner = term if dinner is None else dinner + term
                gvec_ref[j] += row_sum(moved * inner)
                if j == KERNEL - 1:
                    gvec_ref[4] += row_sum(moved)
            dproj_s[pl.ds(row + a, block), :INNER] = dinner.astype(BF)
        back = dot(flip_ref[0], dproj_s[here, :]).astype(BF)
        dnorm = dot(back, w_in_ref[0], NT)

        @pl.when(natural == 0)
        def _():
            dnorm_s[there, :] = dnorm

        @pl.when(natural == 1)
        def _():
            xf, inv = norm_parts()
            total = dnorm + dnorm_s[there, :]
            scaled = total * gain_ref[...]
            hat = xf * inv
            ggain_ref[...] += row_sum(total * hat)
            mean = jnp.mean(scaled * hat, axis=-1, keepdims=True)
            gin_ref[0] = up_ref[0].astype(F32) + inv * (scaled - hat * mean)

        @pl.when(phase == 2 * chunks - 1)
        def _():
            gwin_ref[1 - natural] += dot(copy_s[...], dproj_s[...], TN)


def run_layer(x, up, w_in, w_x, w_dt, w_out, conv_w, conv_b, dt_bias, a_log, d_skip, gain, perm):
    windows, length, _ = x.shape
    chunks = length // CHUNK
    w_in_pair = jnp.stack([w_in, dot(perm, w_in, TN).astype(BF)])
    w_out_pair = jnp.stack([w_out, dot(w_out, perm).astype(BF)])
    wx_wide = jnp.pad(w_x, ((0, 0), (0, LANES - w_x.shape[1])))
    wdt_wide = jnp.pad(w_dt, ((0, LANES - RANK), (0, 0)))
    vec = jnp.concatenate(
        [conv_w.T, conv_b[None], dt_bias[None], d_skip[None], jnp.zeros((1, INNER), F32)], axis=0
    )
    rate = (-LOG2E) * jnp.exp(a_log).T
    flip = jnp.stack([jnp.eye(CHUNK, dtype=BF), jnp.eye(CHUNK, dtype=BF)[::-1]])
    wide = GROUP * STATE
    lane = jnp.arange(wide)
    narrow = jnp.arange(LANES)
    tile = jnp.stack(
        [(narrow[:, None] == base + lane[None, :] % STATE) for base in (STATE, 2 * STATE)]
    ).astype(BF)
    fold = jnp.swapaxes(tile, 1, 2)
    mask = jnp.arange(GROUP)[:, None] == lane[None, :] // STATE
    sums = jnp.concatenate([mask, jnp.arange(STATE)[:, None] == lane[None, :] % STATE]).astype(BF)
    mask = mask.astype(F32)

    def of_chunk(w, q, p):
        c = jnp.where(p < chunks, p, 2 * chunks - 1 - p)
        return (w, jnp.where(q == 1, c, chunks - 1 - c), 0)

    def out_chunk(w, q, p):
        return (w, jnp.where(q == 1, jnp.minimum(p, chunks - 1), 0), 0)

    def gin_chunk(w, q, p):
        return (w, jnp.where(q == 1, jnp.minimum(2 * chunks - 1 - p, chunks - 1), chunks - 1), 0)

    def whole(shape):
        return pl.BlockSpec(shape, lambda w, q, p: (0,) * len(shape))

    def of_copy(shape):
        return pl.BlockSpec((1,) + shape[1:], lambda w, q, p: (1 - q,) + (0,) * (len(shape) - 1))

    piece = (1, CHUNK, D)
    operands = (
        x, up, flip, w_in_pair, w_out_pair, wx_wide, wdt_wide, vec, rate, gain[None], tile, sums, fold, mask,
    )
    in_specs = [
        pl.BlockSpec(piece, of_chunk),
        pl.BlockSpec(piece, of_chunk),
        of_copy(flip.shape),
        of_copy(w_in_pair.shape),
        of_copy(w_out_pair.shape),
    ] + [whole(item.shape) for item in operands[5:]]
    grads = [
        jax.ShapeDtypeStruct((2, D, 2 * INNER), F32),
        jax.ShapeDtypeStruct((2, INNER, D), F32),
        jax.ShapeDtypeStruct((5 * STATE, INNER), F32),
        jax.ShapeDtypeStruct((7, 8, INNER), F32),
        jax.ShapeDtypeStruct((8, D), F32),
    ]
    wide_f32 = pltpu.VMEM((length, INNER), F32)
    chunk_f32 = pltpu.VMEM((CHUNK, INNER), F32)
    return pl.pallas_call(
        functools.partial(layer_kernel, chunks),
        grid=(windows, 2, 2 * chunks),
        in_specs=in_specs,
        out_specs=[pl.BlockSpec(piece, out_chunk), pl.BlockSpec(piece, gin_chunk)]
        + [whole(item.shape) for item in grads],
        out_shape=[
            jax.ShapeDtypeStruct(x.shape, BF),
            jax.ShapeDtypeStruct(x.shape, F32),
        ]
        + grads,
        scratch_shapes=[
            pltpu.VMEM((length * STATE, INNER), BF),
            wide_f32,
            wide_f32,
            wide_f32,
            wide_f32,
            wide_f32,
            wide_f32,
            pltpu.VMEM((length, LANES), F32),
            pltpu.VMEM((chunks, 3 * STATE, CHUNK), F32),
            pltpu.VMEM((length, LANES), F32),
            pltpu.VMEM((length, 2 * INNER), BF),
            pltpu.VMEM((length, INNER), BF),
            pltpu.VMEM((length, D), BF),
            pltpu.VMEM((length, D), BF),
            pltpu.VMEM((length, D), F32),
            pltpu.VMEM((length, D), F32),
            pltpu.VMEM((CHUNK * STATE, INNER), BF),
            pltpu.VMEM((CHUNK * STATE, INNER), BF),
            chunk_f32,
            chunk_f32,
            chunk_f32,
            chunk_f32,
            pltpu.VMEM((CHUNK + 8, INNER), F32),
            pltpu.VMEM((CHUNK + 8, INNER), F32),
            pltpu.VMEM((CHUNK, wide), BF),
            pltpu.VMEM((CHUNK // GROUP, 2 * GROUP, wide), BF),
            pltpu.VMEM((STATE, INNER), F32),
        ],
        compiler_params=pltpu.CompilerParams(vmem_limit_bytes=62 * 2**20),
    )(*operands)


def layer_grads(results, complement_map):
    gwin, gwout, gsmall, gvec, ggain = results
    vec = jnp.sum(gvec, axis=1)
    return [
        gwin[0] + jnp.take(gwin[1], complement_map, axis=0),
        gsmall[2 * STATE :].T,
        gsmall[STATE : 2 * STATE],
        gwout[0] + jnp.take(gwout[1], complement_map, axis=1),
        vec[:KERNEL].T,
        vec[4],
        vec[5],
        gsmall[:STATE].T,
        vec[6],
        jnp.sum(ggain, axis=0),
    ]


def param_shapes():
    return [
        (D, 2 * INNER),
        (INNER, RANK + 2 * STATE),
        (RANK, INNER),
        (INNER, D),
        (INNER, KERNEL),
        (INNER,),
        (INNER,),
        (INNER, STATE),
        (INNER,),
        (D,),
    ]


def bounds():
    edges = [0]
    for shape in param_shapes():
        edges.append(edges[-1] + math.prod(shape))
    return edges


def slot_index(owners):
    count = owners.shape[0]
    order = jnp.arange(count, dtype=jnp.int32)
    same = (owners[None, :] == owners[:, None]) & (order[None, :] < order[:, None])
    return jnp.sum(same.astype(jnp.int32), axis=1)


def swap(value, axis, bit):
    size = lax.axis_size(axis)
    return lax.ppermute(value, axis, [(i, i ^ bit) for i in range(size)])


def up_to(value, multiple):
    return -(-value // multiple) * multiple


def pad_rows(value, rows, axis):
    widths = [(0, 0)] * value.ndim
    widths[axis] = (0, rows - value.shape[axis])
    return jnp.pad(value, widths)


def gather_params(weights, owners, rank, matches):
    size = lax.axis_size("dp")
    me = lax.axis_index("dp")
    core = lax.axis_index("seq")
    blocks, block_len = owners.shape[0], weights.shape[1]
    rows = block_len // LANES
    padded = up_to(rows, 16)
    near = min(4, size)
    tiles = weights.reshape(SLOTS, rows, LANES)
    rounded = lax.reduce_precision(tiles, 8, 7)
    pair = SLOTS // 2
    mine = lax.dynamic_slice_in_dim(rounded, core * pair, pair, 0).astype(BF)
    many = pad_rows(mine, padded, 1).reshape(pair * padded, LANES)
    first = MATRIX_END // block_len
    last = (PARAMS - 1) // block_len + 1
    here = matches[:, first:last].T[:, :, None, None]
    fine = jnp.sum(jnp.where(here, (tiles - rounded)[None], 0.0), axis=1).astype(BF)
    fine_rows = (last - first) * rows
    fine_half = up_to(fine_rows, 32) // 2
    fine = pad_rows(fine.reshape(fine_rows, LANES), 2 * fine_half, 0)
    fine = lax.dynamic_slice_in_dim(fine, core * fine_half, fine_half, 0)
    away = owners ^ me
    spot = jnp.zeros_like(owners)
    bit, step = size // 2, 0
    while bit >= near:
        got = swap(jnp.concatenate([many, fine], axis=0), "dp", bit)
        count = many.shape[0]
        many = jnp.concatenate([many, got[:count]], axis=0)
        fine = fine + got[count:]
        spot = spot + jnp.where((away & bit) != 0, 1 << step, 0)
        bit, step = bit // 2, step + 1
    count = many.shape[0]
    sent = jnp.concatenate([many, fine], axis=0)
    others = [swap(sent, "dp", k) for k in range(1, near)]
    many = jnp.stack([many] + [item[:count] for item in others])
    for item in others:
        fine = fine + item[count:]
    spot = (spot + (away & (near - 1)) * (size // near)) * pair + rank % pair
    chosen = many.reshape(size * pair, padded, LANES)[spot]
    sent = jnp.concatenate([chosen.reshape(blocks * padded, LANES), fine], axis=0)
    got = swap(sent, "seq", 1)
    theirs = got[: blocks * padded].reshape(blocks, padded, LANES)
    local = (rank // pair == core)[:, None, None]
    theta = jnp.where(local, chosen, theirs)[:, :rows].reshape(blocks * rows, LANES)
    fine_got = got[blocks * padded :]
    fine = jnp.concatenate(
        [jnp.where(core == 0, fine, fine_got), jnp.where(core == 0, fine_got, fine)], axis=0
    )
    begin = (MATRIX_END - first * block_len) // LANES
    fine = fine[begin : begin + (PARAMS - MATRIX_END) // LANES]
    return lax.optimization_barrier((theta, fine))


def scatter_sum(value, size):
    me = lax.axis_index("dp")
    stride = 1
    total = value
    while stride < size:
        radix = min(4, size // stride)
        total = total.reshape((size // (stride * radix), radix) + value.shape[1:])
        digit = (me // stride) % radix
        low = total.astype(BF)
        kept = lax.dynamic_index_in_dim(total, digit, 1, keepdims=False).astype(F32)
        for k in range(1, radix):
            given = lax.dynamic_index_in_dim(low, digit ^ k, 1, keepdims=False)
            kept = kept + swap(given, "dp", k * stride).astype(F32)
        total = kept
        stride *= radix
    return total[0]


def trade(value, core):
    half = value.shape[1] // 2
    kept = lax.dynamic_slice_in_dim(value, core * half, half, 1)
    given = lax.dynamic_slice_in_dim(value, (1 - core) * half, half, 1)
    got = swap(given, "seq", 1)
    return jnp.concatenate(
        [jnp.where(core == 0, kept, got), jnp.where(core == 0, got, kept)], axis=0
    )


def untrade(value, core):
    count = value.shape[0] // 2
    kept = lax.dynamic_slice_in_dim(value, core * count, count, 0)
    given = lax.dynamic_slice_in_dim(value, (1 - core) * count, count, 0)
    got = swap(given, "seq", 1)
    return jnp.concatenate(
        [jnp.where(core == 0, kept, got), jnp.where(core == 0, got, kept)], axis=1
    )


def on_device(
    inputs, cotangent, loss_mask, complement_map, owners, weights, first_moment, second_moment
):
    size = lax.axis_size("dp")
    me = lax.axis_index("dp")
    core = lax.axis_index("seq")
    blocks, block_len = owners.shape[0], weights.shape[1]
    rows = block_len // LANES
    pair = SLOTS // 2
    rank = slot_index(owners)
    order = jnp.arange(blocks, dtype=jnp.int32)
    matches = (owners[None, :] == me) & (
        rank[None, :] == jnp.arange(SLOTS, dtype=jnp.int32)[:, None]
    )
    occupied = jnp.any(matches, axis=1)
    block_of = jnp.sum(jnp.where(matches, order[None, :], 0), axis=1)
    theta, fine = gather_params(weights, owners, rank, matches)
    x = untrade(inputs, core)
    up = untrade(cotangent * loss_mask.astype(BF)[..., None], core)

    edges = [edge // LANES for edge in bounds()]
    shapes = param_shapes()
    tail = edges[4]

    def high_of(index):
        return theta[edges[index] : edges[index + 1]].reshape(shapes[index])

    def full_of(index):
        part = theta[edges[index] : edges[index + 1]].astype(F32)
        part = part + fine[edges[index] - tail : edges[index + 1] - tail].astype(F32)
        return part.reshape(shapes[index])

    perm = (complement_map[:, None] == jnp.arange(D, dtype=jnp.int32)[None, :]).astype(BF)
    results = run_layer(
        x, up, *[high_of(index) for index in range(4)], *[full_of(index) for index in range(4, 10)], perm
    )
    pieces = layer_grads(results[2:], complement_map)
    flat_grad = jnp.concatenate([item.reshape(-1) for item in pieces])
    flat_grad = jnp.pad(flat_grad, (0, (blocks + 1) * block_len - PARAMS))
    grad_blocks = flat_grad.reshape(blocks + 1, rows, LANES)
    source = jnp.full((size * SLOTS,), blocks, jnp.int32).at[owners * SLOTS + rank].set(order)
    source = source.reshape(size, 2, pair)

    def for_core(which):
        index = lax.dynamic_index_in_dim(source, which, 1, keepdims=False)
        return grad_blocks[index.reshape(-1)].reshape(size, pair, rows, LANES)

    got = swap(for_core(1 - core).astype(BF), "seq", 1)
    chip = (for_core(core) + got.astype(F32)).astype(BF)
    chip = pad_rows(chip, up_to(rows, 16), 2).reshape(size, -1, LANES)
    summed = scatter_sum(chip, size).reshape(pair, -1, LANES)[:, :rows]
    other = swap(summed, "seq", 1)
    owned = jnp.concatenate(
        [jnp.where(core == 0, summed, other), jnp.where(core == 0, other, summed)], axis=0
    ).reshape(SLOTS, block_len)
    output = trade(results[0], core)
    grad_input = trade(results[1], core)
    new_first = BETA_ONE * first_moment + (1.0 - BETA_ONE) * owned
    new_second = BETA_TWO * second_moment + (1.0 - BETA_TWO) * owned * owned
    position = block_of[:, None] * block_len + jnp.arange(block_len, dtype=jnp.int32)[None, :]
    is_matrix = position < MATRIX_END
    rate = jnp.where(is_matrix, RATE_MATRIX, RATE_VECTOR)
    decay = jnp.where(is_matrix, WEIGHT_DECAY, 0.0)
    corrected = (
        new_first
        / (1.0 - BETA_ONE**STEP_COUNT)
        / (jnp.sqrt(new_second / (1.0 - BETA_TWO**STEP_COUNT)) + ADAM_EPSILON)
    )
    new_theta = weights - rate * (corrected + decay * weights)
    keep = occupied[:, None]
    return (
        output,
        grad_input,
        jnp.where(keep, new_theta, 0.0),
        jnp.where(keep, new_first, 0.0),
        jnp.where(keep, new_second, 0.0),
    )


def solution(mesh):
    in_specs = (
        P("dp", "seq", None),
        P("dp", "seq", None),
        P("dp", "seq"),
        P(),
        P(),
        P("dp", None),
        P("dp", None),
        P("dp", None),
    )
    out_specs = (
        P("dp", "seq", None),
        P("dp", "seq", None),
        P("dp", None),
        P("dp", None),
        P("dp", None),
    )
    return jax.shard_map(
        on_device, mesh=mesh, in_specs=in_specs, out_specs=out_specs, check_vma=False
    )
```

```python
import functools
import math

import jax
import jax.numpy as jnp
from jax import lax
from jax.experimental import pallas as pl
from jax.experimental.pallas import tpu as pltpu
from jax.sharding import PartitionSpec as P

D = 256
INNER = 512
STATE = 16
RANK = 16
KERNEL = 4
SLOTS = 4
STEP_COUNT = 10
PARAMS = 438016
MATRIX_END = 425984
BETA_ONE = 0.9
BETA_TWO = 0.95
ADAM_EPSILON = 1e-08
RATE_MATRIX = 0.1
RATE_VECTOR = 0.5
WEIGHT_DECAY = 0.1
NORM_EPSILON = 1e-05
LOG2E = 1.4426950408889634
LN2 = 0.6931471805599453
CHUNK = 128
GROUP = 16
SLAB = 512
BLOCK = 32
LANES = 128
WIDE = GROUP * STATE
BF = jnp.bfloat16
F32 = jnp.float32
NT = (((1,), (1,)), ((), ()))
TN = (((0,), (0,)), ((), ()))


def split_low(value):
    high = value.astype(BF)
    return high, (value - high.astype(F32)).astype(BF)


def dot(a, b, dims=None):
    if dims is None:
        return jnp.dot(a, b, preferred_element_type=F32)
    return lax.dot_general(a, b, dims, preferred_element_type=F32)


def row_sum(value):
    return jnp.sum(value.reshape(value.shape[0] // 8, 8, value.shape[1]), axis=0)


def span(start, count, step=None):
    return pl.ds(pl.multiple_of(start, step or count), count)


def iota(shape, axis):
    return lax.broadcasted_iota(jnp.int32, shape, axis)


def spread(value, index):
    return jnp.broadcast_to(value[index : index + 1, :], (8, LANES))


def each(count, body):
    lax.fori_loop(0, count, lambda i, c: (body(i), c)[1], 0)


def layer_kernel(
    core_ref,
    x_kept_ref,
    x_got_ref,
    up_kept_ref,
    up_got_ref,
    perm_ref,
    w_in_ref,
    w_out_ref,
    wx_ref,
    wdt_ref,
    vec_ref,
    rate_ref,
    gain_ref,
    out_ref,
    gin_ref,
    gwin_ref,
    gwout_ref,
    gsmall_ref,
    gvec_ref,
    ggain_ref,
    states,
    act_s,
    slope_s,
    delta_s,
    ratio_s,
    dscan_s,
    u_s,
    y_s,
    gsilu_s,
    gslope_s,
    inner_s,
    proj_s,
    dread_s,
    projt_s,
    dproj_s,
    gated_s,
    copy_s,
    dmix_s,
    x_s,
    up_s,
    mixed_s,
    dnorm_s,
    wide_s,
    read_s,
    entry_s,
    w_in_s,
    w_out_s,
    flip_s,
    tile_s,
    fold_s,
    sums_s,
    mask_s,
    near_s,
):
    window = pl.program_id(0)
    natural = pl.program_id(1)
    core = core_ref[0]
    length = x_s.shape[0]
    half = length // 2
    chunks = length // CHUNK
    slabs = length // SLAB
    groups = CHUNK // GROUP
    pieces = range(0, SLAB, BLOCK)

    @pl.when((window == 0) & (natural == 0))
    def _():
        gwin_ref[...] = jnp.zeros_like(gwin_ref)
        gwout_ref[...] = jnp.zeros_like(gwout_ref)
        gsmall_ref[...] = jnp.zeros_like(gsmall_ref)
        gvec_ref[...] = jnp.zeros_like(gvec_ref)
        ggain_ref[...] = jnp.zeros_like(ggain_ref)
        inner_s[0:8, :] = jnp.zeros((8, INNER), F32)
        gsilu_s[length : length + 8, :] = jnp.zeros((8, INNER), F32)
        rows, lanes = iota((CHUNK, CHUNK), 0), iota((CHUNK, CHUNK), 1)
        flip_s[1] = jnp.where(rows == lanes, 1.0, 0.0).astype(BF)
        flip_s[0] = jnp.where(rows + lanes == CHUNK - 1, 1.0, 0.0).astype(BF)
        rows, lanes = iota((LANES, WIDE), 0), iota((LANES, WIDE), 1)
        for k in range(2):
            tile_s[k] = jnp.where(rows == STATE * (k + 1) + lanes % STATE, 1.0, 0.0).astype(BF)
        rows, lanes = iota((WIDE, LANES), 0), iota((WIDE, LANES), 1)
        for k in range(2):
            fold_s[k] = jnp.where(lanes == STATE * (k + 1) + rows % STATE, 1.0, 0.0).astype(BF)
        rows, lanes = iota((GROUP, WIDE), 0), iota((GROUP, WIDE), 1)
        mask = jnp.where(rows == lanes // STATE, 1.0, 0.0)
        mask_s[...] = mask
        sums_s[:GROUP, :] = mask.astype(BF)
        sums_s[GROUP:, :] = jnp.where(rows == lanes % STATE, 1.0, 0.0).astype(BF)

    @pl.when(natural == 0)
    def _():
        kept, got = span(core * half, half), span((1 - core) * half, half)
        x_s[kept, :] = x_kept_ref[0]
        x_s[got, :] = x_got_ref[0]
        up_s[kept, :] = up_kept_ref[0]
        up_s[got, :] = up_got_ref[0]
        w_in_s[...] = dot(perm_ref[...], w_in_ref[...], TN).astype(BF)
        w_out_s[...] = dot(w_out_ref[...], perm_ref[...]).astype(BF)

    @pl.when(natural == 1)
    def _():
        w_in_s[...] = w_in_ref[...]
        w_out_s[...] = w_out_ref[...]

    def place_of(chunk):
        return jnp.where(natural == 1, chunk, chunks - 1 - chunk) * CHUNK

    def norm_parts(rows):
        xf = x_s[rows, :].astype(F32)
        inv = lax.rsqrt(jnp.mean(xf * xf, axis=-1, keepdims=True) + NORM_EPSILON)
        return xf, inv

    def load_copies(chunk):
        there = span(place_of(chunk), CHUNK)
        xf, inv = norm_parts(there)
        normed = (xf * inv * gain_ref[...]).astype(BF)
        copy_s[span(chunk * CHUNK, CHUNK), :] = dot(flip_s[natural], normed).astype(BF)
        dmix_s[span(chunk * CHUNK, CHUNK), :] = dot(flip_s[natural], up_s[there, :]).astype(BF)

    each(chunks, load_copies)

    def project(slab):
        row = slab * SLAB
        copy = copy_s[span(row, SLAB), :]
        inner_s[span(row + 8, SLAB, 8), :] = (
            dot(copy, w_in_s[:, :INNER]).astype(BF).astype(F32)
        )
        gate_all = dot(copy, w_in_s[:, INNER:])
        dgated_all = dot(dmix_s[span(row, SLAB), :], w_out_s[...], NT)
        for a in pieces:
            rows = span(row + a, BLOCK)
            gate = gate_all[a : a + BLOCK].astype(BF).astype(F32)
            dgated = dgated_all[a : a + BLOCK].astype(BF).astype(F32)
            sig = 1.0 / (1.0 + jnp.exp(-gate))
            silu = gate * sig
            gsilu_s[rows, :] = silu
            dscan_s[rows, :] = dgated * silu
            gslope_s[rows, :] = dgated * (sig + silu * (1.0 - sig))

    each(slabs, project)

    def convolve(slab):
        row = slab * SLAB
        near_s[...] = inner_s[span(row, SLAB + 8, 8), :]
        for a in pieces:
            rows = span(row + a, BLOCK)
            conv = vec_ref[4:5, :]
            for j in range(KERNEL):
                conv = conv + vec_ref[j : j + 1, :] * near_s[a + 5 + j : a + 5 + j + BLOCK, :]
            sig = 1.0 / (1.0 + jnp.exp(-conv))
            act = conv * sig
            act_s[rows, :] = act
            slope_s[rows, :] = sig + act * (1.0 - sig)
        act_high, act_low = split_low(act_s[span(row, SLAB), :])
        proj = dot(act_high, wx_ref[...]) + dot(act_low, wx_ref[...])
        proj_s[span(row, SLAB), :] = proj
        for k in range(SLAB // CHUNK):
            turned = jnp.transpose(proj[k * CHUNK : (k + 1) * CHUNK])
            projt_s[slab * (SLAB // CHUNK) + k] = turned[: 3 * STATE]
        proj_high, proj_low = split_low(proj)
        for kind, target in ((0, entry_s), (1, read_s)):
            wide = dot(proj_high, tile_s[kind])
            for g in range(SLAB // GROUP):
                part = wide[g * GROUP : (g + 1) * GROUP] * mask_s[...]
                target[span(row + g * GROUP, GROUP), :] = part.astype(BF)
        pre_all = dot(proj_high, wdt_ref[...]) + dot(proj_low, wdt_ref[...])
        for a in pieces:
            rows = span(row + a, BLOCK)
            pre = pre_all[a : a + BLOCK] + vec_ref[5:6, :]
            small = jnp.exp(-jnp.abs(pre))
            delta = jnp.maximum(pre, 0.0) + jnp.log1p(small)
            sig = jnp.where(pre >= 0.0, 1.0, small) / (1.0 + small)
            delta_s[rows, :] = delta
            ratio_s[rows, :] = jnp.where(delta > 1e-30, sig / delta, 1.0)
            u_s[rows, :] = delta * act_s[rows, :]

    each(slabs, convolve)

    zero = jnp.zeros((8, LANES), F32)
    ones = jnp.ones((GROUP, LANES), BF)
    lane_sets = [slice(LANES * e, LANES * (e + 1)) for e in range(4)]

    def pack(top, bottom):
        return jnp.concatenate([top, bottom], axis=0).astype(BF)

    def scan_chunk(chunk, carry):
        state = [list(carry[0:4]), list(carry[4:8])]
        last = list(carry[8:])
        columns = projt_s[chunk]
        for g in range(groups):
            base = chunk * CHUNK + g * GROUP
            rows = span(base, GROUP)
            steps = delta_s[rows, :]
            feeds = u_s[rows, :]
            pulls = dscan_s[rows, :]
            held, sums = [], []
            for t in range(GROUP):
                at = g * GROUP + t
                entry = [
                    jnp.broadcast_to(
                        columns[STATE + 8 * h : STATE + 8 * h + 8, at : at + 1], (8, LANES)
                    )
                    for h in range(2)
                ]
                place = span((base + t) * STATE, STATE)
                total = [None, None]
                for e, lanes in enumerate(lane_sets):
                    step = spread(steps[:, lanes], t)
                    feed = spread(feeds[:, lanes], t)
                    pull = spread(pulls[:, lanes], t)
                    for h in range(2):
                        decay = jnp.exp2(step * rate_ref[8 * h : 8 * h + 8, lanes])
                        state[h][e] = decay * state[h][e] + feed * entry[h]
                        part = pull * state[h][e]
                        total[h] = part if e == 0 else total[h] + part
                    states[place, lanes] = last[e]
                    last[e] = pack(state[0][e], state[1][e])
                held.append(jnp.concatenate(last, axis=1))
                sums.append(pack(*total))
            y_s[rows, :] = dot(read_s[rows, :], jnp.concatenate(held, axis=0))
            found = dot(ones, jnp.concatenate(sums, axis=0), NT)
            wide_s[rows, :] = (found * mask_s[...]).astype(BF)
        return tuple(state[0] + state[1] + last)

    lax.fori_loop(0, chunks, scan_chunk, (zero,) * 8 + (pack(zero, zero),) * 4)

    def finish(slab):
        row = slab * SLAB
        dread_s[span(row, SLAB), :] = dot(wide_s[span(row, SLAB), :], fold_s[1])
        for a in pieces:
            rows = span(row + a, BLOCK)
            scanned = y_s[rows, :] + vec_ref[6:7, :] * act_s[rows, :]
            gated_s[rows, :] = (scanned * gsilu_s[rows, :]).astype(BF)
            dproj_s[rows, INNER:] = (scanned * gslope_s[rows, :]).astype(BF)

    each(slabs, finish)

    def mirror_mixed(slab):
        mixed_all = dot(gated_s[span(slab * SLAB, SLAB), :], w_out_s[...])
        for k in range(SLAB // CHUNK):
            high, low = split_low(mixed_all[k * CHUNK : (k + 1) * CHUNK])
            there = span(place_of(slab * (SLAB // CHUNK) + k), CHUNK)
            mixed_s[there, :] = dot(flip_s[0], high) + dot(flip_s[0], low)

    def natural_mixed(slab):
        rows = span(slab * SLAB, SLAB)
        mixed = dot(gated_s[rows, :], w_out_s[...])
        total = x_s[rows, :].astype(F32) + (mixed + mixed_s[rows, :])
        out_ref[jnp.where(slab == core, 0, 1), 0] = total.astype(BF)

    @pl.when(natural == 0)
    def _():
        each(slabs, mirror_mixed)
        dmix_s[...] = dot(dmix_s[...], perm_ref[...], NT).astype(BF)

    @pl.when(natural == 1)
    def _():
        each(slabs, natural_mixed)

    gwout_ref[...] += dot(gated_s[...], dmix_s[...], TN)

    def back_chunk(step_index, carry_all):
        chunk = chunks - 1 - step_index
        carry = [list(carry_all[0:4]), list(carry_all[4:8])]
        rate_sum = carry_all[8]
        columns = projt_s[chunk]
        for g in reversed(range(groups)):
            base = chunk * CHUNK + g * GROUP
            rows = span(base, GROUP)
            steps = delta_s[rows, :]
            feeds = dscan_s[rows, :]
            pulls = u_s[rows, :]
            held, prods, sums = [], [], []
            for t in reversed(range(GROUP)):
                at = g * GROUP + t
                read = [
                    jnp.broadcast_to(
                        columns[2 * STATE + 8 * h : 2 * STATE + 8 * h + 8, at : at + 1], (8, LANES)
                    )
                    for h in range(2)
                ]
                place = span((base + t) * STATE, STATE)
                held_row, prod_row = [], []
                total = [None, None]
                for e, lanes in enumerate(lane_sets):
                    step = spread(steps[:, lanes], t)
                    feed = spread(feeds[:, lanes], t)
                    pull = spread(pulls[:, lanes], t)
                    before = states[place, lanes].astype(F32)
                    lams, both = [], []
                    for h in range(2):
                        power = step * rate_ref[8 * h : 8 * h + 8, lanes]
                        lam = feed * read[h] + carry[h][e]
                        carry[h][e] = jnp.exp2(power) * lam
                        lams.append(lam)
                        part = pull * lam
                        total[h] = part if e == 0 else total[h] + part
                        both.append(power * (carry[h][e] * before[8 * h : 8 * h + 8]))
                    held_row.append(pack(*lams))
                    prod_row.append(pack(*both))
                held.insert(0, jnp.concatenate(held_row, axis=1))
                prods.insert(0, jnp.concatenate(prod_row, axis=1))
                sums.insert(0, pack(*total))
            y_s[rows, :] = dot(entry_s[rows, :], jnp.concatenate(held, axis=0))
            both = dot(sums_s[...], jnp.concatenate(prods, axis=0))
            gslope_s[rows, :] = both[:GROUP]
            rate_sum = rate_sum + both[GROUP:]
            found = dot(ones, jnp.concatenate(sums, axis=0), NT)
            wide_s[rows, :] = (found * mask_s[...]).astype(BF)
        return tuple(carry[0] + carry[1]) + (rate_sum,)

    done = lax.fori_loop(
        0, chunks, back_chunk, (zero,) * 8 + (jnp.zeros((STATE, INNER), F32),)
    )
    gsmall_ref[0:STATE, :] += done[8] * LN2

    def gradients(slab):
        row = slab * SLAB
        sum_pre = sum_skip = None
        for a in pieces:
            rows = span(row + a, BLOCK)
            dfeed = y_s[rows, :]
            dpre = ratio_s[rows, :] * (gslope_s[rows, :] * LN2 + dfeed * u_s[rows, :])
            gsilu_s[rows, :] = dpre
            dscan = dscan_s[rows, :]
            y_s[rows, :] = dscan * vec_ref[6:7, :] + dfeed * delta_s[rows, :]
            one, two = row_sum(dpre), row_sum(dscan * act_s[rows, :])
            sum_pre = one if sum_pre is None else sum_pre + one
            sum_skip = two if sum_skip is None else sum_skip + two
        gvec_ref[5] += sum_pre
        gvec_ref[6] += sum_skip
        dpre_all = gsilu_s[span(row, SLAB), :].astype(BF)
        dproj = (
            dot(dpre_all, wdt_ref[...], NT)
            + dot(wide_s[span(row, SLAB), :], fold_s[0])
            + dread_s[span(row, SLAB), :]
        )
        extra = dot(dproj.astype(BF), wx_ref[...], NT)
        low = proj_s[span(row, SLAB), :].astype(BF)
        gsmall_ref[STATE : 2 * STATE, :] += dot(low, dpre_all, TN)[:RANK]
        gsmall_ref[2 * STATE : 5 * STATE, :] += dot(
            dproj.astype(BF), act_s[span(row, SLAB), :].astype(BF), TN
        )[: 3 * STATE]
        for a in pieces:
            rows = span(row + a, BLOCK)
            gsilu_s[rows, :] = (y_s[rows, :] + extra[a : a + BLOCK]) * slope_s[rows, :]

    each(slabs, gradients)

    def unconvolve(slab):
        row = slab * SLAB
        totals = [None] * 5
        near_s[...] = gsilu_s[span(row, SLAB + 8, 8), :]
        for a in pieces:
            rows = span(row + a, BLOCK)
            inner = inner_s[span(row + a + 8, BLOCK, 8), :]
            dinner = None
            for j in range(KERNEL):
                moved = near_s[a + 3 - j : a + 3 - j + BLOCK, :]
                term = vec_ref[j : j + 1, :] * moved
                dinner = term if dinner is None else dinner + term
                part = row_sum(moved * inner)
                totals[j] = part if totals[j] is None else totals[j] + part
            part = row_sum(near_s[a : a + BLOCK, :])
            totals[4] = part if totals[4] is None else totals[4] + part
            dproj_s[rows, :INNER] = dinner.astype(BF)
        for j in range(5):
            gvec_ref[j] += totals[j]

    each(slabs, unconvolve)

    def mirror_dnorm(slab):
        dnorm_all = dot(dproj_s[span(slab * SLAB, SLAB), :], w_in_s[...], NT)
        for k in range(SLAB // CHUNK):
            high, low = split_low(dnorm_all[k * CHUNK : (k + 1) * CHUNK])
            there = span(place_of(slab * (SLAB // CHUNK) + k), CHUNK)
            dnorm_s[there, :] = dot(flip_s[0], high) + dot(flip_s[0], low)

    def natural_dnorm(slab):
        rows = span(slab * SLAB, SLAB)
        total = dot(dproj_s[rows, :], w_in_s[...], NT) + dnorm_s[rows, :]
        xf, inv = norm_parts(rows)
        scaled = total * gain_ref[...]
        hat = xf * inv
        ggain_ref[...] += row_sum(total * hat)
        mean = jnp.mean(scaled * hat, axis=-1, keepdims=True)
        gin_ref[jnp.where(slab == core, 0, 1), 0] = up_s[rows, :].astype(F32) + inv * (
            scaled - hat * mean
        )

    @pl.when(natural == 0)
    def _():
        each(slabs, mirror_dnorm)
        copy_s[...] = dot(copy_s[...], perm_ref[...], NT).astype(BF)

    @pl.when(natural == 1)
    def _():
        each(slabs, natural_dnorm)

    gwin_ref[...] += dot(copy_s[...], dproj_s[...], TN)


def run_layer(
    core, x, x_got, up, up_got, perm, w_in, w_x, w_dt, w_out, conv_w, conv_b, dt_bias, a_log, d_skip, gain
):
    windows, half, _ = x_got.shape
    length = 2 * half
    wx_wide = jnp.pad(w_x, ((0, 0), (0, LANES - w_x.shape[1])))
    wdt_wide = jnp.pad(w_dt, ((0, LANES - RANK), (0, 0)))
    vec = jnp.concatenate(
        [conv_w.T, conv_b[None], dt_bias[None], d_skip[None], jnp.zeros((1, INNER), F32)], axis=0
    )
    rate = (-LOG2E) * jnp.exp(a_log).T

    def whole(shape):
        return pl.BlockSpec(shape, lambda w, q, core: (0,) * len(shape))

    kept = pl.BlockSpec((1, half, D), lambda w, q, core: (windows * core[0] + w, 0, 0))
    got = pl.BlockSpec((1, half, D), lambda w, q, core: (w, 0, 0))
    both = pl.BlockSpec((2, 1, half, D), lambda w, q, core: (0, w, 0, 0))
    fixed = (perm, w_in, w_out, wx_wide, wdt_wide, vec, rate, gain[None])
    grads = [
        jax.ShapeDtypeStruct((D, 2 * INNER), F32),
        jax.ShapeDtypeStruct((INNER, D), F32),
        jax.ShapeDtypeStruct((5 * STATE, INNER), F32),
        jax.ShapeDtypeStruct((7, 8, INNER), F32),
        jax.ShapeDtypeStruct((8, D), F32),
    ]
    inner_f32 = [pltpu.VMEM((length, INNER), F32)]
    outer_bf = [pltpu.VMEM((length, D), BF)]
    outer_f32 = [pltpu.VMEM((length, D), F32)]
    halo_f32 = [pltpu.VMEM((length + 8, INNER), F32)]
    scratch = (
        [pltpu.VMEM((length * STATE, INNER), BF)]
        + inner_f32 * 7
        + halo_f32
        + inner_f32
        + halo_f32
        + [pltpu.VMEM((length, LANES), F32)] * 2
        + [
            pltpu.VMEM((length // CHUNK, 3 * STATE, CHUNK), F32),
            pltpu.VMEM((length, 2 * INNER), BF),
            pltpu.VMEM((length, INNER), BF),
        ]
        + outer_bf * 4
        + outer_f32 * 2
        + [pltpu.VMEM((length, WIDE), BF)] * 3
        + [
            pltpu.VMEM((D, 2 * INNER), BF),
            pltpu.VMEM((INNER, D), BF),
            pltpu.VMEM((2, CHUNK, CHUNK), BF),
            pltpu.VMEM((2, LANES, WIDE), BF),
            pltpu.VMEM((2, WIDE, LANES), BF),
            pltpu.VMEM((2 * GROUP, WIDE), BF),
            pltpu.VMEM((GROUP, WIDE), F32),
            pltpu.VMEM((SLAB + 8, INNER), F32),
        ]
    )
    return pl.pallas_call(
        layer_kernel,
        grid_spec=pltpu.PrefetchScalarGridSpec(
            num_scalar_prefetch=1,
            grid=(windows, 2),
            in_specs=[kept, got, kept, got] + [whole(item.shape) for item in fixed],
            out_specs=[both, both] + [whole(item.shape) for item in grads],
            scratch_shapes=scratch,
        ),
        out_shape=[
            jax.ShapeDtypeStruct((2, windows, half, D), BF),
            jax.ShapeDtypeStruct((2, windows, half, D), F32),
        ]
        + grads,
        compiler_params=pltpu.CompilerParams(vmem_limit_bytes=63 * 2**20),
    )(core.reshape(1).astype(jnp.int32), x, x_got, up, up_got, *fixed)


def layer_grads(results):
    gwin, gwout, gsmall, gvec, ggain = results
    vec = jnp.sum(gvec, axis=1)
    return [
        gwin,
        gsmall[2 * STATE :].T,
        gsmall[STATE : 2 * STATE],
        gwout,
        vec[:KERNEL].T,
        vec[4],
        vec[5],
        gsmall[:STATE].T,
        vec[6],
        jnp.sum(ggain, axis=0),
    ]


def param_shapes():
    return [
        (D, 2 * INNER),
        (INNER, RANK + 2 * STATE),
        (RANK, INNER),
        (INNER, D),
        (INNER, KERNEL),
        (INNER,),
        (INNER,),
        (INNER, STATE),
        (INNER,),
        (D,),
    ]


def bounds():
    edges = [0]
    for shape in param_shapes():
        edges.append(edges[-1] + math.prod(shape))
    return edges


def slot_index(owners):
    count = owners.shape[0]
    order = jnp.arange(count, dtype=jnp.int32)
    same = (owners[None, :] == owners[:, None]) & (order[None, :] < order[:, None])
    return jnp.sum(same.astype(jnp.int32), axis=1)


def swap(value, axis, bit):
    size = lax.axis_size(axis)
    return lax.ppermute(value, axis, [(i, i ^ bit) for i in range(size)])


def up_to(value, multiple):
    return -(-value // multiple) * multiple


def pad_rows(value, rows, axis):
    widths = [(0, 0)] * value.ndim
    widths[axis] = (0, rows - value.shape[axis])
    return jnp.pad(value, widths)


def gather_params(weights, owners, rank, matches):
    size = lax.axis_size("dp")
    me = lax.axis_index("dp")
    core = lax.axis_index("seq")
    blocks, block_len = owners.shape[0], weights.shape[1]
    rows = block_len // LANES
    padded = up_to(rows, 16)
    near = min(4, size)
    tiles = weights.reshape(SLOTS, rows, LANES)
    rounded = lax.reduce_precision(tiles, 8, 7)
    pair = SLOTS // 2
    mine = lax.dynamic_slice_in_dim(rounded, core * pair, pair, 0).astype(BF)
    many = pad_rows(mine, padded, 1).reshape(pair * padded, LANES)
    first = MATRIX_END // block_len
    last = (PARAMS - 1) // block_len + 1
    here = matches[:, first:last].T[:, :, None, None]
    fine = jnp.sum(jnp.where(here, (tiles - rounded)[None], 0.0), axis=1).astype(BF)
    fine_rows = (last - first) * rows
    fine_half = up_to(fine_rows, 32) // 2
    fine = pad_rows(fine.reshape(fine_rows, LANES), 2 * fine_half, 0)
    fine = lax.dynamic_slice_in_dim(fine, core * fine_half, fine_half, 0)
    away = owners ^ me
    spot = jnp.zeros_like(owners)
    bit, step = size // 2, 0
    while bit >= near:
        got = swap(jnp.concatenate([many, fine], axis=0), "dp", bit)
        count = many.shape[0]
        many = jnp.concatenate([many, got[:count]], axis=0)
        fine = fine + got[count:]
        spot = spot + jnp.where((away & bit) != 0, 1 << step, 0)
        bit, step = bit // 2, step + 1
    count = many.shape[0]
    sent = jnp.concatenate([many, fine], axis=0)
    others = [swap(sent, "dp", k) for k in range(1, near)]
    many = jnp.stack([many] + [item[:count] for item in others])
    for item in others:
        fine = fine + item[count:]
    spot = (spot + (away & (near - 1)) * (size // near)) * pair + rank % pair
    chosen = many.reshape(size * pair, padded, LANES)[spot]
    sent = jnp.concatenate([chosen.reshape(blocks * padded, LANES), fine], axis=0)
    got = swap(sent, "seq", 1)
    theirs = got[: blocks * padded].reshape(blocks, padded, LANES)
    local = (rank // pair == core)[:, None, None]
    theta = jnp.where(local, chosen, theirs)[:, :rows].reshape(blocks * rows, LANES)
    fine_got = got[blocks * padded :]
    fine = jnp.concatenate(
        [jnp.where(core == 0, fine, fine_got), jnp.where(core == 0, fine_got, fine)], axis=0
    )
    begin = (MATRIX_END - first * block_len) // LANES
    fine = fine[begin : begin + (PARAMS - MATRIX_END) // LANES]
    return lax.optimization_barrier((theta, fine))


def scatter_sum(value, size):
    me = lax.axis_index("dp")
    stride = 1
    total = value
    while stride < size:
        radix = min(4, size // stride)
        total = total.reshape((size // (stride * radix), radix) + value.shape[1:])
        digit = (me // stride) % radix
        low = total.astype(BF)
        kept = lax.dynamic_index_in_dim(total, digit, 1, keepdims=False).astype(F32)
        for k in range(1, radix):
            given = lax.dynamic_index_in_dim(low, digit ^ k, 1, keepdims=False)
            kept = kept + swap(given, "dp", k * stride).astype(F32)
        total = kept
        stride *= radix
    return total[0]


def other_half(value, core):
    count = value.shape[0] // 2
    return swap(lax.dynamic_slice_in_dim(value, (1 - core) * count, count, 0), "seq", 1)


def by_position(pair, core):
    kept, got = pair[0], swap(pair[1], "seq", 1)
    return jnp.concatenate(
        [jnp.where(core == 0, kept, got), jnp.where(core == 0, got, kept)], axis=0
    )


def on_device(
    inputs, cotangent, loss_mask, complement_map, owners, weights, first_moment, second_moment
):
    size = lax.axis_size("dp")
    me = lax.axis_index("dp")
    core = lax.axis_index("seq")
    blocks, block_len = owners.shape[0], weights.shape[1]
    rows = block_len // LANES
    pair = SLOTS // 2
    rank = slot_index(owners)
    order = jnp.arange(blocks, dtype=jnp.int32)
    matches = (owners[None, :] == me) & (
        rank[None, :] == jnp.arange(SLOTS, dtype=jnp.int32)[:, None]
    )
    occupied = jnp.any(matches, axis=1)
    block_of = jnp.sum(jnp.where(matches, order[None, :], 0), axis=1)
    theta, fine = gather_params(weights, owners, rank, matches)
    upstream = cotangent * loss_mask.astype(BF)[..., None]
    x_got = other_half(inputs, core)
    up_got = other_half(upstream, core)

    edges = [edge // LANES for edge in bounds()]
    shapes = param_shapes()
    tail = edges[4]

    def high_of(index):
        return theta[edges[index] : edges[index + 1]].reshape(shapes[index])

    def full_of(index):
        part = theta[edges[index] : edges[index + 1]].astype(F32)
        part = part + fine[edges[index] - tail : edges[index + 1] - tail].astype(F32)
        return part.reshape(shapes[index])

    perm = (complement_map[:, None] == jnp.arange(D, dtype=jnp.int32)[None, :]).astype(BF)
    results = run_layer(
        core,
        inputs,
        x_got,
        upstream,
        up_got,
        perm,
        *[high_of(index) for index in range(4)],
        *[full_of(index) for index in range(4, 10)],
    )
    pieces = layer_grads(results[2:])
    flat_grad = jnp.concatenate([item.reshape(-1) for item in pieces])
    flat_grad = jnp.pad(flat_grad, (0, (blocks + 1) * block_len - PARAMS))
    grad_blocks = flat_grad.reshape(blocks + 1, rows, LANES)
    source = jnp.full((size * SLOTS,), blocks, jnp.int32).at[owners * SLOTS + rank].set(order)
    source = source.reshape(size, 2, pair)

    def for_core(which):
        index = lax.dynamic_index_in_dim(source, which, 1, keepdims=False)
        return grad_blocks[index.reshape(-1)].reshape(size, pair, rows, LANES)

    got = swap(for_core(1 - core).astype(BF), "seq", 1)
    chip = (for_core(core) + got.astype(F32)).astype(BF)
    chip = pad_rows(chip, up_to(rows, 16), 2).reshape(size, -1, LANES)
    summed = scatter_sum(chip, size).reshape(pair, -1, LANES)[:, :rows]
    other = swap(summed, "seq", 1)
    owned = jnp.concatenate(
        [jnp.where(core == 0, summed, other), jnp.where(core == 0, other, summed)], axis=0
    ).reshape(SLOTS, block_len)
    output = by_position(results[0], core)
    grad_input = by_position(results[1], core)
    new_first = BETA_ONE * first_moment + (1.0 - BETA_ONE) * owned
    new_second = BETA_TWO * second_moment + (1.0 - BETA_TWO) * owned * owned
    position = block_of[:, None] * block_len + jnp.arange(block_len, dtype=jnp.int32)[None, :]
    is_matrix = position < MATRIX_END
    rate = jnp.where(is_matrix, RATE_MATRIX, RATE_VECTOR)
    decay = jnp.where(is_matrix, WEIGHT_DECAY, 0.0)
    corrected = (
        new_first
        / (1.0 - BETA_ONE**STEP_COUNT)
        / (jnp.sqrt(new_second / (1.0 - BETA_TWO**STEP_COUNT)) + ADAM_EPSILON)
    )
    new_theta = weights - rate * (corrected + decay * weights)
    keep = occupied[:, None]
    return (
        output,
        grad_input,
        jnp.where(keep, new_theta, 0.0),
        jnp.where(keep, new_first, 0.0),
        jnp.where(keep, new_second, 0.0),
    )


def solution(mesh):
    in_specs = (
        P("dp", "seq", None),
        P("dp", "seq", None),
        P("dp", "seq"),
        P(),
        P(),
        P("dp", None),
        P("dp", None),
        P("dp", None),
    )
    out_specs = (
        P("dp", "seq", None),
        P("dp", "seq", None),
        P("dp", None),
        P("dp", None),
        P("dp", None),
    )
    return jax.shard_map(
        on_device, mesh=mesh, in_specs=in_specs, out_specs=out_specs, check_vma=False
    )
```

```python
import functools
import math

import jax
import jax.numpy as jnp
from jax import lax
from jax.experimental import pallas as pl
from jax.experimental.pallas import tpu as pltpu
from jax.sharding import PartitionSpec as P

D = 256
INNER = 512
STATE = 16
RANK = 16
KERNEL = 4
SLOTS = 4
STEP_COUNT = 10
PARAMS = 438016
MATRIX_END = 425984
BETA_ONE = 0.9
BETA_TWO = 0.95
ADAM_EPSILON = 1e-08
RATE_MATRIX = 0.1
RATE_VECTOR = 0.5
WEIGHT_DECAY = 0.1
NORM_EPSILON = 1e-05
LOG2E = 1.4426950408889634
LN2 = 0.6931471805599453
CHUNK = 128
GROUP = 16
SLAB = 512
REACH = 256
BLOCK = 32
LANES = 128
WIDE = GROUP * STATE
BF = jnp.bfloat16
F32 = jnp.float32
NT = (((1,), (1,)), ((), ()))
TN = (((0,), (0,)), ((), ()))


def split_low(value):
    high = value.astype(BF)
    return high, (value - high.astype(F32)).astype(BF)


def dot(a, b, dims=None):
    if dims is None:
        return jnp.dot(a, b, preferred_element_type=F32)
    return lax.dot_general(a, b, dims, preferred_element_type=F32)


def row_sum(value):
    return jnp.sum(value.reshape(value.shape[0] // 8, 8, value.shape[1]), axis=0)


def span(start, count, step=None):
    return pl.ds(pl.multiple_of(start, step or count), count)


def iota(shape, axis):
    return lax.broadcasted_iota(jnp.int32, shape, axis)


def spread(value, index):
    return jnp.broadcast_to(value[index : index + 1, :], (8, LANES))


def each(count, body):
    lax.fori_loop(0, count, lambda i, c: (body(i), c)[1], 0)


def layer_kernel(
    core_ref,
    x_kept_ref,
    x_got_ref,
    up_kept_ref,
    up_got_ref,
    perm_ref,
    w_in_ref,
    w_out_ref,
    wx_ref,
    wdt_ref,
    vec_ref,
    rate_ref,
    gain_ref,
    out_kept_ref,
    out_given_ref,
    gin_kept_ref,
    gin_given_ref,
    gwin_ref,
    gwout_ref,
    gsmall_ref,
    gvec_ref,
    ggain_ref,
    states,
    act_s,
    slope_s,
    delta_s,
    ratio_s,
    dscan_s,
    u_s,
    y_s,
    gsilu_s,
    gslope_s,
    inner_s,
    proj_s,
    dread_s,
    projt_s,
    dproj_s,
    gated_s,
    copy_s,
    dmix_s,
    x_s,
    up_s,
    dnorm_s,
    wide_s,
    read_s,
    entry_s,
    w_in_s,
    w_out_s,
    flip_s,
    tile_s,
    fold_s,
    sums_s,
    mask_s,
    near_s,
    wx_s,
    wdt_s,
):
    window = pl.program_id(0)
    natural = pl.program_id(1)
    core = core_ref[0]
    length = x_s.shape[0]
    half = length // 2
    chunks = length // CHUNK
    slabs = length // SLAB
    groups = REACH // GROUP
    pieces = range(0, SLAB, BLOCK)

    @pl.when((window == 0) & (natural == 0))
    def _():
        gwin_ref[...] = jnp.zeros_like(gwin_ref)
        gwout_ref[...] = jnp.zeros_like(gwout_ref)
        gsmall_ref[...] = jnp.zeros_like(gsmall_ref)
        gvec_ref[...] = jnp.zeros_like(gvec_ref)
        ggain_ref[...] = jnp.zeros_like(ggain_ref)
        wx_s[...] = jnp.zeros_like(wx_s)
        wx_s[:, : 3 * STATE] = wx_ref[...]
        wdt_s[...] = jnp.zeros_like(wdt_s)
        wdt_s[:RANK, :] = wdt_ref[...]
        inner_s[0:16, :] = jnp.zeros((16, INNER), BF)
        gsilu_s[length : length + 8, :] = jnp.zeros((8, INNER), F32)
        rows, lanes = iota((CHUNK, CHUNK), 0), iota((CHUNK, CHUNK), 1)
        flip_s[1] = jnp.where(rows == lanes, 1.0, 0.0).astype(BF)
        flip_s[0] = jnp.where(rows + lanes == CHUNK - 1, 1.0, 0.0).astype(BF)
        rows, lanes = iota((LANES, WIDE), 0), iota((LANES, WIDE), 1)
        for k in range(2):
            tile_s[k] = jnp.where(rows == STATE * (k + 1) + lanes % STATE, 1.0, 0.0).astype(BF)
        rows, lanes = iota((WIDE, LANES), 0), iota((WIDE, LANES), 1)
        for k in range(2):
            fold_s[k] = jnp.where(lanes == STATE * (k + 1) + rows % STATE, 1.0, 0.0).astype(BF)
        rows, lanes = iota((GROUP, WIDE), 0), iota((GROUP, WIDE), 1)
        mask = jnp.where(rows == lanes // STATE, 1.0, 0.0)
        mask_s[...] = mask
        sums_s[:GROUP, :] = mask.astype(BF)
        sums_s[GROUP:, :] = jnp.where(rows == lanes % STATE, 1.0, 0.0).astype(BF)

    @pl.when(natural == 0)
    def _():
        kept, got = span(core * half, half), span((1 - core) * half, half)
        x_s[kept, :] = x_kept_ref[0]
        x_s[got, :] = x_got_ref[0]
        up_s[kept, :] = up_kept_ref[0]
        up_s[got, :] = up_got_ref[0]
        w_in_s[...] = dot(perm_ref[...], w_in_ref[...], TN).astype(BF)
        w_out_s[...] = dot(w_out_ref[...], perm_ref[...]).astype(BF)

    @pl.when(natural == 1)
    def _():
        w_in_s[...] = w_in_ref[...]
        w_out_s[...] = w_out_ref[...]

    def place_of(chunk):
        return jnp.where(natural == 1, chunk, chunks - 1 - chunk) * CHUNK

    def norm_parts(rows):
        xf = x_s[rows, :].astype(F32)
        inv = lax.rsqrt(jnp.mean(xf * xf, axis=-1, keepdims=True) + NORM_EPSILON)
        return xf, inv

    def load_copies(chunk):
        there = span(place_of(chunk), CHUNK)
        xf, inv = norm_parts(there)
        normed = (xf * inv * gain_ref[...]).astype(BF)
        copy_s[span(chunk * CHUNK, CHUNK), :] = dot(flip_s[natural], normed).astype(BF)
        dmix_s[span(chunk * CHUNK, CHUNK), :] = dot(flip_s[natural], up_s[there, :]).astype(BF)

    each(chunks, load_copies)

    def project(slab):
        row = slab * SLAB
        copy = copy_s[span(row, SLAB), :]
        inner_s[span(row + 16, SLAB, 16), :] = dot(copy, w_in_s[:, :INNER]).astype(BF)
        gate_all = dot(copy, w_in_s[:, INNER:]).astype(BF)
        dgated_all = dot(dmix_s[span(row, SLAB), :], w_out_s[...], NT).astype(BF)
        for a in pieces:
            rows = span(row + a, BLOCK)
            gate = gate_all[a : a + BLOCK].astype(F32)
            dgated = dgated_all[a : a + BLOCK].astype(F32)
            sig = 1.0 / (1.0 + jnp.exp(-gate))
            silu = gate * sig
            gsilu_s[rows, :] = silu
            dscan_s[rows, :] = dgated * silu
            gslope_s[rows, :] = dgated * (sig + silu * (1.0 - sig))

    each(slabs, project)

    def convolve(slab):
        row = slab * SLAB
        near_s[...] = inner_s[span(row, SLAB + 16, 16), :].astype(F32)
        for a in pieces:
            rows = span(row + a, BLOCK)
            conv = vec_ref[4:5, :]
            for j in range(KERNEL):
                conv = conv + vec_ref[j : j + 1, :] * near_s[a + 13 + j : a + 13 + j + BLOCK, :]
            sig = 1.0 / (1.0 + jnp.exp(-conv))
            act = conv * sig
            act_s[rows, :] = act
            slope_s[rows, :] = sig + act * (1.0 - sig)
        act_high, act_low = split_low(act_s[span(row, SLAB), :])
        proj = dot(act_high, wx_s[...]) + dot(act_low, wx_s[...])
        proj_s[span(row, SLAB), :] = proj.astype(BF)
        for k in range(SLAB // CHUNK):
            turned = jnp.transpose(proj[k * CHUNK : (k + 1) * CHUNK])
            projt_s[slab * (SLAB // CHUNK) + k] = turned[: 3 * STATE]
        proj_high, proj_low = split_low(proj)
        for kind, target in ((0, entry_s), (1, read_s)):
            wide = dot(proj_high, tile_s[kind])
            for g in range(SLAB // GROUP):
                part = wide[g * GROUP : (g + 1) * GROUP] * mask_s[...]
                target[span(row + g * GROUP, GROUP), :] = part.astype(BF)
        pre_all = dot(proj_high, wdt_s[...]) + dot(proj_low, wdt_s[...])
        for a in pieces:
            rows = span(row + a, BLOCK)
            pre = pre_all[a : a + BLOCK] + vec_ref[5:6, :]
            small = jnp.exp(-jnp.abs(pre))
            delta = jnp.maximum(pre, 0.0) + jnp.log1p(small)
            scaled = jnp.where(pre >= 0.0, 1.0, small) / ((1.0 + small) * delta)
            delta_s[rows, :] = delta
            ratio_s[rows, :] = jnp.where(delta > 1e-30, scaled, 1.0)
            u_s[rows, :] = delta * act_s[rows, :]

    each(slabs, convolve)

    zero = jnp.zeros((8, LANES), F32)
    ones = jnp.ones((GROUP, LANES), BF)
    lane_sets = [slice(LANES * e, LANES * (e + 1)) for e in range(4)]

    def pack(top, bottom):
        return jnp.concatenate([top, bottom], axis=0).astype(BF)

    def turned_of(index):
        each_chunk = REACH // CHUNK
        return [projt_s[index * each_chunk + k] for k in range(each_chunk)]

    def scan_chunk(index, carry):
        state = [list(carry[0:4]), list(carry[4:8])]
        last = list(carry[8:])
        turned = turned_of(index)
        for g in range(groups):
            base = index * REACH + g * GROUP
            columns = turned[g * GROUP // CHUNK]
            rows = span(base, GROUP)
            steps = delta_s[rows, :]
            feeds = u_s[rows, :]
            pulls = dscan_s[rows, :]
            held, sums = [], []
            for t in range(GROUP):
                at = (g * GROUP + t) % CHUNK
                entry = [
                    jnp.broadcast_to(
                        columns[STATE + 8 * h : STATE + 8 * h + 8, at : at + 1], (8, LANES)
                    )
                    for h in range(2)
                ]
                place = span((base + t) * STATE, STATE)
                total = [None, None]
                for e, lanes in enumerate(lane_sets):
                    step = spread(steps[:, lanes], t)
                    feed = spread(feeds[:, lanes], t)
                    pull = spread(pulls[:, lanes], t)
                    for h in range(2):
                        decay = jnp.exp2(step * rate_ref[8 * h : 8 * h + 8, lanes])
                        state[h][e] = decay * state[h][e] + feed * entry[h]
                        part = pull * state[h][e]
                        total[h] = part if e == 0 else total[h] + part
                    states[place, lanes] = last[e]
                    last[e] = pack(state[0][e], state[1][e])
                held.append(jnp.concatenate(last, axis=1))
                sums.append(pack(*total))
            y_s[rows, :] = dot(read_s[rows, :], jnp.concatenate(held, axis=0))
            found = dot(ones, jnp.concatenate(sums, axis=0), NT)
            wide_s[rows, :] = (found * mask_s[...]).astype(BF)
        return tuple(state[0] + state[1] + last)

    lax.fori_loop(0, length // REACH, scan_chunk, (zero,) * 8 + (pack(zero, zero),) * 4)

    def finish(slab):
        row = slab * SLAB
        dread_s[span(row, SLAB), :] = dot(wide_s[span(row, SLAB), :], fold_s[1]).astype(BF)
        for a in pieces:
            rows = span(row + a, BLOCK)
            scanned = y_s[rows, :] + vec_ref[6:7, :] * act_s[rows, :]
            gated_s[rows, :] = (scanned * gsilu_s[rows, :]).astype(BF)
            dproj_s[rows, INNER:] = (scanned * gslope_s[rows, :]).astype(BF)

    each(slabs, finish)

    def store_half(kept_ref, given_ref, which, rows, value):
        @pl.when(which == core)
        def _():
            kept_ref[0, rows, :] = value

        @pl.when(which != core)
        def _():
            given_ref[0, rows, :] = value

    def mirror_mixed(slab):
        mixed_all = dot(gated_s[span(slab * SLAB, SLAB), :], w_out_s[...])
        for k in range(SLAB // CHUNK):
            high, low = split_low(mixed_all[k * CHUNK : (k + 1) * CHUNK])
            place = place_of(slab * (SLAB // CHUNK) + k)
            mixed = dot(flip_s[0], high) + dot(flip_s[0], low)
            store_half(gin_kept_ref, gin_given_ref, place // half, span(place % half, CHUNK), mixed)

    def natural_mixed(slab):
        rows = span(slab * SLAB, SLAB)
        mixed = dot(gated_s[rows, :], w_out_s[...])
        total = x_s[rows, :].astype(F32) + mixed

        @pl.when(slab == core)
        def _():
            out_kept_ref[0] = (total + gin_kept_ref[0]).astype(BF)

        @pl.when(slab != core)
        def _():
            out_given_ref[0] = (total + gin_given_ref[0]).astype(BF)

    @pl.when(natural == 0)
    def _():
        each(slabs, mirror_mixed)
        dmix_s[...] = dot(dmix_s[...], perm_ref[...], NT).astype(BF)

    @pl.when(natural == 1)
    def _():
        each(slabs, natural_mixed)

    gwout_ref[...] += dot(gated_s[...], dmix_s[...], TN)

    def back_chunk(step_index, carry_all):
        index = length // REACH - 1 - step_index
        carry = [list(carry_all[0:4]), list(carry_all[4:8])]
        rate_sum = carry_all[8]
        turned = turned_of(index)
        for g in reversed(range(groups)):
            base = index * REACH + g * GROUP
            columns = turned[g * GROUP // CHUNK]
            rows = span(base, GROUP)
            steps = delta_s[rows, :]
            feeds = dscan_s[rows, :]
            pulls = u_s[rows, :]
            held, prods, sums = [], [], []
            for t in reversed(range(GROUP)):
                at = (g * GROUP + t) % CHUNK
                read = [
                    jnp.broadcast_to(
                        columns[2 * STATE + 8 * h : 2 * STATE + 8 * h + 8, at : at + 1], (8, LANES)
                    )
                    for h in range(2)
                ]
                place = span((base + t) * STATE, STATE)
                held_row, prod_row = [], []
                total = [None, None]
                for e, lanes in enumerate(lane_sets):
                    step = spread(steps[:, lanes], t)
                    feed = spread(feeds[:, lanes], t)
                    pull = spread(pulls[:, lanes], t)
                    before = states[place, lanes]
                    lams, both = [], []
                    for h in range(2):
                        power = step * rate_ref[8 * h : 8 * h + 8, lanes]
                        lam = feed * read[h] + carry[h][e]
                        carry[h][e] = jnp.exp2(power) * lam
                        lams.append(lam)
                        part = pull * lam
                        total[h] = part if e == 0 else total[h] + part
                        both.append(power * carry[h][e])
                    held_row.append(pack(*lams))
                    prod_row.append(pack(*both) * before)
                held.insert(0, jnp.concatenate(held_row, axis=1))
                prods.insert(0, jnp.concatenate(prod_row, axis=1))
                sums.insert(0, pack(*total))
            y_s[rows, :] = dot(entry_s[rows, :], jnp.concatenate(held, axis=0))
            both = dot(sums_s[...], jnp.concatenate(prods, axis=0))
            gslope_s[rows, :] = both[:GROUP]
            rate_sum = rate_sum + both[GROUP:]
            found = dot(ones, jnp.concatenate(sums, axis=0), NT)
            wide_s[rows, :] = (found * mask_s[...]).astype(BF)
        return tuple(carry[0] + carry[1]) + (rate_sum,)

    done = lax.fori_loop(
        0, length // REACH, back_chunk, (zero,) * 8 + (jnp.zeros((STATE, INNER), F32),)
    )
    gsmall_ref[0:STATE, :] += done[8] * LN2

    def gradients(slab):
        row = slab * SLAB
        sum_pre = sum_skip = None
        for a in pieces:
            rows = span(row + a, BLOCK)
            dfeed = y_s[rows, :]
            dpre = ratio_s[rows, :] * (gslope_s[rows, :] * LN2 + dfeed * u_s[rows, :])
            gsilu_s[rows, :] = dpre
            dscan = dscan_s[rows, :]
            y_s[rows, :] = dscan * vec_ref[6:7, :] + dfeed * delta_s[rows, :]
            one, two = row_sum(dpre), row_sum(dscan * act_s[rows, :])
            sum_pre = one if sum_pre is None else sum_pre + one
            sum_skip = two if sum_skip is None else sum_skip + two
        gvec_ref[5] += sum_pre
        gvec_ref[6] += sum_skip
        dpre_all = gsilu_s[span(row, SLAB), :].astype(BF)
        dproj = (
            dot(dpre_all, wdt_s[...], NT)
            + dot(wide_s[span(row, SLAB), :], fold_s[0])
            + dread_s[span(row, SLAB), :].astype(F32)
        )
        extra = dot(dproj.astype(BF), wx_s[...], NT)
        low = proj_s[span(row, SLAB), :]
        gsmall_ref[STATE : 2 * STATE, :] += dot(low, dpre_all, TN)[:RANK]
        gsmall_ref[2 * STATE : 5 * STATE, :] += dot(
            dproj.astype(BF), act_s[span(row, SLAB), :].astype(BF), TN
        )[: 3 * STATE]
        for a in pieces:
            rows = span(row + a, BLOCK)
            gsilu_s[rows, :] = (y_s[rows, :] + extra[a : a + BLOCK]) * slope_s[rows, :]

    each(slabs, gradients)

    def unconvolve(slab):
        row = slab * SLAB
        totals = [None] * 5
        near_s[: SLAB + 8, :] = gsilu_s[span(row, SLAB + 8, 8), :]
        for a in pieces:
            rows = span(row + a, BLOCK)
            inner = inner_s[span(row + a + 16, BLOCK, 16), :].astype(F32)
            dinner = None
            for j in range(KERNEL):
                moved = near_s[a + 3 - j : a + 3 - j + BLOCK, :]
                term = vec_ref[j : j + 1, :] * moved
                dinner = term if dinner is None else dinner + term
                part = row_sum(moved * inner)
                totals[j] = part if totals[j] is None else totals[j] + part
            part = row_sum(near_s[a : a + BLOCK, :])
            totals[4] = part if totals[4] is None else totals[4] + part
            dproj_s[rows, :INNER] = dinner.astype(BF)
        for j in range(5):
            gvec_ref[j] += totals[j]

    each(slabs, unconvolve)

    def mirror_dnorm(slab):
        dnorm_all = dot(dproj_s[span(slab * SLAB, SLAB), :], w_in_s[...], NT)
        for k in range(SLAB // CHUNK):
            high, low = split_low(dnorm_all[k * CHUNK : (k + 1) * CHUNK])
            there = span(place_of(slab * (SLAB // CHUNK) + k), CHUNK)
            dnorm_s[there, :] = dot(flip_s[0], high) + dot(flip_s[0], low)

    def natural_dnorm(slab):
        rows = span(slab * SLAB, SLAB)
        total = dot(dproj_s[rows, :], w_in_s[...], NT) + dnorm_s[rows, :]
        xf, inv = norm_parts(rows)
        scaled = total * gain_ref[...]
        hat = xf * inv
        ggain_ref[...] += row_sum(total * hat)
        mean = jnp.mean(scaled * hat, axis=-1, keepdims=True)
        result = up_s[rows, :].astype(F32) + inv * (scaled - hat * mean)
        store_half(gin_kept_ref, gin_given_ref, slab, slice(None), result)

    @pl.when(natural == 0)
    def _():
        each(slabs, mirror_dnorm)
        copy_s[...] = dot(copy_s[...], perm_ref[...], NT).astype(BF)

    @pl.when(natural == 1)
    def _():
        each(slabs, natural_dnorm)

    gwin_ref[...] += dot(copy_s[...], dproj_s[...], TN)


def run_layer(
    core, x, x_got, up, up_got, perm, w_in, w_x, w_dt, w_out, conv_w, conv_b, dt_bias, a_log, d_skip, gain
):
    windows, half, _ = x_got.shape
    length = 2 * half
    vec = jnp.concatenate(
        [conv_w.T, conv_b[None], dt_bias[None], d_skip[None], jnp.zeros((1, INNER), F32)], axis=0
    )
    rate = (-LOG2E) * jnp.exp(a_log).T

    def whole(shape):
        return pl.BlockSpec(shape, lambda w, q, core: (0,) * len(shape))

    kept = pl.BlockSpec((1, half, D), lambda w, q, core: (windows * core[0] + w, 0, 0))
    got = pl.BlockSpec((1, half, D), lambda w, q, core: (w, 0, 0))
    fixed = (perm, w_in, w_out, w_x, w_dt, vec, rate, gain[None])
    grads = [
        jax.ShapeDtypeStruct((D, 2 * INNER), F32),
        jax.ShapeDtypeStruct((INNER, D), F32),
        jax.ShapeDtypeStruct((5 * STATE, INNER), F32),
        jax.ShapeDtypeStruct((7, 8, INNER), F32),
        jax.ShapeDtypeStruct((8, D), F32),
    ]
    inner_f32 = [pltpu.VMEM((length, INNER), F32)]
    outer_bf = [pltpu.VMEM((length, D), BF)]
    outer_f32 = [pltpu.VMEM((length, D), F32)]
    halo_f32 = [pltpu.VMEM((length + 8, INNER), F32)]
    scratch = (
        [pltpu.VMEM((length * STATE, INNER), BF)]
        + inner_f32 * 7
        + halo_f32
        + inner_f32
        + [pltpu.VMEM((length + 16, INNER), BF)]
        + [pltpu.VMEM((length, LANES), BF)] * 2
        + [
            pltpu.VMEM((length // CHUNK, 3 * STATE, CHUNK), F32),
            pltpu.VMEM((length, 2 * INNER), BF),
            pltpu.VMEM((length, INNER), BF),
        ]
        + outer_bf * 4
        + outer_f32
        + [pltpu.VMEM((length, WIDE), BF)] * 3
        + [
            pltpu.VMEM((D, 2 * INNER), BF),
            pltpu.VMEM((INNER, D), BF),
            pltpu.VMEM((2, CHUNK, CHUNK), BF),
            pltpu.VMEM((2, LANES, WIDE), BF),
            pltpu.VMEM((2, WIDE, LANES), BF),
            pltpu.VMEM((2 * GROUP, WIDE), BF),
            pltpu.VMEM((GROUP, WIDE), F32),
            pltpu.VMEM((SLAB + 16, INNER), F32),
            pltpu.VMEM((INNER, LANES), BF),
            pltpu.VMEM((LANES, INNER), BF),
        ]
    )
    return pl.pallas_call(
        layer_kernel,
        grid_spec=pltpu.PrefetchScalarGridSpec(
            num_scalar_prefetch=1,
            grid=(windows, 2),
            in_specs=[kept, got, kept, got] + [whole(item.shape) for item in fixed],
            out_specs=[got] * 4 + [whole(item.shape) for item in grads],
            scratch_shapes=scratch,
        ),
        out_shape=[
            jax.ShapeDtypeStruct((windows, half, D), kind) for kind in (BF, BF, F32, F32)
        ]
        + grads,
        compiler_params=pltpu.CompilerParams(vmem_limit_bytes=64 * 2**20 - 65536),
    )(core.reshape(1).astype(jnp.int32), x, x_got, up, up_got, *fixed)


def layer_grads(results):
    gwin, gwout, gsmall, gvec, ggain = results
    vec = jnp.sum(gvec, axis=1)
    return [
        gwin,
        gsmall[2 * STATE :].T,
        gsmall[STATE : 2 * STATE],
        gwout,
        vec[:KERNEL].T,
        vec[4],
        vec[5],
        gsmall[:STATE].T,
        vec[6],
        jnp.sum(ggain, axis=0),
    ]


def param_shapes():
    return [
        (D, 2 * INNER),
        (INNER, RANK + 2 * STATE),
        (RANK, INNER),
        (INNER, D),
        (INNER, KERNEL),
        (INNER,),
        (INNER,),
        (INNER, STATE),
        (INNER,),
        (D,),
    ]


def bounds():
    edges = [0]
    for shape in param_shapes():
        edges.append(edges[-1] + math.prod(shape))
    return edges


def slot_index(owners):
    count = owners.shape[0]
    order = jnp.arange(count, dtype=jnp.int32)
    same = (owners[None, :] == owners[:, None]) & (order[None, :] < order[:, None])
    return jnp.sum(same.astype(jnp.int32), axis=1)


def swap(value, axis, bit):
    size = lax.axis_size(axis)
    return lax.ppermute(value, axis, [(i, i ^ bit) for i in range(size)])


def up_to(value, multiple):
    return -(-value // multiple) * multiple


def pad_rows(value, rows, axis):
    widths = [(0, 0)] * value.ndim
    widths[axis] = (0, rows - value.shape[axis])
    return jnp.pad(value, widths)


def gather_params(weights, owners, rank, matches):
    size = lax.axis_size("dp")
    me = lax.axis_index("dp")
    core = lax.axis_index("seq")
    blocks, block_len = owners.shape[0], weights.shape[1]
    rows = block_len // LANES
    padded = up_to(rows, 16)
    near = min(4, size)
    tiles = weights.reshape(SLOTS, rows, LANES)
    rounded = lax.reduce_precision(tiles, 8, 7)
    pair = SLOTS // 2
    mine = lax.dynamic_slice_in_dim(rounded, core * pair, pair, 0).astype(BF)
    many = pad_rows(mine, padded, 1).reshape(pair * padded, LANES)
    first = MATRIX_END // block_len
    last = (PARAMS - 1) // block_len + 1
    here = matches[:, first:last].T[:, :, None, None]
    fine = jnp.sum(jnp.where(here, (tiles - rounded)[None], 0.0), axis=1).astype(BF)
    fine_rows = (last - first) * rows
    fine_half = up_to(fine_rows, 32) // 2
    fine = pad_rows(fine.reshape(fine_rows, LANES), 2 * fine_half, 0)
    fine = lax.dynamic_slice_in_dim(fine, core * fine_half, fine_half, 0)
    away = owners ^ me
    spot = jnp.zeros_like(owners)
    bit, step = size // 2, 0
    while bit >= near:
        got = swap(jnp.concatenate([many, fine], axis=0), "dp", bit)
        count = many.shape[0]
        many = jnp.concatenate([many, got[:count]], axis=0)
        fine = fine + got[count:]
        spot = spot + jnp.where((away & bit) != 0, 1 << step, 0)
        bit, step = bit // 2, step + 1
    count = many.shape[0]
    sent = jnp.concatenate([many, fine], axis=0)
    others = [swap(sent, "dp", k) for k in range(1, near)]
    many = jnp.stack([many] + [item[:count] for item in others])
    for item in others:
        fine = fine + item[count:]
    spot = (spot + (away & (near - 1)) * (size // near)) * pair + rank % pair
    chosen = many.reshape(size * pair, padded, LANES)[spot]
    sent = jnp.concatenate([chosen.reshape(blocks * padded, LANES), fine], axis=0)
    got = swap(sent, "seq", 1)
    theirs = got[: blocks * padded].reshape(blocks, padded, LANES)
    local = (rank // pair == core)[:, None, None]
    theta = jnp.where(local, chosen, theirs)[:, :rows].reshape(blocks * rows, LANES)
    fine_got = got[blocks * padded :]
    fine = jnp.concatenate(
        [jnp.where(core == 0, fine, fine_got), jnp.where(core == 0, fine_got, fine)], axis=0
    )
    begin = (MATRIX_END - first * block_len) // LANES
    fine = fine[begin : begin + (PARAMS - MATRIX_END) // LANES]
    return lax.optimization_barrier((theta, fine))


def scatter_sum(value, size):
    me = lax.axis_index("dp")
    stride = 1
    total = value
    while stride < size:
        radix = min(4, size // stride)
        total = total.reshape((size // (stride * radix), radix) + value.shape[1:])
        digit = (me // stride) % radix
        low = total.astype(BF)
        kept = lax.dynamic_index_in_dim(total, digit, 1, keepdims=False).astype(F32)
        for k in range(1, radix):
            given = lax.dynamic_index_in_dim(low, digit ^ k, 1, keepdims=False)
            kept = kept + swap(given, "dp", k * stride).astype(F32)
        total = kept
        stride *= radix
    return total[0]


def other_half(value, core):
    count = value.shape[0] // 2
    return swap(lax.dynamic_slice_in_dim(value, (1 - core) * count, count, 0), "seq", 1)


def by_position(kept, given, core):
    got = swap(given, "seq", 1)
    return jnp.concatenate(
        [jnp.where(core == 0, kept, got), jnp.where(core == 0, got, kept)], axis=0
    )


def on_device(
    inputs, cotangent, loss_mask, complement_map, owners, weights, first_moment, second_moment
):
    size = lax.axis_size("dp")
    me = lax.axis_index("dp")
    core = lax.axis_index("seq")
    blocks, block_len = owners.shape[0], weights.shape[1]
    rows = block_len // LANES
    pair = SLOTS // 2
    rank = slot_index(owners)
    order = jnp.arange(blocks, dtype=jnp.int32)
    matches = (owners[None, :] == me) & (
        rank[None, :] == jnp.arange(SLOTS, dtype=jnp.int32)[:, None]
    )
    occupied = jnp.any(matches, axis=1)
    block_of = jnp.sum(jnp.where(matches, order[None, :], 0), axis=1)
    theta, fine = gather_params(weights, owners, rank, matches)
    upstream = cotangent * loss_mask.astype(BF)[..., None]
    x_got = other_half(inputs, core)
    up_got = other_half(upstream, core)

    edges = [edge // LANES for edge in bounds()]
    shapes = param_shapes()
    tail = edges[4]

    def high_of(index):
        return theta[edges[index] : edges[index + 1]].reshape(shapes[index])

    def full_of(index):
        part = theta[edges[index] : edges[index + 1]].astype(F32)
        part = part + fine[edges[index] - tail : edges[index + 1] - tail].astype(F32)
        return part.reshape(shapes[index])

    perm = (complement_map[:, None] == jnp.arange(D, dtype=jnp.int32)[None, :]).astype(BF)
    results = run_layer(
        core,
        inputs,
        x_got,
        upstream,
        up_got,
        perm,
        *[high_of(index) for index in range(4)],
        *[full_of(index) for index in range(4, 10)],
    )
    pieces = layer_grads(results[4:])
    padded = up_to(rows, 16)
    spare = jnp.zeros(((blocks + 1) * rows - PARAMS // LANES, LANES), BF)
    tiles = [item.astype(BF).reshape(-1, LANES) for item in pieces] + [spare]
    grad_blocks = jnp.concatenate(tiles, axis=0).reshape(blocks + 1, rows, LANES)
    grad_blocks = pad_rows(grad_blocks, padded, 1)
    source = jnp.full((size * SLOTS,), blocks, jnp.int32).at[owners * SLOTS + rank].set(order)
    source = source.reshape(size, 2, pair)

    def for_core(which):
        index = lax.dynamic_index_in_dim(source, which, 1, keepdims=False)
        return grad_blocks[index.reshape(-1)].reshape(size * pair * padded, LANES)

    got = swap(for_core(1 - core), "seq", 1)
    chip = (for_core(core).astype(F32) + got.astype(F32)).astype(BF)
    chip = chip.reshape(size, pair * padded, LANES)
    summed = scatter_sum(chip, size).reshape(pair, -1, LANES)[:, :rows]
    other = swap(summed, "seq", 1)
    owned = jnp.concatenate(
        [jnp.where(core == 0, summed, other), jnp.where(core == 0, other, summed)], axis=0
    ).reshape(SLOTS, block_len)
    output = by_position(results[0], results[1], core)
    grad_input = by_position(results[2], results[3], core)
    new_first = BETA_ONE * first_moment + (1.0 - BETA_ONE) * owned
    new_second = BETA_TWO * second_moment + (1.0 - BETA_TWO) * owned * owned
    position = block_of[:, None] * block_len + jnp.arange(block_len, dtype=jnp.int32)[None, :]
    is_matrix = position < MATRIX_END
    rate = jnp.where(is_matrix, RATE_MATRIX, RATE_VECTOR)
    decay = jnp.where(is_matrix, WEIGHT_DECAY, 0.0)
    corrected = (
        new_first
        / (1.0 - BETA_ONE**STEP_COUNT)
        / (jnp.sqrt(new_second / (1.0 - BETA_TWO**STEP_COUNT)) + ADAM_EPSILON)
    )
    new_theta = weights - rate * (corrected + decay * weights)
    keep = occupied[:, None]
    return (
        output,
        grad_input,
        jnp.where(keep, new_theta, 0.0),
        jnp.where(keep, new_first, 0.0),
        jnp.where(keep, new_second, 0.0),
    )


def solution(mesh):
    in_specs = (
        P("dp", "seq", None),
        P("dp", "seq", None),
        P("dp", "seq"),
        P(),
        P(),
        P("dp", None),
        P("dp", None),
        P("dp", None),
    )
    out_specs = (
        P("dp", "seq", None),
        P("dp", "seq", None),
        P("dp", None),
        P("dp", None),
        P("dp", None),
    )
    return jax.shard_map(
        on_device, mesh=mesh, in_specs=in_specs, out_specs=out_specs, check_vma=False
    )
```

```python
import functools
import math

import jax
import jax.numpy as jnp
from jax import lax
from jax.experimental import pallas as pl
from jax.experimental.pallas import tpu as pltpu
from jax.sharding import PartitionSpec as P

D = 256
INNER = 512
STATE = 16
RANK = 16
KERNEL = 4
SLOTS = 4
STEP_COUNT = 10
PARAMS = 438016
MATRIX_END = 425984
BETA_ONE = 0.9
BETA_TWO = 0.95
ADAM_EPSILON = 1e-08
RATE_MATRIX = 0.1
RATE_VECTOR = 0.5
WEIGHT_DECAY = 0.1
NORM_EPSILON = 1e-05
LOG2E = 1.4426950408889634
LN2 = 0.6931471805599453
CHUNK = 128
GROUP = 16
SLAB = 512
REACH = 256
BLOCK = 32
LANES = 128
WIDE = GROUP * STATE
BF = jnp.bfloat16
F32 = jnp.float32
NT = (((1,), (1,)), ((), ()))
TN = (((0,), (0,)), ((), ()))


def split_low(value):
    high = value.astype(BF)
    return high, (value - high.astype(F32)).astype(BF)


def dot(a, b, dims=None):
    if dims is None:
        return jnp.dot(a, b, preferred_element_type=F32)
    return lax.dot_general(a, b, dims, preferred_element_type=F32)


def row_sum(value):
    return jnp.sum(value.reshape(value.shape[0] // 8, 8, value.shape[1]), axis=0)


def span(start, count, step=None):
    return pl.ds(pl.multiple_of(start, step or count), count)


def iota(shape, axis):
    return lax.broadcasted_iota(jnp.int32, shape, axis)


def spread(value, index):
    return jnp.broadcast_to(value[index : index + 1, :], (8, LANES))


def each(count, body):
    lax.fori_loop(0, count, lambda i, c: (body(i), c)[1], 0)


def layer_kernel(
    core_ref,
    x_kept_ref,
    x_got_ref,
    up_kept_ref,
    up_got_ref,
    perm_ref,
    w_in_ref,
    w_out_ref,
    wx_ref,
    wdt_ref,
    vec_ref,
    rate_ref,
    gain_ref,
    out_kept_ref,
    out_given_ref,
    gin_kept_ref,
    gin_given_ref,
    gwin_out,
    gwout_out,
    gsmall_out,
    gvec_out,
    ggain_out,
    states,
    act_s,
    slope_s,
    delta_s,
    ratio_s,
    dscan_s,
    u_s,
    y_s,
    gsilu_s,
    gslope_s,
    inner_s,
    proj_s,
    dread_s,
    projt_s,
    dproj_s,
    gated_s,
    copy_s,
    dmix_s,
    x_s,
    up_s,
    dnorm_s,
    wide_s,
    read_s,
    entry_s,
    w_in_s,
    w_out_s,
    flip_s,
    tile_s,
    fold_s,
    sums_s,
    mask_s,
    near_s,
    wx_s,
    wdt_s,
    gwin_ref,
    gwout_ref,
    gsmall_ref,
    gvec_ref,
    ggain_ref,
):
    window = pl.program_id(0)
    natural = pl.program_id(1)
    core = core_ref[0]
    length = x_s.shape[0]
    half = length // 2
    chunks = length // CHUNK
    slabs = length // SLAB
    groups = REACH // GROUP
    pieces = range(0, SLAB, BLOCK)

    @pl.when((window == 0) & (natural == 0))
    def _():
        gwin_ref[...] = jnp.zeros_like(gwin_ref)
        gwout_ref[...] = jnp.zeros_like(gwout_ref)
        gsmall_ref[...] = jnp.zeros_like(gsmall_ref)
        gvec_ref[...] = jnp.zeros_like(gvec_ref)
        ggain_ref[...] = jnp.zeros_like(ggain_ref)
        wx_s[...] = jnp.zeros_like(wx_s)
        wx_s[:, : 3 * STATE] = wx_ref[...]
        wdt_s[...] = jnp.zeros_like(wdt_s)
        wdt_s[:RANK, :] = wdt_ref[...]
        inner_s[0:16, :] = jnp.zeros((16, INNER), BF)
        gsilu_s[length : length + 8, :] = jnp.zeros((8, INNER), F32)
        rows, lanes = iota((CHUNK, CHUNK), 0), iota((CHUNK, CHUNK), 1)
        flip_s[1] = jnp.where(rows == lanes, 1.0, 0.0).astype(BF)
        flip_s[0] = jnp.where(rows + lanes == CHUNK - 1, 1.0, 0.0).astype(BF)
        rows, lanes = iota((LANES, WIDE), 0), iota((LANES, WIDE), 1)
        for k in range(2):
            tile_s[k] = jnp.where(rows == STATE * (k + 1) + lanes % STATE, 1.0, 0.0).astype(BF)
        rows, lanes = iota((WIDE, LANES), 0), iota((WIDE, LANES), 1)
        for k in range(2):
            fold_s[k] = jnp.where(lanes == STATE * (k + 1) + rows % STATE, 1.0, 0.0).astype(BF)
        rows, lanes = iota((GROUP, WIDE), 0), iota((GROUP, WIDE), 1)
        mask_s[0] = jnp.where(GROUP - 1 - rows == lanes // STATE, 1.0, 0.0)
        mask_s[1] = jnp.where(rows == lanes // STATE, 1.0, 0.0)
        sums_s[:GROUP, :] = mask_s[0].astype(BF)
        sums_s[GROUP:, :] = jnp.where(rows == lanes % STATE, 1.0, 0.0).astype(BF)

    @pl.when(natural == 0)
    def _():
        kept, got = span(core * half, half), span((1 - core) * half, half)
        x_s[kept, :] = x_kept_ref[0]
        x_s[got, :] = x_got_ref[0]
        up_s[kept, :] = up_kept_ref[0]
        up_s[got, :] = up_got_ref[0]
        w_in_s[...] = dot(perm_ref[...], w_in_ref[...], TN).astype(BF)
        w_out_s[...] = dot(w_out_ref[...], perm_ref[...]).astype(BF)

    @pl.when(natural == 1)
    def _():
        w_in_s[...] = w_in_ref[...]
        w_out_s[...] = w_out_ref[...]

    def place_of(chunk):
        return jnp.where(natural == 1, chunk, chunks - 1 - chunk) * CHUNK

    def norm_parts(rows):
        xf = x_s[rows, :].astype(F32)
        inv = lax.rsqrt(jnp.mean(xf * xf, axis=-1, keepdims=True) + NORM_EPSILON)
        return xf, inv

    def load_copies(slab):
        rows = span(slab * SLAB, SLAB)
        xf, inv = norm_parts(rows)
        normed = (xf * inv * gain_ref[...]).astype(BF)
        upstream = up_s[rows, :]
        for k in range(SLAB // CHUNK):
            part = slice(k * CHUNK, (k + 1) * CHUNK)
            there = span(place_of(slab * (SLAB // CHUNK) + k), CHUNK)
            copy_s[there, :] = dot(flip_s[natural], normed[part]).astype(BF)
            dmix_s[there, :] = dot(flip_s[natural], upstream[part]).astype(BF)

    each(slabs, load_copies)

    def project(slab):
        row = slab * SLAB
        copy = copy_s[span(row, SLAB), :]
        inner_s[span(row + 16, SLAB, 16), :] = dot(copy, w_in_s[:, :INNER]).astype(BF)
        gate_all = dot(copy, w_in_s[:, INNER:]).astype(BF)
        dgated_all = dot(dmix_s[span(row, SLAB), :], w_out_s[...], NT).astype(BF)
        for a in pieces:
            rows = span(row + a, BLOCK)
            gate = gate_all[a : a + BLOCK].astype(F32)
            dgated = dgated_all[a : a + BLOCK].astype(F32)
            sig = 0.5 + 0.5 * jnp.tanh(0.5 * gate)
            silu = gate * sig
            gsilu_s[rows, :] = silu
            dscan_s[rows, :] = dgated * silu
            gslope_s[rows, :] = dgated * (sig + silu * (1.0 - sig))

    each(slabs, project)

    def convolve(slab):
        row = slab * SLAB
        near_s[...] = inner_s[span(row, SLAB + 16, 16), :].astype(F32)
        for a in pieces:
            rows = span(row + a, BLOCK)
            conv = vec_ref[4:5, :]
            for j in range(KERNEL):
                conv = conv + vec_ref[j : j + 1, :] * near_s[a + 13 + j : a + 13 + j + BLOCK, :]
            sig = 0.5 + 0.5 * jnp.tanh(0.5 * conv)
            act = conv * sig
            act_s[rows, :] = act
            slope_s[rows, :] = sig + act * (1.0 - sig)
        act_high, act_low = split_low(act_s[span(row, SLAB), :])
        proj = dot(act_high, wx_s[...]) + dot(act_low, wx_s[...])
        proj_s[span(row, SLAB), :] = proj.astype(BF)
        for k in range(SLAB // CHUNK):
            turned = jnp.transpose(proj[k * CHUNK : (k + 1) * CHUNK])
            projt_s[slab * (SLAB // CHUNK) + k] = turned[: 3 * STATE]
        proj_high, proj_low = split_low(proj)
        for kind, target in ((0, entry_s), (1, read_s)):
            wide = dot(proj_high, tile_s[kind])
            for g in range(SLAB // GROUP):
                part = wide[g * GROUP : (g + 1) * GROUP] * mask_s[kind]
                target[span(row + g * GROUP, GROUP), :] = part.astype(BF)
        pre_all = dot(proj_high, wdt_s[...]) + dot(proj_low, wdt_s[...])
        for a in pieces:
            rows = span(row + a, BLOCK)
            pre = pre_all[a : a + BLOCK] + vec_ref[5:6, :]
            small = jnp.exp(-jnp.abs(pre))
            whole = 1.0 + small
            share = 1.0 / whole
            log_part = jnp.log(whole) + (small - (whole - 1.0)) * share
            delta = jnp.maximum(pre, 0.0) + log_part
            scaled = jnp.where(pre >= 0.0, share, small * share) / delta
            delta_s[rows, :] = delta
            ratio_s[rows, :] = jnp.where(delta > 1e-30, scaled, 1.0)
            u_s[rows, :] = delta * act_s[rows, :]

    each(slabs, convolve)

    zero = jnp.zeros((8, LANES), F32)
    ones = jnp.ones((GROUP, LANES), BF)
    lane_sets = [slice(LANES * e, LANES * (e + 1)) for e in range(4)]

    def pack(top, bottom):
        return jnp.concatenate([top, bottom], axis=0).astype(BF)

    def turned_of(index):
        each_chunk = REACH // CHUNK
        return [projt_s[index * each_chunk + k] for k in range(each_chunk)]

    def scan_chunk(index, carry):
        state = [list(carry[0:4]), list(carry[4:8])]
        last = list(carry[8:])
        turned = turned_of(index)
        for g in range(groups):
            base = index * REACH + g * GROUP
            columns = turned[g * GROUP // CHUNK]
            rows = span(base, GROUP)
            steps = delta_s[rows, :]
            feeds = u_s[rows, :]
            pulls = dscan_s[rows, :]
            held, sums = [], []
            for t in range(GROUP):
                at = (g * GROUP + t) % CHUNK
                entry = [
                    jnp.broadcast_to(
                        columns[STATE + 8 * h : STATE + 8 * h + 8, at : at + 1], (8, LANES)
                    )
                    for h in range(2)
                ]
                place = span((base + t) * STATE, STATE)
                total = [None, None]
                for e, lanes in enumerate(lane_sets):
                    step = spread(steps[:, lanes], t)
                    feed = spread(feeds[:, lanes], t)
                    pull = spread(pulls[:, lanes], t)
                    for h in range(2):
                        decay = jnp.exp2(step * rate_ref[8 * h : 8 * h + 8, lanes])
                        state[h][e] = decay * state[h][e] + feed * entry[h]
                        part = pull * state[h][e]
                        total[h] = part if e == 0 else total[h] + part
                    states[place, lanes] = last[e]
                    last[e] = pack(state[0][e], state[1][e])
                held.append(jnp.concatenate(last, axis=1))
                sums.append(pack(*total))
            y_s[rows, :] = dot(read_s[rows, :], jnp.concatenate(held, axis=0))
            found = dot(ones, jnp.concatenate(sums, axis=0), NT)
            wide_s[rows, :] = (found * mask_s[1]).astype(BF)
        return tuple(state[0] + state[1] + last)

    lax.fori_loop(0, length // REACH, scan_chunk, (zero,) * 8 + (pack(zero, zero),) * 4)

    def finish(slab):
        row = slab * SLAB
        dread_s[span(row, SLAB), :] = dot(wide_s[span(row, SLAB), :], fold_s[1]).astype(BF)
        for a in pieces:
            rows = span(row + a, BLOCK)
            scanned = y_s[rows, :] + vec_ref[6:7, :] * act_s[rows, :]
            gated_s[rows, :] = (scanned * gsilu_s[rows, :]).astype(BF)
            dproj_s[rows, INNER:] = (scanned * gslope_s[rows, :]).astype(BF)

    each(slabs, finish)

    def store_half(kept_ref, given_ref, which, rows, value):
        @pl.when(which == core)
        def _():
            kept_ref[0, rows, :] = value

        @pl.when(which != core)
        def _():
            given_ref[0, rows, :] = value

    def mirror_mixed(slab):
        mixed_all = dot(gated_s[span(slab * SLAB, SLAB), :], w_out_s[...])
        for k in range(SLAB // CHUNK):
            high, low = split_low(mixed_all[k * CHUNK : (k + 1) * CHUNK])
            place = place_of(slab * (SLAB // CHUNK) + k)
            mixed = dot(flip_s[0], high) + dot(flip_s[0], low)
            store_half(gin_kept_ref, gin_given_ref, place // half, span(place % half, CHUNK), mixed)

    def natural_mixed(slab):
        rows = span(slab * SLAB, SLAB)
        mixed = dot(gated_s[rows, :], w_out_s[...])
        total = x_s[rows, :].astype(F32) + mixed

        @pl.when(slab == core)
        def _():
            out_kept_ref[0] = (total + gin_kept_ref[0]).astype(BF)

        @pl.when(slab != core)
        def _():
            out_given_ref[0] = (total + gin_given_ref[0]).astype(BF)

    @pl.when(natural == 0)
    def _():
        each(slabs, mirror_mixed)
        dmix_s[...] = dot(dmix_s[...], perm_ref[...], NT).astype(BF)

    @pl.when(natural == 1)
    def _():
        each(slabs, natural_mixed)

    gwout_ref[...] += dot(gated_s[...], dmix_s[...], TN)

    def back_chunk(step_index, carry_all):
        index = length // REACH - 1 - step_index
        carry = [list(carry_all[0:4]), list(carry_all[4:8])]
        rate_sum = carry_all[8]
        turned = turned_of(index)
        for g in reversed(range(groups)):
            base = index * REACH + g * GROUP
            columns = turned[g * GROUP // CHUNK]
            rows = span(base, GROUP)
            steps = delta_s[rows, :]
            feeds = dscan_s[rows, :]
            pulls = u_s[rows, :]
            held, prods, sums = [], [], []
            for t in reversed(range(GROUP)):
                at = (g * GROUP + t) % CHUNK
                read = [
                    jnp.broadcast_to(
                        columns[2 * STATE + 8 * h : 2 * STATE + 8 * h + 8, at : at + 1], (8, LANES)
                    )
                    for h in range(2)
                ]
                place = span((base + t) * STATE, STATE)
                held_row, prod_row = [], []
                total = [None, None]
                for e, lanes in enumerate(lane_sets):
                    step = spread(steps[:, lanes], t)
                    feed = spread(feeds[:, lanes], t)
                    pull = spread(pulls[:, lanes], t)
                    before = states[place, lanes]
                    lams, both = [], []
                    for h in range(2):
                        power = step * rate_ref[8 * h : 8 * h + 8, lanes]
                        lam = feed * read[h] + carry[h][e]
                        carry[h][e] = jnp.exp2(power) * lam
                        lams.append(lam)
                        part = pull * lam
                        total[h] = part if e == 0 else total[h] + part
                        both.append(power * carry[h][e])
                    held_row.append(pack(*lams))
                    prod_row.append(pack(*both) * before)
                held.append(jnp.concatenate(held_row, axis=1))
                prods.append(jnp.concatenate(prod_row, axis=1))
                sums.append(pack(*total))
            y_s[rows, :] = dot(entry_s[rows, :], jnp.concatenate(held, axis=0))
            both = dot(sums_s[...], jnp.concatenate(prods, axis=0))
            gslope_s[rows, :] = both[:GROUP]
            rate_sum = rate_sum + both[GROUP:]
            found = dot(ones, jnp.concatenate(sums, axis=0), NT)
            wide_s[rows, :] = (found * mask_s[0]).astype(BF)
        return tuple(carry[0] + carry[1]) + (rate_sum,)

    done = lax.fori_loop(
        0, length // REACH, back_chunk, (zero,) * 8 + (jnp.zeros((STATE, INNER), F32),)
    )
    gsmall_ref[0:STATE, :] += done[8] * LN2

    def gradients(slab):
        row = slab * SLAB
        sum_pre = sum_skip = None
        for a in pieces:
            rows = span(row + a, BLOCK)
            dfeed = y_s[rows, :]
            dpre = ratio_s[rows, :] * (gslope_s[rows, :] * LN2 + dfeed * u_s[rows, :])
            gsilu_s[rows, :] = dpre
            dscan = dscan_s[rows, :]
            y_s[rows, :] = dscan * vec_ref[6:7, :] + dfeed * delta_s[rows, :]
            one, two = row_sum(dpre), row_sum(dscan * act_s[rows, :])
            sum_pre = one if sum_pre is None else sum_pre + one
            sum_skip = two if sum_skip is None else sum_skip + two
        gvec_ref[5] += sum_pre
        gvec_ref[6] += sum_skip
        dpre_all = gsilu_s[span(row, SLAB), :].astype(BF)
        dproj = (
            dot(dpre_all, wdt_s[...], NT)
            + dot(wide_s[span(row, SLAB), :], fold_s[0])
            + dread_s[span(row, SLAB), :].astype(F32)
        )
        extra = dot(dproj.astype(BF), wx_s[...], NT)
        low = proj_s[span(row, SLAB), :]
        gsmall_ref[STATE : 2 * STATE, :] += dot(low, dpre_all, TN)[:RANK]
        gsmall_ref[2 * STATE : 5 * STATE, :] += dot(
            dproj.astype(BF), act_s[span(row, SLAB), :].astype(BF), TN
        )[: 3 * STATE]
        for a in pieces:
            rows = span(row + a, BLOCK)
            gsilu_s[rows, :] = (y_s[rows, :] + extra[a : a + BLOCK]) * slope_s[rows, :]

    each(slabs, gradients)

    def unconvolve(slab):
        row = slab * SLAB
        totals = [None] * 5
        near_s[: SLAB + 8, :] = gsilu_s[span(row, SLAB + 8, 8), :]
        for a in pieces:
            rows = span(row + a, BLOCK)
            inner = inner_s[span(row + a + 16, BLOCK, 16), :].astype(F32)
            dinner = None
            for j in range(KERNEL):
                moved = near_s[a + 3 - j : a + 3 - j + BLOCK, :]
                term = vec_ref[j : j + 1, :] * moved
                dinner = term if dinner is None else dinner + term
                part = row_sum(moved * inner)
                totals[j] = part if totals[j] is None else totals[j] + part
            part = row_sum(near_s[a : a + BLOCK, :])
            totals[4] = part if totals[4] is None else totals[4] + part
            dproj_s[rows, :INNER] = dinner.astype(BF)
        for j in range(5):
            gvec_ref[j] += totals[j]

    each(slabs, unconvolve)

    def mirror_dnorm(slab):
        dnorm_all = dot(dproj_s[span(slab * SLAB, SLAB), :], w_in_s[...], NT)
        for k in range(SLAB // CHUNK):
            high, low = split_low(dnorm_all[k * CHUNK : (k + 1) * CHUNK])
            there = span(place_of(slab * (SLAB // CHUNK) + k), CHUNK)
            dnorm_s[there, :] = dot(flip_s[0], high) + dot(flip_s[0], low)

    def natural_dnorm(slab):
        rows = span(slab * SLAB, SLAB)
        total = dot(dproj_s[rows, :], w_in_s[...], NT) + dnorm_s[rows, :]
        xf, inv = norm_parts(rows)
        scaled = total * gain_ref[...]
        hat = xf * inv
        ggain_ref[...] += row_sum(total * hat)
        mean = jnp.mean(scaled * hat, axis=-1, keepdims=True)
        result = up_s[rows, :].astype(F32) + inv * (scaled - hat * mean)
        store_half(gin_kept_ref, gin_given_ref, slab, slice(None), result)

    @pl.when(natural == 0)
    def _():
        each(slabs, mirror_dnorm)
        copy_s[...] = dot(copy_s[...], perm_ref[...], NT).astype(BF)

    @pl.when(natural == 1)
    def _():
        each(slabs, natural_dnorm)

    gwin_ref[...] += dot(copy_s[...], dproj_s[...], TN)

    @pl.when((window == pl.num_programs(0) - 1) & (natural == 1))
    def _():
        gwin_out[...] = gwin_ref[...].astype(BF)
        gwout_out[...] = gwout_ref[...].astype(BF)
        gsmall_out[...] = gsmall_ref[...].astype(BF)
        vectors = [jnp.sum(gvec_ref[j], axis=0, keepdims=True) for j in range(7)]
        vectors.append(jnp.zeros((9, INNER), F32))
        gvec_out[...] = jnp.concatenate(vectors, axis=0).astype(BF)
        gain = jnp.sum(ggain_ref[...], axis=0, keepdims=True)
        ggain_out[...] = jnp.broadcast_to(gain, (16, D)).astype(BF)


def run_layer(
    core, x, x_got, up, up_got, perm, w_in, w_x, w_dt, w_out, conv_w, conv_b, dt_bias, a_log, d_skip, gain
):
    windows, half, _ = x_got.shape
    length = 2 * half
    vec = jnp.concatenate(
        [conv_w.T, conv_b[None], dt_bias[None], d_skip[None], jnp.zeros((1, INNER), F32)], axis=0
    )
    rate = (-LOG2E) * jnp.exp(a_log).T

    def whole(shape):
        return pl.BlockSpec(shape, lambda w, q, core: (0,) * len(shape))

    kept = pl.BlockSpec((1, half, D), lambda w, q, core: (windows * core[0] + w, 0, 0))
    got = pl.BlockSpec((1, half, D), lambda w, q, core: (w, 0, 0))
    fixed = (perm, w_in, w_out, w_x, w_dt, vec, rate, gain[None])
    grads = [
        jax.ShapeDtypeStruct((D, 2 * INNER), BF),
        jax.ShapeDtypeStruct((INNER, D), BF),
        jax.ShapeDtypeStruct((5 * STATE, INNER), BF),
        jax.ShapeDtypeStruct((16, INNER), BF),
        jax.ShapeDtypeStruct((16, D), BF),
    ]
    inner_f32 = [pltpu.VMEM((length, INNER), F32)]
    outer_bf = [pltpu.VMEM((length, D), BF)]
    outer_f32 = [pltpu.VMEM((length, D), F32)]
    halo_f32 = [pltpu.VMEM((length + 8, INNER), F32)]
    scratch = (
        [pltpu.VMEM((length * STATE, INNER), BF)]
        + inner_f32 * 7
        + halo_f32
        + inner_f32
        + [pltpu.VMEM((length + 16, INNER), BF)]
        + [pltpu.VMEM((length, LANES), BF)] * 2
        + [
            pltpu.VMEM((length // CHUNK, 3 * STATE, CHUNK), F32),
            pltpu.VMEM((length, 2 * INNER), BF),
            pltpu.VMEM((length, INNER), BF),
        ]
        + outer_bf * 4
        + outer_f32
        + [pltpu.VMEM((length, WIDE), BF)] * 3
        + [
            pltpu.VMEM((D, 2 * INNER), BF),
            pltpu.VMEM((INNER, D), BF),
            pltpu.VMEM((2, CHUNK, CHUNK), BF),
            pltpu.VMEM((2, LANES, WIDE), BF),
            pltpu.VMEM((2, WIDE, LANES), BF),
            pltpu.VMEM((2 * GROUP, WIDE), BF),
            pltpu.VMEM((2, GROUP, WIDE), F32),
            pltpu.VMEM((SLAB + 16, INNER), F32),
            pltpu.VMEM((INNER, LANES), BF),
            pltpu.VMEM((LANES, INNER), BF),
            pltpu.VMEM((D, 2 * INNER), F32),
            pltpu.VMEM((INNER, D), F32),
            pltpu.VMEM((5 * STATE, INNER), F32),
            pltpu.VMEM((7, 8, INNER), F32),
            pltpu.VMEM((8, D), F32),
        ]
    )
    return pl.pallas_call(
        layer_kernel,
        grid_spec=pltpu.PrefetchScalarGridSpec(
            num_scalar_prefetch=1,
            grid=(windows, 2),
            in_specs=[kept, got, kept, got] + [whole(item.shape) for item in fixed],
            out_specs=[got] * 4 + [whole(item.shape) for item in grads],
            scratch_shapes=scratch,
        ),
        out_shape=[
            jax.ShapeDtypeStruct((windows, half, D), kind) for kind in (BF, BF, F32, F32)
        ]
        + grads,
        compiler_params=pltpu.CompilerParams(vmem_limit_bytes=64 * 2**20 - 65536),
    )(core.reshape(1).astype(jnp.int32), x, x_got, up, up_got, *fixed)


def layer_grads(results):
    gwin, gwout, gsmall, gvec, ggain = results
    return [
        gwin,
        gsmall[2 * STATE :].T,
        gsmall[STATE : 2 * STATE],
        gwout,
        gvec[:KERNEL].T,
        gvec[4],
        gvec[5],
        gsmall[:STATE].T,
        gvec[6],
        ggain[0],
    ]


def param_shapes():
    return [
        (D, 2 * INNER),
        (INNER, RANK + 2 * STATE),
        (RANK, INNER),
        (INNER, D),
        (INNER, KERNEL),
        (INNER,),
        (INNER,),
        (INNER, STATE),
        (INNER,),
        (D,),
    ]


def bounds():
    edges = [0]
    for shape in param_shapes():
        edges.append(edges[-1] + math.prod(shape))
    return edges


def slot_index(owners):
    count = owners.shape[0]
    order = jnp.arange(count, dtype=jnp.int32)
    same = (owners[None, :] == owners[:, None]) & (order[None, :] < order[:, None])
    return jnp.sum(same.astype(jnp.int32), axis=1)


def swap(value, axis, bit):
    size = lax.axis_size(axis)
    return lax.ppermute(value, axis, [(i, i ^ bit) for i in range(size)])


def up_to(value, multiple):
    return -(-value // multiple) * multiple


def pad_rows(value, rows, axis):
    widths = [(0, 0)] * value.ndim
    widths[axis] = (0, rows - value.shape[axis])
    return jnp.pad(value, widths)


def gather_params(weights, owners, rank):
    size = lax.axis_size("dp")
    me = lax.axis_index("dp")
    core = lax.axis_index("seq")
    blocks, block_len = owners.shape[0], weights.shape[1]
    rows = block_len // LANES
    padded = up_to(rows, 16)
    near = min(4, size)
    tiles = weights.reshape(SLOTS, rows, LANES)
    rounded = lax.reduce_precision(tiles, 8, 7)
    pair = SLOTS // 2
    mine = lax.dynamic_slice_in_dim(rounded, core * pair, pair, 0).astype(BF)
    many = pad_rows(mine, padded, 1).reshape(pair * padded, LANES)
    first = MATRIX_END // block_len
    last = (PARAMS - 1) // block_len + 1
    own = owners == me
    order = jnp.arange(blocks, dtype=jnp.int32)
    before = order[None, :] < order[first:last, None]
    earlier = jnp.sum((before & own[None, :]).astype(jnp.int32), axis=1)
    slot = jnp.where(own[first:last], earlier, SLOTS)
    here = (slot[:, None] == jnp.arange(SLOTS, dtype=jnp.int32)[None, :])[:, :, None, None]
    fine = jnp.sum(jnp.where(here, (tiles - rounded)[None], 0.0), axis=1).astype(BF)
    fine_rows = (last - first) * rows
    fine_half = up_to(fine_rows, 32) // 2
    fine = pad_rows(fine.reshape(fine_rows, LANES), 2 * fine_half, 0)
    fine = lax.dynamic_slice_in_dim(fine, core * fine_half, fine_half, 0)
    away = owners ^ me
    spot = jnp.zeros_like(owners)
    bit, step = size // 2, 0
    while bit >= near:
        got = swap(jnp.concatenate([many, fine], axis=0), "dp", bit)
        count = many.shape[0]
        many = jnp.concatenate([many, got[:count]], axis=0)
        fine = fine + got[count:]
        spot = spot + jnp.where((away & bit) != 0, 1 << step, 0)
        bit, step = bit // 2, step + 1
    count = many.shape[0]
    sent = jnp.concatenate([many, fine], axis=0)
    others = [swap(sent, "dp", k) for k in range(1, near)]
    many = jnp.stack([many] + [item[:count] for item in others])
    for item in others:
        fine = fine + item[count:]
    spot = (spot + (away & (near - 1)) * (size // near)) * pair + rank % pair
    chosen = many.reshape(size * pair, padded, LANES)[spot]
    theirs = swap(chosen, "seq", 1)
    fine_got = swap(fine, "seq", 1)
    local = (rank // pair == core)[:, None, None]
    theta = jnp.where(local, chosen, theirs)[:, :rows].reshape(blocks * rows, LANES)
    fine = jnp.concatenate(
        [jnp.where(core == 0, fine, fine_got), jnp.where(core == 0, fine_got, fine)], axis=0
    )
    begin = (MATRIX_END - first * block_len) // LANES
    fine = fine[begin : begin + (PARAMS - MATRIX_END) // LANES]
    return lax.optimization_barrier((theta, fine))


def scatter_sum(value, size):
    me = lax.axis_index("dp")
    stride = 1
    total = value
    while stride < size:
        radix = min(4, size // stride)
        total = total.reshape((size // (stride * radix), radix) + value.shape[1:])
        digit = (me // stride) % radix
        low = total.astype(BF)
        kept = lax.dynamic_index_in_dim(total, digit, 1, keepdims=False).astype(F32)
        for k in range(1, radix):
            given = lax.dynamic_index_in_dim(low, digit ^ k, 1, keepdims=False)
            kept = kept + swap(given, "dp", k * stride).astype(F32)
        total = kept
        stride *= radix
    return total[0]


def other_half(value, core):
    count = value.shape[0] // 2
    return swap(lax.dynamic_slice_in_dim(value, (1 - core) * count, count, 0), "seq", 1)


def by_position(kept, given, core):
    got = swap(given, "seq", 1)
    return jnp.concatenate(
        [jnp.where(core == 0, kept, got), jnp.where(core == 0, got, kept)], axis=0
    )


def on_device(
    inputs, cotangent, loss_mask, complement_map, owners, weights, first_moment, second_moment
):
    size = lax.axis_size("dp")
    me = lax.axis_index("dp")
    core = lax.axis_index("seq")
    blocks, block_len = owners.shape[0], weights.shape[1]
    rows = block_len // LANES
    pair = SLOTS // 2
    rank = slot_index(owners)
    order = jnp.arange(blocks, dtype=jnp.int32)
    matches = (owners[None, :] == me) & (
        rank[None, :] == jnp.arange(SLOTS, dtype=jnp.int32)[:, None]
    )
    occupied = jnp.any(matches, axis=1)
    block_of = jnp.sum(jnp.where(matches, order[None, :], 0), axis=1)
    theta, fine = gather_params(weights, owners, rank)
    upstream = cotangent * loss_mask.astype(BF)[..., None]
    x_got = other_half(inputs, core)
    up_got = other_half(upstream, core)

    edges = [edge // LANES for edge in bounds()]
    shapes = param_shapes()
    tail = edges[4]

    def high_of(index):
        return theta[edges[index] : edges[index + 1]].reshape(shapes[index])

    def full_of(index):
        part = theta[edges[index] : edges[index + 1]].astype(F32)
        part = part + fine[edges[index] - tail : edges[index + 1] - tail].astype(F32)
        return part.reshape(shapes[index])

    perm = (complement_map[:, None] == jnp.arange(D, dtype=jnp.int32)[None, :]).astype(BF)
    results = run_layer(
        core,
        inputs,
        x_got,
        upstream,
        up_got,
        perm,
        *[high_of(index) for index in range(4)],
        *[full_of(index) for index in range(4, 10)],
    )
    pieces = layer_grads(results[4:])
    padded = up_to(rows, 16)
    spare = jnp.zeros(((blocks + 1) * rows - PARAMS // LANES, LANES), BF)
    tiles = [item.astype(BF).reshape(-1, LANES) for item in pieces] + [spare]
    grad_blocks = jnp.concatenate(tiles, axis=0).reshape(blocks + 1, rows, LANES)
    grad_blocks = pad_rows(grad_blocks, padded, 1)
    source = jnp.full((size * SLOTS,), blocks, jnp.int32).at[owners * SLOTS + rank].set(order)
    source = source.reshape(size, 2, pair)

    def for_core(which):
        index = lax.dynamic_index_in_dim(source, which, 1, keepdims=False)
        return grad_blocks[index.reshape(-1)].reshape(size * pair * padded, LANES)

    got = swap(for_core(1 - core), "seq", 1)
    chip = (for_core(core).astype(F32) + got.astype(F32)).astype(BF)
    chip = chip.reshape(size, pair * padded, LANES)
    summed = scatter_sum(chip, size).reshape(pair, -1, LANES)[:, :rows]
    other = swap(summed, "seq", 1)
    owned = jnp.concatenate(
        [jnp.where(core == 0, summed, other), jnp.where(core == 0, other, summed)], axis=0
    ).reshape(SLOTS, block_len)
    output = by_position(results[0], results[1], core)
    grad_input = by_position(results[2], results[3], core)
    new_first = BETA_ONE * first_moment + (1.0 - BETA_ONE) * owned
    new_second = BETA_TWO * second_moment + (1.0 - BETA_TWO) * owned * owned
    position = block_of[:, None] * block_len + jnp.arange(block_len, dtype=jnp.int32)[None, :]
    is_matrix = position < MATRIX_END
    rate = jnp.where(is_matrix, RATE_MATRIX, RATE_VECTOR)
    decay = jnp.where(is_matrix, WEIGHT_DECAY, 0.0)
    corrected = (
        new_first
        / (1.0 - BETA_ONE**STEP_COUNT)
        / (jnp.sqrt(new_second / (1.0 - BETA_TWO**STEP_COUNT)) + ADAM_EPSILON)
    )
    new_theta = weights - rate * (corrected + decay * weights)
    keep = occupied[:, None]
    return (
        output,
        grad_input,
        jnp.where(keep, new_theta, 0.0),
        jnp.where(keep, new_first, 0.0),
        jnp.where(keep, new_second, 0.0),
    )


def solution(mesh):
    in_specs = (
        P("dp", "seq", None),
        P("dp", "seq", None),
        P("dp", "seq"),
        P(),
        P(),
        P("dp", None),
        P("dp", None),
        P("dp", None),
    )
    out_specs = (
        P("dp", "seq", None),
        P("dp", "seq", None),
        P("dp", None),
        P("dp", None),
        P("dp", None),
    )
    return jax.shard_map(
        on_device, mesh=mesh, in_specs=in_specs, out_specs=out_specs, check_vma=False
    )
```

```python
import functools
import math

import jax
import jax.numpy as jnp
from jax import lax
from jax.experimental import pallas as pl
from jax.experimental.pallas import tpu as pltpu
from jax.sharding import PartitionSpec as P

D = 256
INNER = 512
STATE = 16
RANK = 16
KERNEL = 4
SLOTS = 4
STEP_COUNT = 10
PARAMS = 438016
MATRIX_END = 425984
BETA_ONE = 0.9
BETA_TWO = 0.95
ADAM_EPSILON = 1e-08
RATE_MATRIX = 0.1
RATE_VECTOR = 0.5
WEIGHT_DECAY = 0.1
NORM_EPSILON = 1e-05
LOG2E = 1.4426950408889634
LN2 = 0.6931471805599453
CHUNK = 128
GROUP = 16
SLAB = 512
REACH = 256
BLOCK = 32
LANES = 128
WIDE = GROUP * STATE
BF = jnp.bfloat16
F32 = jnp.float32
NT = (((1,), (1,)), ((), ()))
TN = (((0,), (0,)), ((), ()))


def split_low(value):
    high = value.astype(BF)
    return high, (value - high.astype(F32)).astype(BF)


def dot(a, b, dims=None):
    if dims is None:
        return jnp.dot(a, b, preferred_element_type=F32)
    return lax.dot_general(a, b, dims, preferred_element_type=F32)


def row_sum(value):
    return jnp.sum(value.reshape(value.shape[0] // 8, 8, value.shape[1]), axis=0)


def span(start, count, step=None):
    return pl.ds(pl.multiple_of(start, step or count), count)


def iota(shape, axis):
    return lax.broadcasted_iota(jnp.int32, shape, axis)


def spread(value, index):
    return jnp.broadcast_to(value[index : index + 1, :], (8, LANES))


def each(count, body):
    lax.fori_loop(0, count, lambda i, c: (body(i), c)[1], 0)


def layer_kernel(
    core_ref,
    x_kept_ref,
    x_got_ref,
    up_kept_ref,
    up_got_ref,
    perm_ref,
    w_in_ref,
    w_out_ref,
    wx_ref,
    wdt_ref,
    vec_ref,
    rate_ref,
    gain_ref,
    out_kept_ref,
    out_given_ref,
    gin_kept_ref,
    gin_given_ref,
    gwin_out,
    gwout_out,
    gsmall_out,
    gvec_out,
    ggain_out,
    states,
    act_s,
    slope_s,
    delta_s,
    ratio_s,
    dscan_s,
    u_s,
    y_s,
    gsilu_s,
    gslope_s,
    inner_s,
    dread_s,
    projt_s,
    dproj_s,
    gated_s,
    copy_s,
    dmix_s,
    x_s,
    up_s,
    dnorm_s,
    wide_s,
    read_s,
    entry_s,
    w_in_s,
    w_out_s,
    flip_s,
    tile_s,
    fold_s,
    sums_s,
    mask_s,
    near_s,
    wx_s,
    wdt_s,
    gwin_ref,
    gwout_ref,
    gsmall_ref,
    gvec_ref,
    ggain_ref,
    flat_s,
):
    window = pl.program_id(0)
    natural = pl.program_id(1)
    core = core_ref[0]
    length = x_s.shape[0]
    half = length // 2
    chunks = length // CHUNK
    slabs = length // SLAB
    groups = REACH // GROUP
    pieces = range(0, SLAB, BLOCK)

    @pl.when((window == 0) & (natural == 0))
    def _():
        gwin_ref[...] = jnp.zeros_like(gwin_ref)
        gwout_ref[...] = jnp.zeros_like(gwout_ref)
        gsmall_ref[...] = jnp.zeros_like(gsmall_ref)
        gvec_ref[...] = jnp.zeros_like(gvec_ref)
        ggain_ref[...] = jnp.zeros_like(ggain_ref)
        wx_s[...] = jnp.zeros_like(wx_s)
        wx_s[:, : 3 * STATE] = wx_ref[...]
        wdt_s[...] = jnp.zeros_like(wdt_s)
        wdt_s[:RANK, :] = wdt_ref[...]
        inner_s[0:16, :] = jnp.zeros((16, INNER), BF)
        gsilu_s[length : length + 8, :] = jnp.zeros((8, INNER), F32)
        rows, lanes = iota((CHUNK, CHUNK), 0), iota((CHUNK, CHUNK), 1)
        flip_s[1] = jnp.where(rows == lanes, 1.0, 0.0).astype(BF)
        flip_s[0] = jnp.where(rows + lanes == CHUNK - 1, 1.0, 0.0).astype(BF)
        rows, lanes = iota((LANES, WIDE), 0), iota((LANES, WIDE), 1)
        for k in range(2):
            tile_s[k] = jnp.where(rows == STATE * (k + 1) + lanes % STATE, 1.0, 0.0).astype(BF)
        rows, lanes = iota((WIDE, LANES), 0), iota((WIDE, LANES), 1)
        for k in range(2):
            fold_s[k] = jnp.where(lanes == STATE * (k + 1) + rows % STATE, 1.0, 0.0).astype(BF)
        rows, lanes = iota((GROUP, WIDE), 0), iota((GROUP, WIDE), 1)
        mask_s[0] = jnp.where(GROUP - 1 - rows == lanes // STATE, 1.0, 0.0)
        mask_s[1] = jnp.where(rows == lanes // STATE, 1.0, 0.0)
        sums_s[:GROUP, :] = mask_s[0].astype(BF)
        sums_s[GROUP:, :] = jnp.where(rows == lanes % STATE, 1.0, 0.0).astype(BF)

    @pl.when(natural == 0)
    def _():
        kept, got = span(core * half, half), span((1 - core) * half, half)
        x_s[kept, :] = x_kept_ref[0]
        x_s[got, :] = x_got_ref[0]
        up_s[kept, :] = up_kept_ref[0]
        up_s[got, :] = up_got_ref[0]
        w_in_s[...] = dot(perm_ref[...], w_in_ref[...], TN).astype(BF)
        w_out_s[...] = dot(w_out_ref[...], perm_ref[...]).astype(BF)

    @pl.when(natural == 1)
    def _():
        w_in_s[...] = w_in_ref[...]
        w_out_s[...] = w_out_ref[...]

    def place_of(chunk):
        return jnp.where(natural == 1, chunk, chunks - 1 - chunk) * CHUNK

    def norm_parts(rows):
        xf = x_s[rows, :].astype(F32)
        inv = lax.rsqrt(jnp.mean(xf * xf, axis=-1, keepdims=True) + NORM_EPSILON)
        return xf, inv

    def load_copies(slab):
        rows = span(slab * SLAB, SLAB)
        xf, inv = norm_parts(rows)
        normed = (xf * inv * gain_ref[...]).astype(BF)
        upstream = up_s[rows, :]
        for k in range(SLAB // CHUNK):
            part = slice(k * CHUNK, (k + 1) * CHUNK)
            there = span(place_of(slab * (SLAB // CHUNK) + k), CHUNK)
            copy_s[there, :] = dot(flip_s[natural], normed[part]).astype(BF)
            dmix_s[there, :] = dot(flip_s[natural], upstream[part]).astype(BF)

    each(slabs, load_copies)

    def project(slab):
        row = slab * SLAB
        copy = copy_s[span(row, SLAB), :]
        inner_s[span(row + 16, SLAB, 16), :] = dot(copy, w_in_s[:, :INNER]).astype(BF)
        gate_all = dot(copy, w_in_s[:, INNER:]).astype(BF)
        dgated_all = dot(dmix_s[span(row, SLAB), :], w_out_s[...], NT).astype(BF)
        for a in pieces:
            rows = span(row + a, BLOCK)
            gate = gate_all[a : a + BLOCK].astype(F32)
            dgated = dgated_all[a : a + BLOCK].astype(F32)
            sig = 0.5 + 0.5 * jnp.tanh(0.5 * gate)
            silu = gate * sig
            gsilu_s[rows, :] = silu
            dscan_s[rows, :] = dgated * silu
            gslope_s[rows, :] = dgated * (sig + silu * (1.0 - sig))

    each(slabs, project)

    def convolve(slab):
        row = slab * SLAB
        near_s[...] = inner_s[span(row, SLAB + 16, 16), :].astype(F32)
        for a in pieces:
            rows = span(row + a, BLOCK)
            conv = vec_ref[4:5, :]
            for j in range(KERNEL):
                conv = conv + vec_ref[j : j + 1, :] * near_s[a + 13 + j : a + 13 + j + BLOCK, :]
            sig = 0.5 + 0.5 * jnp.tanh(0.5 * conv)
            act = conv * sig
            act_s[rows, :] = act
            slope_s[rows, :] = sig + act * (1.0 - sig)
        act_high, act_low = split_low(act_s[span(row, SLAB), :])
        proj = dot(act_high, wx_s[...]) + dot(act_low, wx_s[...])
        for k in range(SLAB // CHUNK):
            turned = jnp.transpose(proj[k * CHUNK : (k + 1) * CHUNK])
            projt_s[slab * (SLAB // CHUNK) + k] = turned[: 3 * STATE]
        proj_high, proj_low = split_low(proj)
        for kind, target in ((0, entry_s), (1, read_s)):
            wide = dot(proj_high, tile_s[kind])
            for g in range(SLAB // GROUP):
                part = wide[g * GROUP : (g + 1) * GROUP] * mask_s[kind]
                target[span(row + g * GROUP, GROUP), :] = part.astype(BF)
        pre_all = dot(proj_high, wdt_s[...]) + dot(proj_low, wdt_s[...])
        for a in pieces:
            rows = span(row + a, BLOCK)
            pre = pre_all[a : a + BLOCK] + vec_ref[5:6, :]
            small = jnp.exp(-jnp.abs(pre))
            whole = 1.0 + small
            share = 1.0 / whole
            log_part = jnp.log(whole) + (small - (whole - 1.0)) * share
            delta = jnp.maximum(pre, 0.0) + log_part
            scaled = jnp.where(pre >= 0.0, share, small * share) / delta
            delta_s[rows, :] = delta
            ratio_s[rows, :] = jnp.where(delta > 1e-30, scaled, 1.0)
            u_s[rows, :] = delta * act_s[rows, :]

    each(slabs, convolve)

    zero = jnp.zeros((8, LANES), F32)
    ones = jnp.ones((GROUP, LANES), BF)
    lane_sets = [slice(LANES * e, LANES * (e + 1)) for e in range(4)]

    def pack(top, bottom):
        return jnp.concatenate([top, bottom], axis=0).astype(BF)

    def turned_of(index):
        each_chunk = REACH // CHUNK
        return [projt_s[index * each_chunk + k] for k in range(each_chunk)]

    def scan_chunk(index, carry):
        state = [list(carry[0:4]), list(carry[4:8])]
        last = list(carry[8:])
        turned = turned_of(index)
        for g in range(groups):
            base = index * REACH + g * GROUP
            columns = turned[g * GROUP // CHUNK]
            rows = span(base, GROUP)
            steps = delta_s[rows, :]
            feeds = u_s[rows, :]
            pulls = dscan_s[rows, :]
            held, sums = [], []
            for t in range(GROUP):
                at = (g * GROUP + t) % CHUNK
                entry = [
                    jnp.broadcast_to(
                        columns[STATE + 8 * h : STATE + 8 * h + 8, at : at + 1], (8, LANES)
                    )
                    for h in range(2)
                ]
                place = span((base + t) * STATE, STATE)
                total = [None, None]
                for e, lanes in enumerate(lane_sets):
                    step = spread(steps[:, lanes], t)
                    feed = spread(feeds[:, lanes], t)
                    pull = spread(pulls[:, lanes], t)
                    for h in range(2):
                        decay = jnp.exp2(step * rate_ref[8 * h : 8 * h + 8, lanes])
                        state[h][e] = decay * state[h][e] + feed * entry[h]
                        part = pull * state[h][e]
                        total[h] = part if e == 0 else total[h] + part
                    states[place, lanes] = last[e]
                    last[e] = pack(state[0][e], state[1][e])
                held.append(jnp.concatenate(last, axis=1))
                sums.append(pack(*total))
            y_s[rows, :] = dot(read_s[rows, :], jnp.concatenate(held, axis=0))
            found = dot(ones, jnp.concatenate(sums, axis=0), NT)
            wide_s[rows, :] = (found * mask_s[1]).astype(BF)
        return tuple(state[0] + state[1] + last)

    lax.fori_loop(0, length // REACH, scan_chunk, (zero,) * 8 + (pack(zero, zero),) * 4)

    def finish(slab):
        row = slab * SLAB
        dread_s[span(row, SLAB), :] = dot(wide_s[span(row, SLAB), :], fold_s[1]).astype(BF)
        for a in pieces:
            rows = span(row + a, BLOCK)
            scanned = y_s[rows, :] + vec_ref[6:7, :] * act_s[rows, :]
            gated_s[rows, :] = (scanned * gsilu_s[rows, :]).astype(BF)
            dproj_s[rows, INNER:] = (scanned * gslope_s[rows, :]).astype(BF)

    each(slabs, finish)

    def store_half(kept_ref, given_ref, which, rows, value):
        @pl.when(which == core)
        def _():
            kept_ref[0, rows, :] = value

        @pl.when(which != core)
        def _():
            given_ref[0, rows, :] = value

    def mirror_mixed(slab):
        mixed_all = dot(gated_s[span(slab * SLAB, SLAB), :], w_out_s[...])
        for k in range(SLAB // CHUNK):
            high, low = split_low(mixed_all[k * CHUNK : (k + 1) * CHUNK])
            place = place_of(slab * (SLAB // CHUNK) + k)
            mixed = dot(flip_s[0], high) + dot(flip_s[0], low)
            store_half(gin_kept_ref, gin_given_ref, place // half, span(place % half, CHUNK), mixed)

    def natural_mixed(slab):
        rows = span(slab * SLAB, SLAB)
        mixed = dot(gated_s[rows, :], w_out_s[...])
        total = x_s[rows, :].astype(F32) + mixed

        @pl.when(slab == core)
        def _():
            out_kept_ref[0] = (total + gin_kept_ref[0]).astype(BF)

        @pl.when(slab != core)
        def _():
            out_given_ref[0] = (total + gin_given_ref[0]).astype(BF)

    @pl.when(natural == 0)
    def _():
        each(slabs, mirror_mixed)
        dmix_s[...] = dot(dmix_s[...], perm_ref[...], NT).astype(BF)

    @pl.when(natural == 1)
    def _():
        each(slabs, natural_mixed)

    gwout_ref[...] += dot(gated_s[...], dmix_s[...], TN)

    def back_chunk(step_index, carry_all):
        index = length // REACH - 1 - step_index
        carry = [list(carry_all[0:4]), list(carry_all[4:8])]
        rate_sum = carry_all[8]
        turned = turned_of(index)
        for g in reversed(range(groups)):
            base = index * REACH + g * GROUP
            columns = turned[g * GROUP // CHUNK]
            rows = span(base, GROUP)
            steps = delta_s[rows, :]
            feeds = dscan_s[rows, :]
            pulls = u_s[rows, :]
            held, prods, sums = [], [], []
            for t in reversed(range(GROUP)):
                at = (g * GROUP + t) % CHUNK
                read = [
                    jnp.broadcast_to(
                        columns[2 * STATE + 8 * h : 2 * STATE + 8 * h + 8, at : at + 1], (8, LANES)
                    )
                    for h in range(2)
                ]
                place = span((base + t) * STATE, STATE)
                held_row, prod_row = [], []
                total = [None, None]
                for e, lanes in enumerate(lane_sets):
                    step = spread(steps[:, lanes], t)
                    feed = spread(feeds[:, lanes], t)
                    pull = spread(pulls[:, lanes], t)
                    before = states[place, lanes]
                    lams, both = [], []
                    for h in range(2):
                        power = step * rate_ref[8 * h : 8 * h + 8, lanes]
                        lam = feed * read[h] + carry[h][e]
                        carry[h][e] = jnp.exp2(power) * lam
                        lams.append(lam)
                        part = pull * lam
                        total[h] = part if e == 0 else total[h] + part
                        both.append(power * carry[h][e])
                    held_row.append(pack(*lams))
                    prod_row.append(pack(*both) * before)
                held.append(jnp.concatenate(held_row, axis=1))
                prods.append(jnp.concatenate(prod_row, axis=1))
                sums.append(pack(*total))
            y_s[rows, :] = dot(entry_s[rows, :], jnp.concatenate(held, axis=0))
            both = dot(sums_s[...], jnp.concatenate(prods, axis=0))
            gslope_s[rows, :] = both[:GROUP]
            rate_sum = rate_sum + both[GROUP:]
            found = dot(ones, jnp.concatenate(sums, axis=0), NT)
            wide_s[rows, :] = (found * mask_s[0]).astype(BF)
        return tuple(carry[0] + carry[1]) + (rate_sum,)

    done = lax.fori_loop(
        0, length // REACH, back_chunk, (zero,) * 8 + (jnp.zeros((STATE, INNER), F32),)
    )
    gsmall_ref[0:STATE, :] += done[8] * LN2

    def gradients(slab):
        row = slab * SLAB
        sum_pre = sum_skip = None
        for a in pieces:
            rows = span(row + a, BLOCK)
            dfeed = y_s[rows, :]
            dpre = ratio_s[rows, :] * (gslope_s[rows, :] * LN2 + dfeed * u_s[rows, :])
            gsilu_s[rows, :] = dpre
            dscan = dscan_s[rows, :]
            y_s[rows, :] = dscan * vec_ref[6:7, :] + dfeed * delta_s[rows, :]
            one, two = row_sum(dpre), row_sum(dscan * act_s[rows, :])
            sum_pre = one if sum_pre is None else sum_pre + one
            sum_skip = two if sum_skip is None else sum_skip + two
        gvec_ref[5] += sum_pre
        gvec_ref[6] += sum_skip
        dpre_all = gsilu_s[span(row, SLAB), :].astype(BF)
        dproj = (
            dot(dpre_all, wdt_s[...], NT)
            + dot(wide_s[span(row, SLAB), :], fold_s[0])
            + dread_s[span(row, SLAB), :].astype(F32)
        )
        extra = dot(dproj.astype(BF), wx_s[...], NT)
        low_sum = None
        for k in range(SLAB // CHUNK):
            low = projt_s[slab * (SLAB // CHUNK) + k][:RANK].astype(BF)
            part = dot(low, dpre_all[k * CHUNK : (k + 1) * CHUNK])
            low_sum = part if low_sum is None else low_sum + part
        gsmall_ref[STATE : 2 * STATE, :] += low_sum
        gsmall_ref[2 * STATE : 5 * STATE, :] += dot(
            dproj.astype(BF), act_s[span(row, SLAB), :].astype(BF), TN
        )[: 3 * STATE]
        for a in pieces:
            rows = span(row + a, BLOCK)
            gsilu_s[rows, :] = (y_s[rows, :] + extra[a : a + BLOCK]) * slope_s[rows, :]

    each(slabs, gradients)

    def unconvolve(slab):
        row = slab * SLAB
        totals = [None] * 5
        near_s[: SLAB + 8, :] = gsilu_s[span(row, SLAB + 8, 8), :]
        for a in pieces:
            rows = span(row + a, BLOCK)
            inner = inner_s[span(row + a + 16, BLOCK, 16), :].astype(F32)
            dinner = None
            for j in range(KERNEL):
                moved = near_s[a + 3 - j : a + 3 - j + BLOCK, :]
                term = vec_ref[j : j + 1, :] * moved
                dinner = term if dinner is None else dinner + term
                part = row_sum(moved * inner)
                totals[j] = part if totals[j] is None else totals[j] + part
            part = row_sum(near_s[a : a + BLOCK, :])
            totals[4] = part if totals[4] is None else totals[4] + part
            dproj_s[rows, :INNER] = dinner.astype(BF)
        for j in range(5):
            gvec_ref[j] += totals[j]

    each(slabs, unconvolve)

    def mirror_dnorm(slab):
        dnorm_all = dot(dproj_s[span(slab * SLAB, SLAB), :], w_in_s[...], NT)
        for k in range(SLAB // CHUNK):
            high, low = split_low(dnorm_all[k * CHUNK : (k + 1) * CHUNK])
            there = span(place_of(slab * (SLAB // CHUNK) + k), CHUNK)
            dnorm_s[there, :] = dot(flip_s[0], high) + dot(flip_s[0], low)

    def natural_dnorm(slab):
        rows = span(slab * SLAB, SLAB)
        total = dot(dproj_s[rows, :], w_in_s[...], NT) + dnorm_s[rows, :]
        xf, inv = norm_parts(rows)
        scaled = total * gain_ref[...]
        hat = xf * inv
        ggain_ref[...] += row_sum(total * hat)
        mean = jnp.mean(scaled * hat, axis=-1, keepdims=True)
        result = up_s[rows, :].astype(F32) + inv * (scaled - hat * mean)
        store_half(gin_kept_ref, gin_given_ref, slab, slice(None), result)

    @pl.when(natural == 0)
    def _():
        each(slabs, mirror_dnorm)
        copy_s[...] = dot(copy_s[...], perm_ref[...], NT).astype(BF)

    @pl.when(natural == 1)
    def _():
        each(slabs, natural_dnorm)

    gwin_ref[...] += dot(copy_s[...], dproj_s[...], TN)

    @pl.when((window == pl.num_programs(0) - 1) & (natural == 1))
    def _():
        for source, target in ((gwin_ref, gwin_out), (gwout_ref, gwout_out)):
            parts = source.shape[1] // LANES
            count = flat_s.shape[0] // parts
            for p in range(source.shape[0] // count):
                for k in range(parts):
                    flat_s[pl.ds(k, count, stride=parts), :] = source[
                        p * count : (p + 1) * count, k * LANES : (k + 1) * LANES
                    ]
                target[p * flat_s.shape[0] : (p + 1) * flat_s.shape[0], :] = flat_s[...].astype(BF)
        gsmall_out[...] = gsmall_ref[...].astype(BF)
        vectors = [jnp.sum(gvec_ref[j], axis=0, keepdims=True) for j in range(7)]
        vectors.append(jnp.zeros((9, INNER), F32))
        gvec_out[...] = jnp.concatenate(vectors, axis=0).astype(BF)
        gain = jnp.sum(ggain_ref[...], axis=0, keepdims=True)
        ggain_out[...] = jnp.broadcast_to(gain, (16, D)).astype(BF)


def run_layer(
    core, x, x_got, up, up_got, perm, w_in, w_x, w_dt, w_out, conv_w, conv_b, dt_bias, a_log, d_skip, gain
):
    windows, half, _ = x_got.shape
    length = 2 * half
    vec = jnp.concatenate(
        [conv_w.T, conv_b[None], dt_bias[None], d_skip[None], jnp.zeros((1, INNER), F32)], axis=0
    )
    rate = (-LOG2E) * jnp.exp(a_log).T

    def whole(shape):
        return pl.BlockSpec(shape, lambda w, q, core: (0,) * len(shape))

    kept = pl.BlockSpec((1, half, D), lambda w, q, core: (windows * core[0] + w, 0, 0))
    got = pl.BlockSpec((1, half, D), lambda w, q, core: (w, 0, 0))
    fixed = (perm, w_in, w_out, w_x, w_dt, vec, rate, gain[None])
    grads = [
        jax.ShapeDtypeStruct((D * 2 * INNER // LANES, LANES), BF),
        jax.ShapeDtypeStruct((INNER * D // LANES, LANES), BF),
        jax.ShapeDtypeStruct((5 * STATE, INNER), BF),
        jax.ShapeDtypeStruct((16, INNER), BF),
        jax.ShapeDtypeStruct((16, D), BF),
    ]
    inner_f32 = [pltpu.VMEM((length, INNER), F32)]
    outer_bf = [pltpu.VMEM((length, D), BF)]
    outer_f32 = [pltpu.VMEM((length, D), F32)]
    halo_f32 = [pltpu.VMEM((length + 8, INNER), F32)]
    scratch = (
        [pltpu.VMEM((length * STATE, INNER), BF)]
        + inner_f32 * 7
        + halo_f32
        + inner_f32
        + [pltpu.VMEM((length + 16, INNER), BF)]
        + [pltpu.VMEM((length, LANES), BF)]
        + [
            pltpu.VMEM((length // CHUNK, 3 * STATE, CHUNK), F32),
            pltpu.VMEM((length, 2 * INNER), BF),
            pltpu.VMEM((length, INNER), BF),
        ]
        + outer_bf * 4
        + outer_f32
        + [pltpu.VMEM((length, WIDE), BF)] * 3
        + [
            pltpu.VMEM((D, 2 * INNER), BF),
            pltpu.VMEM((INNER, D), BF),
            pltpu.VMEM((2, CHUNK, CHUNK), BF),
            pltpu.VMEM((2, LANES, WIDE), BF),
            pltpu.VMEM((2, WIDE, LANES), BF),
            pltpu.VMEM((2 * GROUP, WIDE), BF),
            pltpu.VMEM((2, GROUP, WIDE), F32),
            pltpu.VMEM((SLAB + 16, INNER), F32),
            pltpu.VMEM((INNER, LANES), BF),
            pltpu.VMEM((LANES, INNER), BF),
            pltpu.VMEM((D, 2 * INNER), F32),
            pltpu.VMEM((INNER, D), F32),
            pltpu.VMEM((5 * STATE, INNER), F32),
            pltpu.VMEM((7, 8, INNER), F32),
            pltpu.VMEM((8, D), F32),
            pltpu.VMEM((SLAB, LANES), F32),
        ]
    )
    return pl.pallas_call(
        layer_kernel,
        grid_spec=pltpu.PrefetchScalarGridSpec(
            num_scalar_prefetch=1,
            grid=(windows, 2),
            in_specs=[kept, got, kept, got] + [whole(item.shape) for item in fixed],
            out_specs=[got] * 4 + [whole(item.shape) for item in grads],
            scratch_shapes=scratch,
        ),
        out_shape=[
            jax.ShapeDtypeStruct((windows, half, D), kind) for kind in (BF, BF, F32, F32)
        ]
        + grads,
        compiler_params=pltpu.CompilerParams(vmem_limit_bytes=64 * 2**20 - 65536),
    )(core.reshape(1).astype(jnp.int32), x, x_got, up, up_got, *fixed)


def layer_grads(results):
    gwin, gwout, gsmall, gvec, ggain = results
    return [
        gwin,
        gsmall[2 * STATE :].T,
        gsmall[STATE : 2 * STATE],
        gwout,
        gvec[:KERNEL].T,
        gvec[4],
        gvec[5],
        gsmall[:STATE].T,
        gvec[6],
        ggain[0],
    ]


def param_shapes():
    return [
        (D, 2 * INNER),
        (INNER, RANK + 2 * STATE),
        (RANK, INNER),
        (INNER, D),
        (INNER, KERNEL),
        (INNER,),
        (INNER,),
        (INNER, STATE),
        (INNER,),
        (D,),
    ]


def bounds():
    edges = [0]
    for shape in param_shapes():
        edges.append(edges[-1] + math.prod(shape))
    return edges


def slot_index(owners):
    count = owners.shape[0]
    order = jnp.arange(count, dtype=jnp.int32)
    same = (owners[None, :] == owners[:, None]) & (order[None, :] < order[:, None])
    return jnp.sum(same.astype(jnp.int32), axis=1)


def swap(value, axis, bit):
    size = lax.axis_size(axis)
    return lax.ppermute(value, axis, [(i, i ^ bit) for i in range(size)])


def up_to(value, multiple):
    return -(-value // multiple) * multiple


def pad_rows(value, rows, axis):
    widths = [(0, 0)] * value.ndim
    widths[axis] = (0, rows - value.shape[axis])
    return jnp.pad(value, widths)


def gather_params(weights, owners, rank, matches):
    size = lax.axis_size("dp")
    me = lax.axis_index("dp")
    core = lax.axis_index("seq")
    blocks, block_len = owners.shape[0], weights.shape[1]
    rows = block_len // LANES
    padded = up_to(rows, 16)
    near = min(4, size)
    tiles = weights.reshape(SLOTS, rows, LANES)
    rounded = lax.reduce_precision(tiles, 8, 7)
    pair = SLOTS // 2
    mine = lax.dynamic_slice_in_dim(rounded, core * pair, pair, 0).astype(BF)
    many = pad_rows(mine, padded, 1).reshape(pair * padded, LANES)
    first = MATRIX_END // block_len
    last = (PARAMS - 1) // block_len + 1
    here = matches[:, first:last].T[:, :, None, None]
    fine = jnp.sum(jnp.where(here, (tiles - rounded)[None], 0.0), axis=1).astype(BF)
    fine_rows = (last - first) * rows
    fine_half = up_to(fine_rows, 32) // 2
    fine = pad_rows(fine.reshape(fine_rows, LANES), 2 * fine_half, 0)
    fine = lax.dynamic_slice_in_dim(fine, core * fine_half, fine_half, 0)
    away = owners ^ me
    spot = jnp.zeros_like(owners)
    bit, step = size // 2, 0
    while bit >= near:
        count = many.shape[0]
        if step == 0:
            got_many, got_fine = swap(many, "dp", bit), swap(fine, "dp", bit)
        else:
            got = swap(jnp.concatenate([many, fine], axis=0), "dp", bit)
            got_many, got_fine = got[:count], got[count:]
        many = jnp.concatenate([many, got_many], axis=0)
        fine = fine + got_fine
        spot = spot + jnp.where((away & bit) != 0, 1 << step, 0)
        bit, step = bit // 2, step + 1
    count = many.shape[0]
    sent = jnp.concatenate([many, fine], axis=0)
    others = [swap(sent, "dp", k) for k in range(1, near)]
    many = jnp.stack([many] + [item[:count] for item in others])
    for item in others:
        fine = fine + item[count:]
    spot = (spot + (away & (near - 1)) * (size // near)) * pair + rank % pair
    chosen = many.reshape(size * pair, padded, LANES)[spot]
    theirs = swap(chosen, "seq", 1)
    fine_got = swap(fine, "seq", 1)
    local = (rank // pair == core)[:, None, None]
    theta = jnp.where(local, chosen, theirs)[:, :rows].reshape(blocks * rows, LANES)
    fine = jnp.concatenate(
        [jnp.where(core == 0, fine, fine_got), jnp.where(core == 0, fine_got, fine)], axis=0
    )
    begin = (MATRIX_END - first * block_len) // LANES
    fine = fine[begin : begin + (PARAMS - MATRIX_END) // LANES]
    return lax.optimization_barrier((theta, fine))


def scatter_sum(value, size):
    me = lax.axis_index("dp")
    stride = 1
    total = value
    while stride < size:
        radix = min(4, size // stride)
        total = total.reshape((size // (stride * radix), radix) + value.shape[1:])
        digit = (me // stride) % radix
        low = total.astype(BF)
        kept = lax.dynamic_index_in_dim(total, digit, 1, keepdims=False).astype(F32)
        for k in range(1, radix):
            given = lax.dynamic_index_in_dim(low, digit ^ k, 1, keepdims=False)
            kept = kept + swap(given, "dp", k * stride).astype(F32)
        total = kept
        stride *= radix
    return total[0]


def other_half(value, core):
    count = value.shape[0] // 2
    return swap(lax.dynamic_slice_in_dim(value, (1 - core) * count, count, 0), "seq", 1)


def by_position(kept, given, core):
    got = swap(given, "seq", 1)
    return jnp.concatenate(
        [jnp.where(core == 0, kept, got), jnp.where(core == 0, got, kept)], axis=0
    )


def on_device(
    inputs, cotangent, loss_mask, complement_map, owners, weights, first_moment, second_moment
):
    size = lax.axis_size("dp")
    me = lax.axis_index("dp")
    core = lax.axis_index("seq")
    blocks, block_len = owners.shape[0], weights.shape[1]
    rows = block_len // LANES
    pair = SLOTS // 2
    rank = slot_index(owners)
    order = jnp.arange(blocks, dtype=jnp.int32)
    matches = (owners[None, :] == me) & (
        rank[None, :] == jnp.arange(SLOTS, dtype=jnp.int32)[:, None]
    )
    occupied = jnp.any(matches, axis=1)
    block_of = jnp.sum(jnp.where(matches, order[None, :], 0), axis=1)
    theta, fine = gather_params(weights, owners, rank, matches)
    upstream = cotangent * loss_mask.astype(BF)[..., None]
    x_got = other_half(inputs, core)
    up_got = other_half(upstream, core)

    edges = [edge // LANES for edge in bounds()]
    shapes = param_shapes()
    tail = edges[4]

    def high_of(index):
        return theta[edges[index] : edges[index + 1]].reshape(shapes[index])

    def full_of(index):
        part = theta[edges[index] : edges[index + 1]].astype(F32)
        part = part + fine[edges[index] - tail : edges[index + 1] - tail].astype(F32)
        return part.reshape(shapes[index])

    perm = (complement_map[:, None] == jnp.arange(D, dtype=jnp.int32)[None, :]).astype(BF)
    results = run_layer(
        core,
        inputs,
        x_got,
        upstream,
        up_got,
        perm,
        *[high_of(index) for index in range(4)],
        *[full_of(index) for index in range(4, 10)],
    )
    pieces = layer_grads(results[4:])
    padded = up_to(rows, 16)
    spare = jnp.zeros(((blocks + 1) * rows - PARAMS // LANES, LANES), BF)
    tiles = [item.astype(BF).reshape(-1, LANES) for item in pieces] + [spare]
    grad_blocks = jnp.concatenate(tiles, axis=0).reshape(blocks + 1, rows, LANES)
    grad_blocks = pad_rows(grad_blocks, padded, 1)
    source = jnp.full((size * SLOTS,), blocks, jnp.int32).at[owners * SLOTS + rank].set(order)
    source = source.reshape(size, 2, pair)

    def for_core(which):
        index = lax.dynamic_index_in_dim(source, which, 1, keepdims=False)
        return grad_blocks[index.reshape(-1)].reshape(size * pair * padded, LANES)

    got = swap(for_core(1 - core), "seq", 1)
    chip = (for_core(core).astype(F32) + got.astype(F32)).astype(BF)
    chip = chip.reshape(size, pair * padded, LANES)
    summed = scatter_sum(chip, size).reshape(pair, -1, LANES)[:, :rows]
    other = swap(summed, "seq", 1)
    owned = jnp.concatenate(
        [jnp.where(core == 0, summed, other), jnp.where(core == 0, other, summed)], axis=0
    ).reshape(SLOTS, block_len)
    output = by_position(results[0], results[1], core)
    grad_input = by_position(results[2], results[3], core)
    new_first = BETA_ONE * first_moment + (1.0 - BETA_ONE) * owned
    new_second = BETA_TWO * second_moment + (1.0 - BETA_TWO) * owned * owned
    position = block_of[:, None] * block_len + jnp.arange(block_len, dtype=jnp.int32)[None, :]
    is_matrix = position < MATRIX_END
    rate = jnp.where(is_matrix, RATE_MATRIX, RATE_VECTOR)
    decay = jnp.where(is_matrix, WEIGHT_DECAY, 0.0)
    corrected = (
        new_first
        / (1.0 - BETA_ONE**STEP_COUNT)
        / (jnp.sqrt(new_second / (1.0 - BETA_TWO**STEP_COUNT)) + ADAM_EPSILON)
    )
    new_theta = weights - rate * (corrected + decay * weights)
    keep = occupied[:, None]
    return (
        output,
        grad_input,
        jnp.where(keep, new_theta, 0.0),
        jnp.where(keep, new_first, 0.0),
        jnp.where(keep, new_second, 0.0),
    )


def solution(mesh):
    in_specs = (
        P("dp", "seq", None),
        P("dp", "seq", None),
        P("dp", "seq"),
        P(),
        P(),
        P("dp", None),
        P("dp", None),
        P("dp", None),
    )
    out_specs = (
        P("dp", "seq", None),
        P("dp", "seq", None),
        P("dp", None),
        P("dp", None),
        P("dp", None),
    )
    return jax.shard_map(
        on_device, mesh=mesh, in_specs=in_specs, out_specs=out_specs, check_vma=False
    )
```

```python
import functools
import math

import jax
import jax.numpy as jnp
from jax import lax
from jax.experimental import pallas as pl
from jax.experimental.pallas import tpu as pltpu
from jax.sharding import PartitionSpec as P

D = 256
INNER = 512
STATE = 16
RANK = 16
KERNEL = 4
SLOTS = 4
STEP_COUNT = 10
PARAMS = 438016
MATRIX_END = 425984
BETA_ONE = 0.9
BETA_TWO = 0.95
ADAM_EPSILON = 1e-08
RATE_MATRIX = 0.1
RATE_VECTOR = 0.5
WEIGHT_DECAY = 0.1
NORM_EPSILON = 1e-05
LOG2E = 1.4426950408889634
LN2 = 0.6931471805599453
CHUNK = 128
GROUP = 16
SLAB = 512
REACH = 256
BLOCK = 32
LANES = 128
WIDE = GROUP * STATE
BF = jnp.bfloat16
F32 = jnp.float32
NT = (((1,), (1,)), ((), ()))
TN = (((0,), (0,)), ((), ()))


def split_low(value):
    high = value.astype(BF)
    return high, (value - high.astype(F32)).astype(BF)


def dot(a, b, dims=None):
    if dims is None:
        return jnp.dot(a, b, preferred_element_type=F32)
    return lax.dot_general(a, b, dims, preferred_element_type=F32)


def row_sum(value):
    return jnp.sum(value.reshape(value.shape[0] // 8, 8, value.shape[1]), axis=0)


def span(start, count, step=None):
    return pl.ds(pl.multiple_of(start, step or count), count)


def iota(shape, axis):
    return lax.broadcasted_iota(jnp.int32, shape, axis)


def spread(value, index):
    return jnp.broadcast_to(value[index : index + 1, :], (8, LANES))


def each(count, body):
    lax.fori_loop(0, count, lambda i, c: (body(i), c)[1], 0)


def layer_kernel(
    core_ref,
    x_kept_ref,
    x_got_ref,
    up_kept_ref,
    up_got_ref,
    perm_ref,
    w_in_ref,
    w_out_ref,
    wx_ref,
    wdt_ref,
    vec_ref,
    rate_ref,
    gain_ref,
    out_kept_ref,
    out_given_ref,
    gin_kept_ref,
    gin_given_ref,
    gwin_out,
    gwout_out,
    gsmall_out,
    gvec_out,
    ggain_out,
    states,
    act_s,
    slope_s,
    delta_s,
    ratio_s,
    dscan_s,
    u_s,
    y_s,
    gsilu_s,
    gslope_s,
    inner_s,
    dread_s,
    projt_s,
    dproj_s,
    gated_s,
    copy_s,
    dmix_s,
    x_s,
    up_s,
    dnorm_s,
    wide_s,
    read_s,
    entry_s,
    w_in_s,
    w_out_s,
    flip_s,
    tile_s,
    fold_s,
    sums_s,
    mask_s,
    near_s,
    wx_s,
    wdt_s,
    gwin_ref,
    gwout_ref,
    gsmall_ref,
    gvec_ref,
    ggain_ref,
):
    window = pl.program_id(0)
    natural = pl.program_id(1)
    core = core_ref[0]
    length = x_s.shape[0]
    half = length // 2
    chunks = length // CHUNK
    slabs = length // SLAB
    groups = REACH // GROUP
    pieces = range(0, SLAB, BLOCK)

    @pl.when((window == 0) & (natural == 0))
    def _():
        gwin_ref[...] = jnp.zeros_like(gwin_ref)
        gwout_ref[...] = jnp.zeros_like(gwout_ref)
        gsmall_ref[...] = jnp.zeros_like(gsmall_ref)
        gvec_ref[...] = jnp.zeros_like(gvec_ref)
        ggain_ref[...] = jnp.zeros_like(ggain_ref)
        wx_s[...] = jnp.zeros_like(wx_s)
        wx_s[:, : 3 * STATE] = wx_ref[...]
        wdt_s[...] = jnp.zeros_like(wdt_s)
        wdt_s[:RANK, :] = wdt_ref[...]
        inner_s[0:16, :] = jnp.zeros((16, INNER), BF)
        gsilu_s[length : length + 8, :] = jnp.zeros((8, INNER), F32)
        rows, lanes = iota((CHUNK, CHUNK), 0), iota((CHUNK, CHUNK), 1)
        flip_s[1] = jnp.where(rows == lanes, 1.0, 0.0).astype(BF)
        flip_s[0] = jnp.where(rows + lanes == CHUNK - 1, 1.0, 0.0).astype(BF)
        rows, lanes = iota((LANES, WIDE), 0), iota((LANES, WIDE), 1)
        for k in range(2):
            tile_s[k] = jnp.where(rows == STATE * (k + 1) + lanes % STATE, 1.0, 0.0).astype(BF)
        rows, lanes = iota((WIDE, LANES), 0), iota((WIDE, LANES), 1)
        for k in range(2):
            fold_s[k] = jnp.where(lanes == STATE * (k + 1) + rows % STATE, 1.0, 0.0).astype(BF)
        rows, lanes = iota((GROUP, WIDE), 0), iota((GROUP, WIDE), 1)
        mask_s[0] = jnp.where(GROUP - 1 - rows == lanes // STATE, 1.0, 0.0)
        mask_s[1] = jnp.where(rows == lanes // STATE, 1.0, 0.0)
        sums_s[:GROUP, :] = mask_s[0].astype(BF)
        sums_s[GROUP:, :] = jnp.where(rows == lanes % STATE, 1.0, 0.0).astype(BF)

    @pl.when(natural == 0)
    def _():
        kept, got = span(core * half, half), span((1 - core) * half, half)
        x_s[kept, :] = x_kept_ref[0]
        x_s[got, :] = x_got_ref[0]
        up_s[kept, :] = up_kept_ref[0]
        up_s[got, :] = up_got_ref[0]
        w_in_s[...] = dot(perm_ref[...], w_in_ref[...], TN).astype(BF)
        w_out_s[...] = dot(w_out_ref[...], perm_ref[...]).astype(BF)

    @pl.when(natural == 1)
    def _():
        w_in_s[...] = w_in_ref[...]
        w_out_s[...] = w_out_ref[...]

    def place_of(chunk):
        return jnp.where(natural == 1, chunk, chunks - 1 - chunk) * CHUNK

    def norm_parts(rows):
        xf = x_s[rows, :].astype(F32)
        inv = lax.rsqrt(jnp.mean(xf * xf, axis=-1, keepdims=True) + NORM_EPSILON)
        return xf, inv

    def load_copies(slab):
        rows = span(slab * SLAB, SLAB)
        xf, inv = norm_parts(rows)
        normed = (xf * inv * gain_ref[...]).astype(BF)
        upstream = up_s[rows, :]
        for k in range(SLAB // CHUNK):
            part = slice(k * CHUNK, (k + 1) * CHUNK)
            there = span(place_of(slab * (SLAB // CHUNK) + k), CHUNK)
            copy_s[there, :] = dot(flip_s[natural], normed[part]).astype(BF)
            dmix_s[there, :] = dot(flip_s[natural], upstream[part]).astype(BF)

    each(slabs, load_copies)

    def project(slab):
        row = slab * SLAB
        copy = copy_s[span(row, SLAB), :]
        inner_s[span(row + 16, SLAB, 16), :] = dot(copy, w_in_s[:, :INNER]).astype(BF)
        gate_all = dot(copy, w_in_s[:, INNER:]).astype(BF)
        dgated_all = dot(dmix_s[span(row, SLAB), :], w_out_s[...], NT).astype(BF)
        for a in pieces:
            rows = span(row + a, BLOCK)
            gate = gate_all[a : a + BLOCK].astype(F32)
            dgated = dgated_all[a : a + BLOCK].astype(F32)
            sig = 1.0 / (1.0 + jnp.exp(-gate))
            silu = gate * sig
            gsilu_s[rows, :] = silu
            dscan_s[rows, :] = dgated * silu
            gslope_s[rows, :] = dgated * (sig + silu * (1.0 - sig))

    each(slabs, project)

    def convolve(slab):
        row = slab * SLAB
        near_s[...] = inner_s[span(row, SLAB + 16, 16), :].astype(F32)
        for a in pieces:
            rows = span(row + a, BLOCK)
            conv = vec_ref[4:5, :]
            for j in range(KERNEL):
                conv = conv + vec_ref[j : j + 1, :] * near_s[a + 13 + j : a + 13 + j + BLOCK, :]
            sig = 1.0 / (1.0 + jnp.exp(-conv))
            act = conv * sig
            act_s[rows, :] = act
            slope_s[rows, :] = sig + act * (1.0 - sig)
        act_high, act_low = split_low(act_s[span(row, SLAB), :])
        proj = dot(act_high, wx_s[...]) + dot(act_low, wx_s[...])
        for k in range(SLAB // CHUNK):
            turned = jnp.transpose(proj[k * CHUNK : (k + 1) * CHUNK])
            projt_s[slab * (SLAB // CHUNK) + k] = turned[: 3 * STATE]
        proj_high, proj_low = split_low(proj)
        for kind, target in ((0, entry_s), (1, read_s)):
            wide = dot(proj_high, tile_s[kind])
            for g in range(SLAB // GROUP):
                part = wide[g * GROUP : (g + 1) * GROUP] * mask_s[kind]
                target[span(row + g * GROUP, GROUP), :] = part.astype(BF)
        pre_all = dot(proj_high, wdt_s[...]) + dot(proj_low, wdt_s[...])
        for a in pieces:
            rows = span(row + a, BLOCK)
            pre = pre_all[a : a + BLOCK] + vec_ref[5:6, :]
            small = jnp.exp(-jnp.abs(pre))
            whole = 1.0 + small
            share = 1.0 / whole
            log_part = jnp.log(whole) + (small - (whole - 1.0)) * share
            delta = jnp.maximum(pre, 0.0) + log_part
            scaled = jnp.where(pre >= 0.0, share, small * share) / delta
            delta_s[rows, :] = delta
            ratio_s[rows, :] = jnp.where(delta > 1e-30, scaled, 1.0)
            u_s[rows, :] = delta * act_s[rows, :]

    each(slabs, convolve)

    zero = jnp.zeros((8, LANES), F32)
    ones = jnp.ones((GROUP, LANES), BF)
    lane_sets = [slice(LANES * e, LANES * (e + 1)) for e in range(4)]

    def pack(top, bottom):
        return jnp.concatenate([top, bottom], axis=0).astype(BF)

    def turned_of(index):
        each_chunk = REACH // CHUNK
        return [projt_s[index * each_chunk + k] for k in range(each_chunk)]

    def scan_chunk(index, carry):
        state = [list(carry[0:4]), list(carry[4:8])]
        last = list(carry[8:])
        turned = turned_of(index)
        for g in range(groups):
            base = index * REACH + g * GROUP
            columns = turned[g * GROUP // CHUNK]
            rows = span(base, GROUP)
            steps = delta_s[rows, :]
            feeds = u_s[rows, :]
            pulls = dscan_s[rows, :]
            held, sums = [], []
            for t in range(GROUP):
                at = (g * GROUP + t) % CHUNK
                entry = [
                    jnp.broadcast_to(
                        columns[STATE + 8 * h : STATE + 8 * h + 8, at : at + 1], (8, LANES)
                    )
                    for h in range(2)
                ]
                place = span((base + t) * STATE, STATE)
                total = [None, None]
                for e, lanes in enumerate(lane_sets):
                    step = spread(steps[:, lanes], t)
                    feed = spread(feeds[:, lanes], t)
                    pull = spread(pulls[:, lanes], t)
                    for h in range(2):
                        decay = jnp.exp2(step * rate_ref[8 * h : 8 * h + 8, lanes])
                        state[h][e] = decay * state[h][e] + feed * entry[h]
                        part = pull * state[h][e]
                        total[h] = part if e == 0 else total[h] + part
                    states[place, lanes] = last[e]
                    last[e] = pack(state[0][e], state[1][e])
                held.append(jnp.concatenate(last, axis=1))
                sums.append(pack(*total))
            y_s[rows, :] = dot(read_s[rows, :], jnp.concatenate(held, axis=0))
            found = dot(ones, jnp.concatenate(sums, axis=0), NT)
            wide_s[rows, :] = (found * mask_s[1]).astype(BF)
        return tuple(state[0] + state[1] + last)

    lax.fori_loop(0, length // REACH, scan_chunk, (zero,) * 8 + (pack(zero, zero),) * 4)

    def finish(slab):
        row = slab * SLAB
        dread_s[span(row, SLAB), :] = dot(wide_s[span(row, SLAB), :], fold_s[1]).astype(BF)
        for a in pieces:
            rows = span(row + a, BLOCK)
            scanned = y_s[rows, :] + vec_ref[6:7, :] * act_s[rows, :]
            gated_s[rows, :] = (scanned * gsilu_s[rows, :]).astype(BF)
            dproj_s[rows, INNER:] = (scanned * gslope_s[rows, :]).astype(BF)

    each(slabs, finish)

    def store_half(kept_ref, given_ref, which, rows, value):
        @pl.when(which == core)
        def _():
            kept_ref[0, rows, :] = value

        @pl.when(which != core)
        def _():
            given_ref[0, rows, :] = value

    def mirror_mixed(slab):
        mixed_all = dot(gated_s[span(slab * SLAB, SLAB), :], w_out_s[...])
        for k in range(SLAB // CHUNK):
            high, low = split_low(mixed_all[k * CHUNK : (k + 1) * CHUNK])
            place = place_of(slab * (SLAB // CHUNK) + k)
            mixed = dot(flip_s[0], high) + dot(flip_s[0], low)
            store_half(gin_kept_ref, gin_given_ref, place // half, span(place % half, CHUNK), mixed)

    def natural_mixed(slab):
        rows = span(slab * SLAB, SLAB)
        mixed = dot(gated_s[rows, :], w_out_s[...])
        total = x_s[rows, :].astype(F32) + mixed

        @pl.when(slab == core)
        def _():
            out_kept_ref[0] = (total + gin_kept_ref[0]).astype(BF)

        @pl.when(slab != core)
        def _():
            out_given_ref[0] = (total + gin_given_ref[0]).astype(BF)

    @pl.when(natural == 0)
    def _():
        each(slabs, mirror_mixed)
        dmix_s[...] = dot(dmix_s[...], perm_ref[...], NT).astype(BF)

    @pl.when(natural == 1)
    def _():
        each(slabs, natural_mixed)

    gwout_ref[...] += dot(gated_s[...], dmix_s[...], TN)

    def back_chunk(step_index, carry_all):
        index = length // REACH - 1 - step_index
        carry = [list(carry_all[0:4]), list(carry_all[4:8])]
        rate_sum = carry_all[8]
        turned = turned_of(index)
        for g in reversed(range(groups)):
            base = index * REACH + g * GROUP
            columns = turned[g * GROUP // CHUNK]
            rows = span(base, GROUP)
            steps = delta_s[rows, :]
            feeds = dscan_s[rows, :]
            pulls = u_s[rows, :]
            held, prods, sums = [], [], []
            for t in reversed(range(GROUP)):
                at = (g * GROUP + t) % CHUNK
                read = [
                    jnp.broadcast_to(
                        columns[2 * STATE + 8 * h : 2 * STATE + 8 * h + 8, at : at + 1], (8, LANES)
                    )
                    for h in range(2)
                ]
                place = span((base + t) * STATE, STATE)
                held_row, prod_row = [], []
                total = [None, None]
                for e, lanes in enumerate(lane_sets):
                    step = spread(steps[:, lanes], t)
                    feed = spread(feeds[:, lanes], t)
                    pull = spread(pulls[:, lanes], t)
                    before = states[place, lanes]
                    lams, both = [], []
                    for h in range(2):
                        power = step * rate_ref[8 * h : 8 * h + 8, lanes]
                        lam = feed * read[h] + carry[h][e]
                        carry[h][e] = jnp.exp2(power) * lam
                        lams.append(lam)
                        part = pull * lam
                        total[h] = part if e == 0 else total[h] + part
                        both.append(power * carry[h][e])
                    held_row.append(pack(*lams))
                    prod_row.append(pack(*both) * before)
                held.append(jnp.concatenate(held_row, axis=1))
                prods.append(jnp.concatenate(prod_row, axis=1))
                sums.append(pack(*total))
            y_s[rows, :] = dot(entry_s[rows, :], jnp.concatenate(held, axis=0))
            both = dot(sums_s[...], jnp.concatenate(prods, axis=0))
            gslope_s[rows, :] = both[:GROUP]
            rate_sum = rate_sum + both[GROUP:]
            found = dot(ones, jnp.concatenate(sums, axis=0), NT)
            wide_s[rows, :] = (found * mask_s[0]).astype(BF)
        return tuple(carry[0] + carry[1]) + (rate_sum,)

    done = lax.fori_loop(
        0, length // REACH, back_chunk, (zero,) * 8 + (jnp.zeros((STATE, INNER), F32),)
    )
    gsmall_ref[0:STATE, :] += done[8] * LN2

    def gradients(slab):
        row = slab * SLAB
        sum_pre = sum_skip = None
        for a in pieces:
            rows = span(row + a, BLOCK)
            dfeed = y_s[rows, :]
            dpre = ratio_s[rows, :] * (gslope_s[rows, :] * LN2 + dfeed * u_s[rows, :])
            gsilu_s[rows, :] = dpre
            dscan = dscan_s[rows, :]
            y_s[rows, :] = dscan * vec_ref[6:7, :] + dfeed * delta_s[rows, :]
            one, two = row_sum(dpre), row_sum(dscan * act_s[rows, :])
            sum_pre = one if sum_pre is None else sum_pre + one
            sum_skip = two if sum_skip is None else sum_skip + two
        gvec_ref[5] += sum_pre
        gvec_ref[6] += sum_skip
        dpre_all = gsilu_s[span(row, SLAB), :].astype(BF)
        dproj = (
            dot(dpre_all, wdt_s[...], NT)
            + dot(wide_s[span(row, SLAB), :], fold_s[0])
            + dread_s[span(row, SLAB), :].astype(F32)
        )
        extra = dot(dproj.astype(BF), wx_s[...], NT)
        low_sum = None
        for k in range(SLAB // CHUNK):
            low = projt_s[slab * (SLAB // CHUNK) + k][:RANK].astype(BF)
            part = dot(low, dpre_all[k * CHUNK : (k + 1) * CHUNK])
            low_sum = part if low_sum is None else low_sum + part
        gsmall_ref[STATE : 2 * STATE, :] += low_sum
        gsmall_ref[2 * STATE : 5 * STATE, :] += dot(
            dproj.astype(BF), act_s[span(row, SLAB), :].astype(BF), TN
        )[: 3 * STATE]
        for a in pieces:
            rows = span(row + a, BLOCK)
            gsilu_s[rows, :] = (y_s[rows, :] + extra[a : a + BLOCK]) * slope_s[rows, :]

    each(slabs, gradients)

    def unconvolve(slab):
        row = slab * SLAB
        totals = [None] * 5
        near_s[: SLAB + 8, :] = gsilu_s[span(row, SLAB + 8, 8), :]
        for a in pieces:
            rows = span(row + a, BLOCK)
            inner = inner_s[span(row + a + 16, BLOCK, 16), :].astype(F32)
            dinner = None
            for j in range(KERNEL):
                moved = near_s[a + 3 - j : a + 3 - j + BLOCK, :]
                term = vec_ref[j : j + 1, :] * moved
                dinner = term if dinner is None else dinner + term
                part = row_sum(moved * inner)
                totals[j] = part if totals[j] is None else totals[j] + part
            part = row_sum(near_s[a : a + BLOCK, :])
            totals[4] = part if totals[4] is None else totals[4] + part
            dproj_s[rows, :INNER] = dinner.astype(BF)
        for j in range(5):
            gvec_ref[j] += totals[j]

    each(slabs, unconvolve)

    def mirror_dnorm(slab):
        dnorm_all = dot(dproj_s[span(slab * SLAB, SLAB), :], w_in_s[...], NT)
        for k in range(SLAB // CHUNK):
            high, low = split_low(dnorm_all[k * CHUNK : (k + 1) * CHUNK])
            there = span(place_of(slab * (SLAB // CHUNK) + k), CHUNK)
            dnorm_s[there, :] = dot(flip_s[0], high) + dot(flip_s[0], low)

    def natural_dnorm(slab):
        rows = span(slab * SLAB, SLAB)
        total = dot(dproj_s[rows, :], w_in_s[...], NT) + dnorm_s[rows, :]
        xf, inv = norm_parts(rows)
        scaled = total * gain_ref[...]
        hat = xf * inv
        ggain_ref[...] += row_sum(total * hat)
        mean = jnp.mean(scaled * hat, axis=-1, keepdims=True)
        result = up_s[rows, :].astype(F32) + inv * (scaled - hat * mean)
        store_half(gin_kept_ref, gin_given_ref, slab, slice(None), result)

    @pl.when(natural == 0)
    def _():
        each(slabs, mirror_dnorm)
        copy_s[...] = dot(copy_s[...], perm_ref[...], NT).astype(BF)

    @pl.when(natural == 1)
    def _():
        each(slabs, natural_dnorm)

    gwin_ref[...] += dot(copy_s[...], dproj_s[...], TN)

    @pl.when((window == pl.num_programs(0) - 1) & (natural == 1))
    def _():
        gwin_out[...] = gwin_ref[...].astype(BF)
        gwout_out[...] = gwout_ref[...].astype(BF)
        gsmall_out[...] = gsmall_ref[...].astype(BF)
        vectors = [jnp.sum(gvec_ref[j], axis=0, keepdims=True) for j in range(7)]
        vectors.append(jnp.zeros((9, INNER), F32))
        gvec_out[...] = jnp.concatenate(vectors, axis=0).astype(BF)
        gain = jnp.sum(ggain_ref[...], axis=0, keepdims=True)
        ggain_out[...] = jnp.broadcast_to(gain, (16, D)).astype(BF)


def run_layer(
    core, x, x_got, up, up_got, perm, w_in, w_x, w_dt, w_out, conv_w, conv_b, dt_bias, a_log, d_skip, gain
):
    windows, half, _ = x_got.shape
    length = 2 * half
    vec = jnp.concatenate(
        [conv_w.T, conv_b[None], dt_bias[None], d_skip[None], jnp.zeros((1, INNER), F32)], axis=0
    )
    rate = (-LOG2E) * jnp.exp(a_log).T

    def whole(shape):
        return pl.BlockSpec(shape, lambda w, q, core: (0,) * len(shape))

    kept = pl.BlockSpec((1, half, D), lambda w, q, core: (windows * core[0] + w, 0, 0))
    got = pl.BlockSpec((1, half, D), lambda w, q, core: (w, 0, 0))
    fixed = (perm, w_in, w_out, w_x, w_dt, vec, rate, gain[None])
    grads = [
        jax.ShapeDtypeStruct((D, 2 * INNER), BF),
        jax.ShapeDtypeStruct((INNER, D), BF),
        jax.ShapeDtypeStruct((5 * STATE, INNER), BF),
        jax.ShapeDtypeStruct((16, INNER), BF),
        jax.ShapeDtypeStruct((16, D), BF),
    ]
    inner_f32 = [pltpu.VMEM((length, INNER), F32)]
    outer_bf = [pltpu.VMEM((length, D), BF)]
    outer_f32 = [pltpu.VMEM((length, D), F32)]
    halo_f32 = [pltpu.VMEM((length + 8, INNER), F32)]
    scratch = (
        [pltpu.VMEM((length * STATE, INNER), BF)]
        + inner_f32 * 7
        + halo_f32
        + inner_f32
        + [pltpu.VMEM((length + 16, INNER), BF)]
        + [pltpu.VMEM((length, LANES), BF)]
        + [
            pltpu.VMEM((length // CHUNK, 3 * STATE, CHUNK), F32),
            pltpu.VMEM((length, 2 * INNER), BF),
            pltpu.VMEM((length, INNER), BF),
        ]
        + outer_bf * 4
        + outer_f32
        + [pltpu.VMEM((length, WIDE), BF)] * 3
        + [
            pltpu.VMEM((D, 2 * INNER), BF),
            pltpu.VMEM((INNER, D), BF),
            pltpu.VMEM((2, CHUNK, CHUNK), BF),
            pltpu.VMEM((2, LANES, WIDE), BF),
            pltpu.VMEM((2, WIDE, LANES), BF),
            pltpu.VMEM((2 * GROUP, WIDE), BF),
            pltpu.VMEM((2, GROUP, WIDE), F32),
            pltpu.VMEM((SLAB + 16, INNER), F32),
            pltpu.VMEM((INNER, LANES), BF),
            pltpu.VMEM((LANES, INNER), BF),
            pltpu.VMEM((D, 2 * INNER), F32),
            pltpu.VMEM((INNER, D), F32),
            pltpu.VMEM((5 * STATE, INNER), F32),
            pltpu.VMEM((7, 8, INNER), F32),
            pltpu.VMEM((8, D), F32),
        ]
    )
    return pl.pallas_call(
        layer_kernel,
        grid_spec=pltpu.PrefetchScalarGridSpec(
            num_scalar_prefetch=1,
            grid=(windows, 2),
            in_specs=[kept, got, kept, got] + [whole(item.shape) for item in fixed],
            out_specs=[got] * 4 + [whole(item.shape) for item in grads],
            scratch_shapes=scratch,
        ),
        out_shape=[
            jax.ShapeDtypeStruct((windows, half, D), kind) for kind in (BF, BF, F32, F32)
        ]
        + grads,
        compiler_params=pltpu.CompilerParams(vmem_limit_bytes=64 * 2**20 - 65536),
    )(core.reshape(1).astype(jnp.int32), x, x_got, up, up_got, *fixed)


def layer_grads(results):
    gwin, gwout, gsmall, gvec, ggain = results
    return [
        gwin,
        gsmall[2 * STATE :].T,
        gsmall[STATE : 2 * STATE],
        gwout,
        gvec[:KERNEL].T,
        gvec[4],
        gvec[5],
        gsmall[:STATE].T,
        gvec[6],
        ggain[0],
    ]


def param_shapes():
    return [
        (D, 2 * INNER),
        (INNER, RANK + 2 * STATE),
        (RANK, INNER),
        (INNER, D),
        (INNER, KERNEL),
        (INNER,),
        (INNER,),
        (INNER, STATE),
        (INNER,),
        (D,),
    ]


def bounds():
    edges = [0]
    for shape in param_shapes():
        edges.append(edges[-1] + math.prod(shape))
    return edges


def slot_index(owners):
    count = owners.shape[0]
    order = jnp.arange(count, dtype=jnp.int32)
    same = (owners[None, :] == owners[:, None]) & (order[None, :] < order[:, None])
    return jnp.sum(same.astype(jnp.int32), axis=1)


def swap(value, axis, bit):
    size = lax.axis_size(axis)
    return lax.ppermute(value, axis, [(i, i ^ bit) for i in range(size)])


def up_to(value, multiple):
    return -(-value // multiple) * multiple


def pad_rows(value, rows, axis):
    widths = [(0, 0)] * value.ndim
    widths[axis] = (0, rows - value.shape[axis])
    return jnp.pad(value, widths)


def gather_params(weights, owners, rank, matches):
    size = lax.axis_size("dp")
    me = lax.axis_index("dp")
    core = lax.axis_index("seq")
    blocks, block_len = owners.shape[0], weights.shape[1]
    rows = block_len // LANES
    padded = up_to(rows, 16)
    near = min(4, size)
    tiles = weights.reshape(SLOTS, rows, LANES)
    rounded = lax.reduce_precision(tiles, 8, 7)
    pair = SLOTS // 2
    mine = lax.dynamic_slice_in_dim(rounded, core * pair, pair, 0).astype(BF)
    many = pad_rows(mine, padded, 1).reshape(pair * padded, LANES)
    first = MATRIX_END // block_len
    last = (PARAMS - 1) // block_len + 1
    here = matches[:, first:last].T[:, :, None, None]
    fine = jnp.sum(jnp.where(here, (tiles - rounded)[None], 0.0), axis=1).astype(BF)
    fine_rows = (last - first) * rows
    fine_half = up_to(fine_rows, 32) // 2
    fine = pad_rows(fine.reshape(fine_rows, LANES), 2 * fine_half, 0)
    fine = lax.dynamic_slice_in_dim(fine, core * fine_half, fine_half, 0)
    away = owners ^ me
    spot = jnp.zeros_like(owners)
    bit, step = size // 2, 0
    while bit >= near:
        got = swap(jnp.concatenate([many, fine], axis=0), "dp", bit)
        count = many.shape[0]
        many = jnp.concatenate([many, got[:count]], axis=0)
        fine = fine + got[count:]
        spot = spot + jnp.where((away & bit) != 0, 1 << step, 0)
        bit, step = bit // 2, step + 1
    count = many.shape[0]
    sent = jnp.concatenate([many, fine], axis=0)
    others = [swap(sent, "dp", k) for k in range(1, near)]
    many = jnp.stack([many] + [item[:count] for item in others])
    for item in others:
        fine = fine + item[count:]
    spot = (spot + (away & (near - 1)) * (size // near)) * pair + rank % pair
    chosen = many.reshape(size * pair, padded, LANES)[spot]
    theirs = swap(chosen, "seq", 1)
    fine_got = swap(fine, "seq", 1)
    local = (rank // pair == core)[:, None, None]
    theta = jnp.where(local, chosen, theirs)[:, :rows].reshape(blocks * rows, LANES)
    fine = jnp.concatenate(
        [jnp.where(core == 0, fine, fine_got), jnp.where(core == 0, fine_got, fine)], axis=0
    )
    begin = (MATRIX_END - first * block_len) // LANES
    fine = fine[begin : begin + (PARAMS - MATRIX_END) // LANES]
    return lax.optimization_barrier((theta, fine))


def scatter_sum(value, size, beside):
    me = lax.axis_index("dp")
    stride = 1
    total = value
    while stride < size:
        radix = min(4, size // stride)
        total = total.reshape((size // (stride * radix), radix) + value.shape[1:])
        digit = (me // stride) % radix
        low = total.astype(BF)
        kept = lax.dynamic_index_in_dim(total, digit, 1, keepdims=False).astype(F32)
        for k in range(1, radix):
            given = lax.dynamic_index_in_dim(low, digit ^ k, 1, keepdims=False)
            kept = kept + swap(given, "dp", k * stride).astype(F32)
        total = kept
        if stride == 1:
            total, beside = lax.optimization_barrier((total, beside))
        stride *= radix
    return total[0], beside


def other_half(value, core):
    count = value.shape[0] // 2
    return swap(lax.dynamic_slice_in_dim(value, (1 - core) * count, count, 0), "seq", 1)


def by_position(kept, given, core):
    got = swap(given, "seq", 1)
    return jnp.concatenate(
        [jnp.where(core == 0, kept, got), jnp.where(core == 0, got, kept)], axis=0
    )


def on_device(
    inputs, cotangent, loss_mask, complement_map, owners, weights, first_moment, second_moment
):
    size = lax.axis_size("dp")
    me = lax.axis_index("dp")
    core = lax.axis_index("seq")
    blocks, block_len = owners.shape[0], weights.shape[1]
    rows = block_len // LANES
    pair = SLOTS // 2
    rank = slot_index(owners)
    order = jnp.arange(blocks, dtype=jnp.int32)
    matches = (owners[None, :] == me) & (
        rank[None, :] == jnp.arange(SLOTS, dtype=jnp.int32)[:, None]
    )
    occupied = jnp.any(matches, axis=1)
    block_of = jnp.sum(jnp.where(matches, order[None, :], 0), axis=1)
    theta, fine = gather_params(weights, owners, rank, matches)
    upstream = cotangent * loss_mask.astype(BF)[..., None]
    x_got = other_half(inputs, core)
    up_got = other_half(upstream, core)

    edges = [edge // LANES for edge in bounds()]
    shapes = param_shapes()
    tail = edges[4]

    def high_of(index):
        return theta[edges[index] : edges[index + 1]].reshape(shapes[index])

    def full_of(index):
        part = theta[edges[index] : edges[index + 1]].astype(F32)
        part = part + fine[edges[index] - tail : edges[index + 1] - tail].astype(F32)
        return part.reshape(shapes[index])

    perm = (complement_map[:, None] == jnp.arange(D, dtype=jnp.int32)[None, :]).astype(BF)
    results = run_layer(
        core,
        inputs,
        x_got,
        upstream,
        up_got,
        perm,
        *[high_of(index) for index in range(4)],
        *[full_of(index) for index in range(4, 10)],
    )
    pieces = layer_grads(results[4:])
    padded = up_to(rows, 16)
    spare = jnp.zeros(((blocks + 1) * rows - PARAMS // LANES, LANES), BF)
    tiles = [item.astype(BF).reshape(-1, LANES) for item in pieces] + [spare]
    grad_blocks = jnp.concatenate(tiles, axis=0).reshape(blocks + 1, rows, LANES)
    grad_blocks = pad_rows(grad_blocks, padded, 1)
    source = jnp.full((size * SLOTS,), blocks, jnp.int32).at[owners * SLOTS + rank].set(order)
    source = source.reshape(size, 2, pair)

    def for_core(which):
        index = lax.dynamic_index_in_dim(source, which, 1, keepdims=False)
        return grad_blocks[index.reshape(-1)].reshape(size * pair * padded, LANES)

    got = swap(for_core(1 - core), "seq", 1)
    chip = (for_core(core).astype(F32) + got.astype(F32)).astype(BF)
    chip = chip.reshape(size, pair * padded, LANES)
    output = by_position(results[0], results[1], core)
    grad_input = by_position(results[2], results[3], core)
    summed, grad_input = scatter_sum(chip, size, grad_input)
    summed = summed.reshape(pair, -1, LANES)[:, :rows]
    other = swap(summed, "seq", 1)
    owned = jnp.concatenate(
        [jnp.where(core == 0, summed, other), jnp.where(core == 0, other, summed)], axis=0
    ).reshape(SLOTS, block_len)
    new_first = BETA_ONE * first_moment + (1.0 - BETA_ONE) * owned
    new_second = BETA_TWO * second_moment + (1.0 - BETA_TWO) * owned * owned
    position = block_of[:, None] * block_len + jnp.arange(block_len, dtype=jnp.int32)[None, :]
    is_matrix = position < MATRIX_END
    rate = jnp.where(is_matrix, RATE_MATRIX, RATE_VECTOR)
    decay = jnp.where(is_matrix, WEIGHT_DECAY, 0.0)
    corrected = (
        new_first
        / (1.0 - BETA_ONE**STEP_COUNT)
        / (jnp.sqrt(new_second / (1.0 - BETA_TWO**STEP_COUNT)) + ADAM_EPSILON)
    )
    new_theta = weights - rate * (corrected + decay * weights)
    keep = occupied[:, None]
    return (
        output,
        grad_input,
        jnp.where(keep, new_theta, 0.0),
        jnp.where(keep, new_first, 0.0),
        jnp.where(keep, new_second, 0.0),
    )


def solution(mesh):
    in_specs = (
        P("dp", "seq", None),
        P("dp", "seq", None),
        P("dp", "seq"),
        P(),
        P(),
        P("dp", None),
        P("dp", None),
        P("dp", None),
    )
    out_specs = (
        P("dp", "seq", None),
        P("dp", "seq", None),
        P("dp", None),
        P("dp", None),
        P("dp", None),
    )
    return jax.shard_map(
        on_device, mesh=mesh, in_specs=in_specs, out_specs=out_specs, check_vma=False
    )
```

```python
import functools
import math

import jax
import jax.numpy as jnp
from jax import lax
from jax.experimental import pallas as pl
from jax.experimental.pallas import tpu as pltpu
from jax.sharding import PartitionSpec as P

D = 256
INNER = 512
STATE = 16
RANK = 16
KERNEL = 4
SLOTS = 4
STEP_COUNT = 10
PARAMS = 438016
MATRIX_END = 425984
BETA_ONE = 0.9
BETA_TWO = 0.95
ADAM_EPSILON = 1e-08
RATE_MATRIX = 0.1
RATE_VECTOR = 0.5
WEIGHT_DECAY = 0.1
NORM_EPSILON = 1e-05
LOG2E = 1.4426950408889634
LN2 = 0.6931471805599453
CHUNK = 128
GROUP = 16
SLAB = 512
REACH = 256
BLOCK = 32
LANES = 128
WIDE = GROUP * STATE
BF = jnp.bfloat16
F32 = jnp.float32
NT = (((1,), (1,)), ((), ()))
TN = (((0,), (0,)), ((), ()))


def split_low(value):
    high = value.astype(BF)
    return high, (value - high.astype(F32)).astype(BF)


def dot(a, b, dims=None):
    if dims is None:
        return jnp.dot(a, b, preferred_element_type=F32)
    return lax.dot_general(a, b, dims, preferred_element_type=F32)


def row_sum(value):
    return jnp.sum(value.reshape(value.shape[0] // 8, 8, value.shape[1]), axis=0)


def span(start, count, step=None):
    return pl.ds(pl.multiple_of(start, step or count), count)


def iota(shape, axis):
    return lax.broadcasted_iota(jnp.int32, shape, axis)


def spread(value, index):
    return jnp.broadcast_to(value[index : index + 1, :], (8, LANES))


def each(count, body):
    lax.fori_loop(0, count, lambda i, c: (body(i), c)[1], 0)


def layer_kernel(
    core_ref,
    x_kept_ref,
    x_got_ref,
    up_kept_ref,
    up_got_ref,
    perm_ref,
    w_in_ref,
    w_out_ref,
    wx_ref,
    wdt_ref,
    vec_ref,
    rate_ref,
    gain_ref,
    out_kept_ref,
    out_given_ref,
    gin_kept_ref,
    gin_given_ref,
    gwin_out,
    gwout_out,
    gsmall_out,
    gvec_out,
    states,
    act_s,
    slope_s,
    delta_s,
    ratio_s,
    dscan_s,
    u_s,
    y_s,
    gsilu_s,
    gslope_s,
    inner_s,
    dread_s,
    projt_s,
    dproj_s,
    gated_s,
    copy_s,
    dmix_s,
    x_s,
    up_s,
    dnorm_s,
    wide_s,
    read_s,
    entry_s,
    w_in_s,
    w_out_s,
    flip_s,
    tile_s,
    fold_s,
    sums_s,
    mask_s,
    near_s,
    wx_s,
    wdt_s,
    gwin_ref,
    gwout_ref,
    gsmall_ref,
    gvec_ref,
    ggain_ref,
):
    window = pl.program_id(0)
    natural = pl.program_id(1)
    core = core_ref[0]
    length = x_s.shape[0]
    half = length // 2
    chunks = length // CHUNK
    slabs = length // SLAB
    groups = REACH // GROUP
    pieces = range(0, SLAB, BLOCK)

    @pl.when((window == 0) & (natural == 0))
    def _():
        gwin_ref[...] = jnp.zeros_like(gwin_ref)
        gwout_ref[...] = jnp.zeros_like(gwout_ref)
        gsmall_ref[...] = jnp.zeros_like(gsmall_ref)
        gvec_ref[...] = jnp.zeros_like(gvec_ref)
        ggain_ref[...] = jnp.zeros_like(ggain_ref)
        wx_s[...] = jnp.zeros_like(wx_s)
        wx_s[:, : 3 * STATE] = wx_ref[...]
        wdt_s[...] = jnp.zeros_like(wdt_s)
        wdt_s[:RANK, :] = wdt_ref[...]
        inner_s[0:16, :] = jnp.zeros((16, INNER), BF)
        gsilu_s[length : length + 8, :] = jnp.zeros((8, INNER), F32)
        rows, lanes = iota((CHUNK, CHUNK), 0), iota((CHUNK, CHUNK), 1)
        flip_s[1] = jnp.where(rows == lanes, 1.0, 0.0).astype(BF)
        flip_s[0] = jnp.where(rows + lanes == CHUNK - 1, 1.0, 0.0).astype(BF)
        rows, lanes = iota((LANES, WIDE), 0), iota((LANES, WIDE), 1)
        for k in range(2):
            tile_s[k] = jnp.where(rows == STATE * (k + 1) + lanes % STATE, 1.0, 0.0).astype(BF)
        rows, lanes = iota((WIDE, LANES), 0), iota((WIDE, LANES), 1)
        for k in range(2):
            fold_s[k] = jnp.where(lanes == STATE * (k + 1) + rows % STATE, 1.0, 0.0).astype(BF)
        rows, lanes = iota((GROUP, WIDE), 0), iota((GROUP, WIDE), 1)
        mask_s[0] = jnp.where(GROUP - 1 - rows == lanes // STATE, 1.0, 0.0)
        mask_s[1] = jnp.where(rows == lanes // STATE, 1.0, 0.0)
        sums_s[:GROUP, :] = mask_s[0].astype(BF)
        sums_s[GROUP:, :] = jnp.where(rows == lanes % STATE, 1.0, 0.0).astype(BF)

    @pl.when(natural == 0)
    def _():
        kept, got = span(core * half, half), span((1 - core) * half, half)
        x_s[kept, :] = x_kept_ref[0]
        x_s[got, :] = x_got_ref[0]
        up_s[kept, :] = up_kept_ref[0]
        up_s[got, :] = up_got_ref[0]
        w_in_s[...] = dot(perm_ref[...], w_in_ref[...], TN).astype(BF)
        w_out_s[...] = dot(w_out_ref[...], perm_ref[...]).astype(BF)

    @pl.when(natural == 1)
    def _():
        w_in_s[...] = w_in_ref[...]
        w_out_s[...] = w_out_ref[...]

    def place_of(chunk):
        return jnp.where(natural == 1, chunk, chunks - 1 - chunk) * CHUNK

    def norm_parts(rows):
        xf = x_s[rows, :].astype(F32)
        inv = lax.rsqrt(jnp.mean(xf * xf, axis=-1, keepdims=True) + NORM_EPSILON)
        return xf, inv

    def load_copies(slab):
        rows = span(slab * SLAB, SLAB)
        xf, inv = norm_parts(rows)
        normed = (xf * inv * gain_ref[...]).astype(BF)
        upstream = up_s[rows, :]
        for k in range(SLAB // CHUNK):
            part = slice(k * CHUNK, (k + 1) * CHUNK)
            there = span(place_of(slab * (SLAB // CHUNK) + k), CHUNK)
            copy_s[there, :] = dot(flip_s[natural], normed[part]).astype(BF)
            dmix_s[there, :] = dot(flip_s[natural], upstream[part]).astype(BF)

    each(slabs, load_copies)

    def project(slab):
        row = slab * SLAB
        copy = copy_s[span(row, SLAB), :]
        inner_s[span(row + 16, SLAB, 16), :] = dot(copy, w_in_s[:, :INNER]).astype(BF)
        gate_all = dot(copy, w_in_s[:, INNER:]).astype(BF)
        dgated_all = dot(dmix_s[span(row, SLAB), :], w_out_s[...], NT).astype(BF)
        for a in pieces:
            rows = span(row + a, BLOCK)
            gate = gate_all[a : a + BLOCK].astype(F32)
            dgated = dgated_all[a : a + BLOCK].astype(F32)
            sig = 1.0 / (1.0 + jnp.exp(-gate))
            silu = gate * sig
            gsilu_s[rows, :] = silu
            dscan_s[rows, :] = dgated * silu
            gslope_s[rows, :] = dgated * (sig + silu * (1.0 - sig))

    each(slabs, project)

    def convolve(slab):
        row = slab * SLAB
        near_s[...] = inner_s[span(row, SLAB + 16, 16), :].astype(F32)
        for a in pieces:
            rows = span(row + a, BLOCK)
            conv = vec_ref[4:5, :]
            for j in range(KERNEL):
                conv = conv + vec_ref[j : j + 1, :] * near_s[a + 13 + j : a + 13 + j + BLOCK, :]
            sig = 1.0 / (1.0 + jnp.exp(-conv))
            act = conv * sig
            act_s[rows, :] = act
            slope_s[rows, :] = sig + act * (1.0 - sig)
        act_high, act_low = split_low(act_s[span(row, SLAB), :])
        proj = dot(act_high, wx_s[...]) + dot(act_low, wx_s[...])
        for k in range(SLAB // CHUNK):
            turned = jnp.transpose(proj[k * CHUNK : (k + 1) * CHUNK])
            projt_s[slab * (SLAB // CHUNK) + k] = turned[: 3 * STATE]
        proj_high, proj_low = split_low(proj)
        for kind, target in ((0, entry_s), (1, read_s)):
            wide = dot(proj_high, tile_s[kind])
            for g in range(SLAB // GROUP):
                part = wide[g * GROUP : (g + 1) * GROUP] * mask_s[kind]
                target[span(row + g * GROUP, GROUP), :] = part.astype(BF)
        pre_all = dot(proj_high, wdt_s[...]) + dot(proj_low, wdt_s[...])
        for a in pieces:
            rows = span(row + a, BLOCK)
            pre = pre_all[a : a + BLOCK] + vec_ref[5:6, :]
            small = jnp.exp(-jnp.abs(pre))
            whole = 1.0 + small
            share = 1.0 / whole
            log_part = jnp.log(whole) + (small - (whole - 1.0)) * share
            delta = jnp.maximum(pre, 0.0) + log_part
            scaled = jnp.where(pre >= 0.0, share, small * share) / delta
            delta_s[rows, :] = delta
            ratio_s[rows, :] = jnp.where(delta > 1e-30, scaled, 1.0)
            u_s[rows, :] = delta * act_s[rows, :]

    each(slabs, convolve)

    zero = jnp.zeros((8, LANES), F32)
    ones = jnp.ones((GROUP, LANES), BF)
    lane_sets = [slice(LANES * e, LANES * (e + 1)) for e in range(4)]

    def pack(top, bottom):
        return jnp.concatenate([top, bottom], axis=0).astype(BF)

    def turned_of(index):
        each_chunk = REACH // CHUNK
        return [projt_s[index * each_chunk + k] for k in range(each_chunk)]

    def scan_chunk(index, carry):
        state = [list(carry[0:4]), list(carry[4:8])]
        last = list(carry[8:])
        turned = turned_of(index)
        for g in range(groups):
            base = index * REACH + g * GROUP
            columns = turned[g * GROUP // CHUNK]
            rows = span(base, GROUP)
            steps = delta_s[rows, :]
            feeds = u_s[rows, :]
            pulls = dscan_s[rows, :]
            held, sums = [], []
            for t in range(GROUP):
                at = (g * GROUP + t) % CHUNK
                entry = [
                    jnp.broadcast_to(
                        columns[STATE + 8 * h : STATE + 8 * h + 8, at : at + 1], (8, LANES)
                    )
                    for h in range(2)
                ]
                place = span((base + t) * STATE, STATE)
                total = [None, None]
                for e, lanes in enumerate(lane_sets):
                    step = spread(steps[:, lanes], t)
                    feed = spread(feeds[:, lanes], t)
                    pull = spread(pulls[:, lanes], t)
                    for h in range(2):
                        decay = jnp.exp2(step * rate_ref[8 * h : 8 * h + 8, lanes])
                        state[h][e] = decay * state[h][e] + feed * entry[h]
                        part = pull * state[h][e]
                        total[h] = part if e == 0 else total[h] + part
                    states[place, lanes] = last[e]
                    last[e] = pack(state[0][e], state[1][e])
                held.append(jnp.concatenate(last, axis=1))
                sums.append(pack(*total))
            y_s[rows, :] = dot(read_s[rows, :], jnp.concatenate(held, axis=0))
            found = dot(ones, jnp.concatenate(sums, axis=0), NT)
            wide_s[rows, :] = (found * mask_s[1]).astype(BF)
        return tuple(state[0] + state[1] + last)

    lax.fori_loop(0, length // REACH, scan_chunk, (zero,) * 8 + (pack(zero, zero),) * 4)

    def finish(slab):
        row = slab * SLAB
        dread_s[span(row, SLAB), :] = dot(wide_s[span(row, SLAB), :], fold_s[1]).astype(BF)
        for a in pieces:
            rows = span(row + a, BLOCK)
            scanned = y_s[rows, :] + vec_ref[6:7, :] * act_s[rows, :]
            gated_s[rows, :] = (scanned * gsilu_s[rows, :]).astype(BF)
            dproj_s[rows, INNER:] = (scanned * gslope_s[rows, :]).astype(BF)

    each(slabs, finish)

    def store_half(kept_ref, given_ref, which, rows, value):
        @pl.when(which == core)
        def _():
            kept_ref[0, rows, :] = value

        @pl.when(which != core)
        def _():
            given_ref[0, rows, :] = value

    def mirror_mixed(slab):
        mixed_all = dot(gated_s[span(slab * SLAB, SLAB), :], w_out_s[...])
        for k in range(SLAB // CHUNK):
            high, low = split_low(mixed_all[k * CHUNK : (k + 1) * CHUNK])
            place = place_of(slab * (SLAB // CHUNK) + k)
            mixed = dot(flip_s[0], high) + dot(flip_s[0], low)
            store_half(gin_kept_ref, gin_given_ref, place // half, span(place % half, CHUNK), mixed)

    def natural_mixed(slab):
        rows = span(slab * SLAB, SLAB)
        mixed = dot(gated_s[rows, :], w_out_s[...])
        total = x_s[rows, :].astype(F32) + mixed

        @pl.when(slab == core)
        def _():
            out_kept_ref[0] = (total + gin_kept_ref[0]).astype(BF)

        @pl.when(slab != core)
        def _():
            out_given_ref[0] = (total + gin_given_ref[0]).astype(BF)

    @pl.when(natural == 0)
    def _():
        each(slabs, mirror_mixed)
        dmix_s[...] = dot(dmix_s[...], perm_ref[...], NT).astype(BF)

    @pl.when(natural == 1)
    def _():
        each(slabs, natural_mixed)

    gwout_ref[...] += dot(gated_s[...], dmix_s[...], TN)

    def back_chunk(step_index, carry_all):
        index = length // REACH - 1 - step_index
        carry = [list(carry_all[0:4]), list(carry_all[4:8])]
        rate_sum = carry_all[8]
        turned = turned_of(index)
        for g in reversed(range(groups)):
            base = index * REACH + g * GROUP
            columns = turned[g * GROUP // CHUNK]
            rows = span(base, GROUP)
            steps = delta_s[rows, :]
            feeds = dscan_s[rows, :]
            pulls = u_s[rows, :]
            held, prods, sums = [], [], []
            for t in reversed(range(GROUP)):
                at = (g * GROUP + t) % CHUNK
                read = [
                    jnp.broadcast_to(
                        columns[2 * STATE + 8 * h : 2 * STATE + 8 * h + 8, at : at + 1], (8, LANES)
                    )
                    for h in range(2)
                ]
                place = span((base + t) * STATE, STATE)
                held_row, prod_row = [], []
                total = [None, None]
                for e, lanes in enumerate(lane_sets):
                    step = spread(steps[:, lanes], t)
                    feed = spread(feeds[:, lanes], t)
                    pull = spread(pulls[:, lanes], t)
                    before = states[place, lanes]
                    lams, both = [], []
                    for h in range(2):
                        power = step * rate_ref[8 * h : 8 * h + 8, lanes]
                        lam = feed * read[h] + carry[h][e]
                        carry[h][e] = jnp.exp2(power) * lam
                        lams.append(lam)
                        part = pull * lam
                        total[h] = part if e == 0 else total[h] + part
                        both.append(power * carry[h][e])
                    held_row.append(pack(*lams))
                    prod_row.append(pack(*both) * before)
                held.append(jnp.concatenate(held_row, axis=1))
                prods.append(jnp.concatenate(prod_row, axis=1))
                sums.append(pack(*total))
            y_s[rows, :] = dot(entry_s[rows, :], jnp.concatenate(held, axis=0))
            both = dot(sums_s[...], jnp.concatenate(prods, axis=0))
            gslope_s[rows, :] = both[:GROUP]
            rate_sum = rate_sum + both[GROUP:]
            found = dot(ones, jnp.concatenate(sums, axis=0), NT)
            wide_s[rows, :] = (found * mask_s[0]).astype(BF)
        return tuple(carry[0] + carry[1]) + (rate_sum,)

    done = lax.fori_loop(
        0, length // REACH, back_chunk, (zero,) * 8 + (jnp.zeros((STATE, INNER), F32),)
    )
    gsmall_ref[0:STATE, :] += done[8] * LN2

    def gradients(slab):
        row = slab * SLAB
        sum_pre = sum_skip = None
        for a in pieces:
            rows = span(row + a, BLOCK)
            dfeed = y_s[rows, :]
            dpre = ratio_s[rows, :] * (gslope_s[rows, :] * LN2 + dfeed * u_s[rows, :])
            gsilu_s[rows, :] = dpre
            dscan = dscan_s[rows, :]
            y_s[rows, :] = dscan * vec_ref[6:7, :] + dfeed * delta_s[rows, :]
            one, two = row_sum(dpre), row_sum(dscan * act_s[rows, :])
            sum_pre = one if sum_pre is None else sum_pre + one
            sum_skip = two if sum_skip is None else sum_skip + two
        gvec_ref[5] += sum_pre
        gvec_ref[6] += sum_skip
        dpre_all = gsilu_s[span(row, SLAB), :].astype(BF)
        dproj = (
            dot(dpre_all, wdt_s[...], NT)
            + dot(wide_s[span(row, SLAB), :], fold_s[0])
            + dread_s[span(row, SLAB), :].astype(F32)
        )
        extra = dot(dproj.astype(BF), wx_s[...], NT)
        low_sum = None
        for k in range(SLAB // CHUNK):
            low = projt_s[slab * (SLAB // CHUNK) + k][:RANK].astype(BF)
            part = dot(low, dpre_all[k * CHUNK : (k + 1) * CHUNK])
            low_sum = part if low_sum is None else low_sum + part
        gsmall_ref[STATE : 2 * STATE, :] += low_sum
        gsmall_ref[2 * STATE : 5 * STATE, :] += dot(
            dproj.astype(BF), act_s[span(row, SLAB), :].astype(BF), TN
        )[: 3 * STATE]
        for a in pieces:
            rows = span(row + a, BLOCK)
            gsilu_s[rows, :] = (y_s[rows, :] + extra[a : a + BLOCK]) * slope_s[rows, :]

    each(slabs, gradients)

    def unconvolve(slab):
        row = slab * SLAB
        totals = [None] * 5
        near_s[: SLAB + 8, :] = gsilu_s[span(row, SLAB + 8, 8), :]
        for a in pieces:
            rows = span(row + a, BLOCK)
            inner = inner_s[span(row + a + 16, BLOCK, 16), :].astype(F32)
            dinner = None
            for j in range(KERNEL):
                moved = near_s[a + 3 - j : a + 3 - j + BLOCK, :]
                term = vec_ref[j : j + 1, :] * moved
                dinner = term if dinner is None else dinner + term
                part = row_sum(moved * inner)
                totals[j] = part if totals[j] is None else totals[j] + part
            part = row_sum(near_s[a : a + BLOCK, :])
            totals[4] = part if totals[4] is None else totals[4] + part
            dproj_s[rows, :INNER] = dinner.astype(BF)
        for j in range(5):
            gvec_ref[j] += totals[j]

    each(slabs, unconvolve)

    def mirror_dnorm(slab):
        dnorm_all = dot(dproj_s[span(slab * SLAB, SLAB), :], w_in_s[...], NT)
        for k in range(SLAB // CHUNK):
            high, low = split_low(dnorm_all[k * CHUNK : (k + 1) * CHUNK])
            there = span(place_of(slab * (SLAB // CHUNK) + k), CHUNK)
            dnorm_s[there, :] = dot(flip_s[0], high) + dot(flip_s[0], low)

    def natural_dnorm(slab):
        rows = span(slab * SLAB, SLAB)
        total = dot(dproj_s[rows, :], w_in_s[...], NT) + dnorm_s[rows, :]
        xf, inv = norm_parts(rows)
        scaled = total * gain_ref[...]
        hat = xf * inv
        ggain_ref[...] += row_sum(total * hat)
        mean = jnp.mean(scaled * hat, axis=-1, keepdims=True)
        result = up_s[rows, :].astype(F32) + inv * (scaled - hat * mean)
        store_half(gin_kept_ref, gin_given_ref, slab, slice(None), result)

    @pl.when(natural == 0)
    def _():
        each(slabs, mirror_dnorm)
        copy_s[...] = dot(copy_s[...], perm_ref[...], NT).astype(BF)

    @pl.when(natural == 1)
    def _():
        each(slabs, natural_dnorm)

    gwin_ref[...] += dot(copy_s[...], dproj_s[...], TN)

    @pl.when((window == pl.num_programs(0) - 1) & (natural == 1))
    def _():
        gwin_out[...] = gwin_ref[...].astype(BF)
        gwout_out[...] = gwout_ref[...].astype(BF)
        gsmall_out[...] = gsmall_ref[...].astype(BF)
        vectors = [jnp.sum(gvec_ref[j], axis=0, keepdims=True) for j in range(7)]
        gain = jnp.sum(ggain_ref[...], axis=0, keepdims=True)
        vectors.append(jnp.concatenate([gain, jnp.zeros((1, INNER - D), F32)], axis=1))
        vectors.append(jnp.zeros((8, INNER), F32))
        gvec_out[...] = jnp.concatenate(vectors, axis=0).astype(BF)


def run_layer(
    core, x, x_got, up, up_got, perm, w_in, w_x, w_dt, w_out, conv_w, conv_b, dt_bias, a_log, d_skip, gain
):
    windows, half, _ = x_got.shape
    length = 2 * half
    vec = jnp.concatenate(
        [conv_w.T, conv_b[None], dt_bias[None], d_skip[None], jnp.zeros((1, INNER), F32)], axis=0
    )
    rate = (-LOG2E) * jnp.exp(a_log).T

    def whole(shape):
        return pl.BlockSpec(shape, lambda w, q, core: (0,) * len(shape))

    kept = pl.BlockSpec((1, half, D), lambda w, q, core: (windows * core[0] + w, 0, 0))
    got = pl.BlockSpec((1, half, D), lambda w, q, core: (w, 0, 0))
    fixed = (perm, w_in, w_out, w_x, w_dt, vec, rate, gain[None])
    grads = [
        jax.ShapeDtypeStruct((D, 2 * INNER), BF),
        jax.ShapeDtypeStruct((INNER, D), BF),
        jax.ShapeDtypeStruct((5 * STATE, INNER), BF),
        jax.ShapeDtypeStruct((16, INNER), BF),
    ]
    inner_f32 = [pltpu.VMEM((length, INNER), F32)]
    outer_bf = [pltpu.VMEM((length, D), BF)]
    outer_f32 = [pltpu.VMEM((length, D), F32)]
    halo_f32 = [pltpu.VMEM((length + 8, INNER), F32)]
    scratch = (
        [pltpu.VMEM((length * STATE, INNER), BF)]
        + inner_f32 * 7
        + halo_f32
        + inner_f32
        + [pltpu.VMEM((length + 16, INNER), BF)]
        + [pltpu.VMEM((length, LANES), BF)]
        + [
            pltpu.VMEM((length // CHUNK, 3 * STATE, CHUNK), F32),
            pltpu.VMEM((length, 2 * INNER), BF),
            pltpu.VMEM((length, INNER), BF),
        ]
        + outer_bf * 4
        + outer_f32
        + [pltpu.VMEM((length, WIDE), BF)] * 3
        + [
            pltpu.VMEM((D, 2 * INNER), BF),
            pltpu.VMEM((INNER, D), BF),
            pltpu.VMEM((2, CHUNK, CHUNK), BF),
            pltpu.VMEM((2, LANES, WIDE), BF),
            pltpu.VMEM((2, WIDE, LANES), BF),
            pltpu.VMEM((2 * GROUP, WIDE), BF),
            pltpu.VMEM((2, GROUP, WIDE), F32),
            pltpu.VMEM((SLAB + 16, INNER), F32),
            pltpu.VMEM((INNER, LANES), BF),
            pltpu.VMEM((LANES, INNER), BF),
            pltpu.VMEM((D, 2 * INNER), F32),
            pltpu.VMEM((INNER, D), F32),
            pltpu.VMEM((5 * STATE, INNER), F32),
            pltpu.VMEM((7, 8, INNER), F32),
            pltpu.VMEM((8, D), F32),
        ]
    )
    return pl.pallas_call(
        layer_kernel,
        grid_spec=pltpu.PrefetchScalarGridSpec(
            num_scalar_prefetch=1,
            grid=(windows, 2),
            in_specs=[kept, got, kept, got] + [whole(item.shape) for item in fixed],
            out_specs=[got] * 4 + [whole(item.shape) for item in grads],
            scratch_shapes=scratch,
        ),
        out_shape=[
            jax.ShapeDtypeStruct((windows, half, D), kind) for kind in (BF, BF, F32, F32)
        ]
        + grads,
        compiler_params=pltpu.CompilerParams(vmem_limit_bytes=64 * 2**20 - 65536),
    )(core.reshape(1).astype(jnp.int32), x, x_got, up, up_got, *fixed)


def layer_grads(results):
    gwin, gwout, gsmall, gvec = results
    return [
        gwin,
        gsmall[2 * STATE :].T,
        gsmall[STATE : 2 * STATE],
        gwout,
        gvec[:KERNEL].T,
        gvec[4:6],
        gsmall[:STATE].T,
        gvec[6:8],
    ]


def param_shapes():
    return [
        (D, 2 * INNER),
        (INNER, RANK + 2 * STATE),
        (RANK, INNER),
        (INNER, D),
        (INNER, KERNEL),
        (INNER,),
        (INNER,),
        (INNER, STATE),
        (INNER,),
        (D,),
    ]


def bounds():
    edges = [0]
    for shape in param_shapes():
        edges.append(edges[-1] + math.prod(shape))
    return edges


def slot_index(owners):
    count = owners.shape[0]
    order = jnp.arange(count, dtype=jnp.int32)
    same = (owners[None, :] == owners[:, None]) & (order[None, :] < order[:, None])
    return jnp.sum(same.astype(jnp.int32), axis=1)


def swap(value, axis, bit):
    size = lax.axis_size(axis)
    return lax.ppermute(value, axis, [(i, i ^ bit) for i in range(size)])


def up_to(value, multiple):
    return -(-value // multiple) * multiple


def pad_rows(value, rows, axis):
    widths = [(0, 0)] * value.ndim
    widths[axis] = (0, rows - value.shape[axis])
    return jnp.pad(value, widths)


def gather_params(weights, owners, rank, matches):
    size = lax.axis_size("dp")
    me = lax.axis_index("dp")
    core = lax.axis_index("seq")
    blocks, block_len = owners.shape[0], weights.shape[1]
    rows = block_len // LANES
    padded = up_to(rows, 16)
    near = min(4, size)
    tiles = weights.reshape(SLOTS, rows, LANES)
    rounded = lax.reduce_precision(tiles, 8, 7)
    pair = SLOTS // 2
    mine = lax.dynamic_slice_in_dim(rounded, core * pair, pair, 0).astype(BF)
    many = pad_rows(mine, padded, 1).reshape(pair * padded, LANES)
    first = MATRIX_END // block_len
    last = (PARAMS - 1) // block_len + 1
    here = matches[:, first:last].T[:, :, None, None]
    fine = jnp.sum(jnp.where(here, (tiles - rounded)[None], 0.0), axis=1).astype(BF)
    fine_rows = (last - first) * rows
    fine_half = up_to(fine_rows, 32) // 2
    fine = pad_rows(fine.reshape(fine_rows, LANES), 2 * fine_half, 0)
    fine = lax.dynamic_slice_in_dim(fine, core * fine_half, fine_half, 0)
    away = owners ^ me
    spot = jnp.zeros_like(owners)
    bit, step = size // 2, 0
    while bit >= near:
        got = swap(jnp.concatenate([many, fine], axis=0), "dp", bit)
        count = many.shape[0]
        many = jnp.concatenate([many, got[:count]], axis=0)
        fine = fine + got[count:]
        spot = spot + jnp.where((away & bit) != 0, 1 << step, 0)
        bit, step = bit // 2, step + 1
    count = many.shape[0]
    sent = jnp.concatenate([many, fine], axis=0)
    others = [swap(sent, "dp", k) for k in range(1, near)]
    many = jnp.stack([many] + [item[:count] for item in others])
    for item in others:
        fine = fine + item[count:]
    spot = (spot + (away & (near - 1)) * (size // near)) * pair + rank % pair
    chosen = many.reshape(size * pair, padded, LANES)[spot]
    theirs = swap(chosen, "seq", 1)
    fine_got = swap(fine, "seq", 1)
    local = (rank // pair == core)[:, None, None]
    theta = jnp.where(local, chosen, theirs)[:, :rows].reshape(blocks * rows, LANES)
    fine = jnp.concatenate(
        [jnp.where(core == 0, fine, fine_got), jnp.where(core == 0, fine_got, fine)], axis=0
    )
    begin = (MATRIX_END - first * block_len) // LANES
    fine = fine[begin : begin + (PARAMS - MATRIX_END) // LANES]
    return lax.optimization_barrier((theta, fine))


def scatter_sum(value, size, beside):
    me = lax.axis_index("dp")
    stride = 1
    total = value
    while stride < size:
        radix = min(4, size // stride)
        total = total.reshape((size // (stride * radix), radix) + value.shape[1:])
        digit = (me // stride) % radix
        low = total.astype(BF)
        kept = lax.dynamic_index_in_dim(total, digit, 1, keepdims=False).astype(F32)
        for k in range(1, radix):
            given = lax.dynamic_index_in_dim(low, digit ^ k, 1, keepdims=False)
            kept = kept + swap(given, "dp", k * stride).astype(F32)
        total = kept
        if stride == 1:
            total, beside = lax.optimization_barrier((total, beside))
        stride *= radix
    return total[0], beside


def other_half(value, core):
    count = value.shape[0] // 2
    return swap(lax.dynamic_slice_in_dim(value, (1 - core) * count, count, 0), "seq", 1)


def by_position(kept, given, core):
    got = swap(given, "seq", 1)
    return jnp.concatenate(
        [jnp.where(core == 0, kept, got), jnp.where(core == 0, got, kept)], axis=0
    )


def on_device(
    inputs, cotangent, loss_mask, complement_map, owners, weights, first_moment, second_moment
):
    size = lax.axis_size("dp")
    me = lax.axis_index("dp")
    core = lax.axis_index("seq")
    blocks, block_len = owners.shape[0], weights.shape[1]
    rows = block_len // LANES
    pair = SLOTS // 2
    rank = slot_index(owners)
    order = jnp.arange(blocks, dtype=jnp.int32)
    matches = (owners[None, :] == me) & (
        rank[None, :] == jnp.arange(SLOTS, dtype=jnp.int32)[:, None]
    )
    occupied = jnp.any(matches, axis=1)
    block_of = jnp.sum(jnp.where(matches, order[None, :], 0), axis=1)
    theta, fine = gather_params(weights, owners, rank, matches)
    upstream = cotangent * loss_mask.astype(BF)[..., None]
    x_got = other_half(inputs, core)
    up_got = other_half(upstream, core)

    edges = [edge // LANES for edge in bounds()]
    shapes = param_shapes()
    tail = edges[4]

    def high_of(index):
        return theta[edges[index] : edges[index + 1]].reshape(shapes[index])

    def full_of(index):
        part = theta[edges[index] : edges[index + 1]].astype(F32)
        part = part + fine[edges[index] - tail : edges[index + 1] - tail].astype(F32)
        return part.reshape(shapes[index])

    perm = (complement_map[:, None] == jnp.arange(D, dtype=jnp.int32)[None, :]).astype(BF)
    results = run_layer(
        core,
        inputs,
        x_got,
        upstream,
        up_got,
        perm,
        *[high_of(index) for index in range(4)],
        *[full_of(index) for index in range(4, 10)],
    )
    pieces = layer_grads(results[4:])
    padded = up_to(rows, 16)
    spare = jnp.zeros(((blocks + 1) * rows - (PARAMS + INNER - D) // LANES, LANES), BF)
    tiles = [item.astype(BF).reshape(-1, LANES) for item in pieces] + [spare]
    grad_blocks = jnp.concatenate(tiles, axis=0).reshape(blocks + 1, rows, LANES)
    grad_blocks = pad_rows(grad_blocks, padded, 1)
    source = jnp.full((size * SLOTS,), blocks, jnp.int32).at[owners * SLOTS + rank].set(order)
    source = source.reshape(size, 2, pair)

    def for_core(which):
        index = lax.dynamic_index_in_dim(source, which, 1, keepdims=False)
        return grad_blocks[index.reshape(-1)].reshape(size * pair * padded, LANES)

    got = swap(for_core(1 - core), "seq", 1)
    chip = (for_core(core).astype(F32) + got.astype(F32)).astype(BF)
    chip = chip.reshape(size, pair * padded, LANES)
    output = by_position(results[0], results[1], core)
    grad_input = by_position(results[2], results[3], core)
    summed, (output, grad_input) = scatter_sum(chip, size, (output, grad_input))
    summed = summed.reshape(pair, -1, LANES)[:, :rows]
    other = swap(summed, "seq", 1)
    owned = jnp.concatenate(
        [jnp.where(core == 0, summed, other), jnp.where(core == 0, other, summed)], axis=0
    ).reshape(SLOTS, block_len)
    new_first = BETA_ONE * first_moment + (1.0 - BETA_ONE) * owned
    new_second = BETA_TWO * second_moment + (1.0 - BETA_TWO) * owned * owned
    position = block_of[:, None] * block_len + jnp.arange(block_len, dtype=jnp.int32)[None, :]
    is_matrix = position < MATRIX_END
    rate = jnp.where(is_matrix, RATE_MATRIX, RATE_VECTOR)
    decay = jnp.where(is_matrix, WEIGHT_DECAY, 0.0)
    corrected = (
        new_first
        / (1.0 - BETA_ONE**STEP_COUNT)
        / (jnp.sqrt(new_second / (1.0 - BETA_TWO**STEP_COUNT)) + ADAM_EPSILON)
    )
    new_theta = weights - rate * (corrected + decay * weights)
    keep = occupied[:, None]
    return (
        output,
        grad_input,
        jnp.where(keep, new_theta, 0.0),
        jnp.where(keep, new_first, 0.0),
        jnp.where(keep, new_second, 0.0),
    )


def solution(mesh):
    in_specs = (
        P("dp", "seq", None),
        P("dp", "seq", None),
        P("dp", "seq"),
        P(),
        P(),
        P("dp", None),
        P("dp", None),
        P("dp", None),
    )
    out_specs = (
        P("dp", "seq", None),
        P("dp", "seq", None),
        P("dp", None),
        P("dp", None),
        P("dp", None),
    )
    return jax.shard_map(
        on_device, mesh=mesh, in_specs=in_specs, out_specs=out_specs, check_vma=False
    )
```
